256 devices in a mesh: section: 16 (over z_lo, y), fsdp: 16 (over z_hi, x, core).
Axes of the slice: x: 4, y: 4, z: 8 (z_hi: 2, z_lo: 4; z = z_hi * 4 + z_lo), core: 2. Of those that a mesh axis runs over, the one named last changes fastest.
Arguments:
- residual: bfloat16 [512, 4608], P('fsdp', 'section'), may hold values from -12 to 12
- final_gain: bfloat16 [4608], P('section'), may hold values from 0.099609375 to 1.8984375
- embedding: bfloat16 [256000, 4608], P(('section', 'fsdp')), may hold values from -0.25 to 0.25
- labels: int32 [512], replicated, may hold values from 0 to 255999
- token_weight: float32 [512], replicated, may hold values from 1 to 8
Outputs:
- token_loss: float32 [512], P('fsdp')
- grad_residual: float32 [512, 4608], P('fsdp', 'section')
The draws below stay inside these ranges and needn't reach their ends.
All inputs are finite; a program needn't handle non-finite values.
Results may differ from the reference program's by a relative error of at most 0.003.
Values may be sent and summed in bfloat16 or wider, within the bound.
No kernel may reach another device: no remote copies, remote signals or barrier semaphores. Data moves between devices by JAX's collectives and lax.ppermute only.
A program may use at most 64 MiB of HBM per device.

```python
import math
import jax
import jax.numpy as jnp
from jax import lax

D = 4608
VOCAB = 256000
TOKENS = 512
N_SECTION = 16
N_FSDP = 16


def draw_residual(key, part):
    key = jax.random.fold_in(key, 5)
    keys = jax.random.split(key, 3)
    shape = (TOKENS, D)
    base = jax.random.truncated_normal(keys[0], -4.0, 4.0, shape, jnp.float32)
    row_scale = jnp.exp(jax.random.uniform(keys[1], (TOKENS, 1), jnp.float32, math.log(0.1), 0.0))
    column_scale = jnp.exp(jax.random.uniform(keys[2], (1, D), jnp.float32, math.log(0.3), math.log(3.0)))
    return (base * row_scale * column_scale).astype(jnp.bfloat16)


def with_ends(array, key, smallest, top_value):
    dims = array.shape
    spot = [jax.random.randint(jax.random.fold_in(key, axis), (), 0, dims[axis]) for axis in range(len(dims))]
    array = array.at[tuple(spot)].set(smallest)
    longest = dims.index(max(dims))
    spot[longest] = (spot[longest] + 1) % dims[longest]
    return array.at[tuple(spot)].set(top_value)


def shard_levels(stream_key, extent, shards, least, largest):
    def one(dim, parts):
        draws = jax.random.uniform(jax.random.fold_in(jax.random.fold_in(stream_key, 6), dim), (parts,), jnp.float32, least / len(shards), largest / len(shards))
        return jnp.repeat(jnp.exp(draws), extent[dim] // parts).reshape((-1,) + (1,) * (len(extent) - dim - 1))

    gain = one(*shards[0])
    for cut in shards[1:]:
        gain = gain * one(*cut)
    return gain


def centred(own_key, shape, deviation, limit, cuts=(), kind=jnp.bfloat16):
    entries = jax.random.normal(own_key, shape, jnp.float32) * deviation
    if len(cuts) > 0:
        entries = shard_levels(own_key, shape, cuts, -0.22, 0.18) * entries
    return jnp.clip(entries, min=-limit, max=limit).astype(kind)


def setup_inputs(seed: int = 0) -> dict:
    splits = jax.random.split(jax.random.key(seed), 6)
    return {
        "residual": draw_residual(jax.random.fold_in(splits[5], 71), 0),
        "final_gain": jnp.clip(1.0 + 0.18 * jax.random.normal(splits[1], (D,), jnp.float32), 0.099609375, 1.8984375).astype(jnp.bfloat16),
        "embedding": centred(splits[2], (VOCAB, D), (D // 9) ** -0.5, 0.25, ((0, 256),)),
        "labels": with_ends(jax.random.randint(splits[3], (TOKENS,), 0, VOCAB), jax.random.fold_in(splits[3], 1), 0, VOCAB - 1).astype(jnp.int32),
        "token_weight": jnp.clip(jnp.exp(jax.random.uniform(splits[4], (TOKENS,), jnp.float32, math.log(1.0), math.log(8.0))), 1.0, 8.0),
    }


EPS = 1e-06
CAP = 30.0

def capped_block(normed, vocab_block):
    logits = lax.dot_general(normed, vocab_block, (((1,), (1,)), ((), ())), preferred_element_type=jnp.float32)
    return CAP * jnp.tanh(logits / CAP)

def reference(residual, final_gain, embedding, labels, token_weight):
    values = residual.astype(jnp.float32)
    scaling = lax.rsqrt(lax.optimization_barrier(jnp.mean(values * values, axis=1, keepdims=True)) + EPS)
    gain_wide = final_gain.astype(jnp.float32)
    normed = (values * scaling * gain_wide).astype(jnp.bfloat16)
    block_rows = VOCAB // (N_SECTION * N_FSDP)
    blocks = embedding.reshape(N_SECTION * N_FSDP, block_rows, D)
    offsets = jnp.arange(N_SECTION * N_FSDP, dtype=jnp.int32) * block_rows
    columns = jnp.arange(block_rows, dtype=jnp.int32)

    def first_pass(running, inputs):
        vocab_block, offset = inputs
        capped = capped_block(normed, vocab_block)
        onehot = labels[:, None] == offset + columns[None, :]
        return ((running[0] + lax.optimization_barrier(jnp.sum(jnp.exp(capped), axis=1)), running[1] + lax.optimization_barrier(jnp.sum(jnp.where(onehot, capped, 0.0), axis=1))), None)
    empty_sums = jnp.zeros((TOKENS,), jnp.float32)
    (sum_exp, target), _ = lax.scan(first_pass, (empty_sums, empty_sums), (blocks, offsets))
    log_total = jnp.log(sum_exp)
    token_loss = log_total - target

    def second_pass(running, inputs):
        vocab_block, offset = inputs
        capped = capped_block(normed, vocab_block)
        onehot = (labels[:, None] == offset + columns[None, :]).astype(jnp.float32)
        weights = jnp.exp(capped - log_total[:, None])
        logit_grad = (weights - onehot) * token_weight[:, None] * (1.0 - (capped / CAP) ** 2)
        return (running + jnp.dot(logit_grad.astype(jnp.bfloat16), vocab_block, preferred_element_type=jnp.float32), None)
    grad_normed, _ = lax.scan(second_pass, jnp.zeros((TOKENS, D), jnp.float32), (blocks, offsets))
    upstream = grad_normed * gain_wide
    inner_sum = lax.optimization_barrier(jnp.sum(upstream * values, axis=1, keepdims=True))
    grad_residual = scaling * upstream - values * scaling ** 3 * inner_sum / D
    return (token_loss, grad_residual)
```

```python
import functools

import jax
import jax.numpy as jnp
from jax import lax
from jax.experimental import pallas as pl
from jax.experimental.pallas import tpu as pltpu
from jax.sharding import Mesh, PartitionSpec as P

D = 4608
EPS = 1e-06
CAP = 30.0
ROWS = 1000
PADDED = 1024
PIECE = 288
WIDE = 1152
BLOCK = 64
TILES = WIDE // 128
SLOTS = 7
PACKED = TILES * BLOCK + 16
F32 = jnp.float32
BF16 = jnp.bfloat16
VMEM = pltpu.MemorySpace.VMEM
BIG = pltpu.CompilerParams(vmem_limit_bytes=56 * 1024 * 1024)


def permute_kernel(in_ref, out_ref):
    block = in_ref[...]
    rows = pl.program_id(0) * block.shape[0] + lax.broadcasted_iota(jnp.int32, (block.shape[0], 1), 0)
    for y in range(4):
        parts = [block[:, (z * 4 + y) * PIECE : (z * 4 + y + 1) * PIECE].astype(F32) for z in range(4)]
        wide = jnp.concatenate(parts, axis=1)
        out_ref[:, y * WIDE : (y + 1) * WIDE] = jnp.where(rows < ROWS, wide, 0.0).astype(BF16)


def permute_embedding(embedding):
    step = 128
    return pl.pallas_call(
        permute_kernel,
        grid=(PADDED // step,),
        in_specs=[pl.BlockSpec((step, D), lambda i: (i, 0))],
        out_specs=pl.BlockSpec((step, D), lambda i: (i, 0)),
        out_shape=jax.ShapeDtypeStruct((PADDED, D), BF16),
        compiler_params=BIG,
        cost_estimate=pl.CostEstimate(flops=0, bytes_accessed=4 * ROWS * D, transcendentals=0),
        name="permute_embedding",
    )(embedding)


def pack_kernel(in_ref, out_ref):
    for zh in range(2):
        parts = [in_ref[zl * 2 + zh, 0:32, :].astype(F32) for zl in range(4)]
        wide = jnp.concatenate(parts, axis=1)
        for k in range(TILES):
            tile = wide[:, k * 128 : (k + 1) * 128].astype(BF16)
            for copy in range(16):
                out_ref[copy, k * BLOCK + zh * 32 : k * BLOCK + zh * 32 + 32, :] = tile
    gains = jnp.concatenate([in_ref[zl * 2, 32:48, :].astype(F32) for zl in range(4)], axis=1)
    rows = [gains[0:1, k * 128 : (k + 1) * 128] for k in range(TILES)]
    tile = jnp.concatenate(rows + [jnp.zeros((16 - TILES, 128), F32)], axis=0).astype(BF16)
    for copy in range(16):
        out_ref[copy, TILES * BLOCK : PACKED, :] = tile


def pack_tokens(gathered):
    return pl.pallas_call(
        pack_kernel,
        out_shape=jax.ShapeDtypeStruct((16, PACKED, 128), BF16),
        compiler_params=BIG,
        name="pack_tokens",
    )(gathered)


def logits_kernel(first_ref, packed_ref, embedding_ref, labels_ref, slot_ref, e_ref, stats_ref, scale_ref, normed, logits):
    y = pl.program_id(0)

    @pl.when(y == 0)
    def _():
        gains = [packed_ref[b * 4, TILES * BLOCK : PACKED, :].astype(F32) for b in range(4)]
        for x in range(4):
            squares = jnp.zeros((BLOCK, 128), F32)
            for b in range(4):
                for k in range(TILES):
                    v = packed_ref[b * 4 + x, k * BLOCK : (k + 1) * BLOCK, :].astype(F32)
                    squares += v * v
            scale = lax.rsqrt(jnp.sum(squares, axis=1, keepdims=True) / D + EPS)
            scale_ref[x * BLOCK : (x + 1) * BLOCK, :] = jnp.broadcast_to(scale, (BLOCK, 128))
            for b in range(4):
                for k in range(TILES):
                    v = packed_ref[b * 4 + x, k * BLOCK : (k + 1) * BLOCK, :].astype(F32)
                    normed[b, x * BLOCK : (x + 1) * BLOCK, k * 128 : (k + 1) * 128] = (
                        v * scale * gains[b][k : k + 1, :]
                    ).astype(BF16)

    term = lax.dot_general(
        embedding_ref[...], normed[y], (((1,), (1,)), ((), ())), preferred_element_type=F32
    )

    @pl.when(y == 0)
    def _():
        logits[...] = term

    @pl.when(y > 0)
    def _():
        logits[...] += term

    @pl.when(y == 3)
    def _():
        raw = logits[...]
        ratio = jnp.tanh(raw / CAP)
        row = lax.broadcasted_iota(jnp.int32, raw.shape, 0)
        inside = row < ROWS
        is_label = jnp.logical_and(inside, row + first_ref[0] == labels_ref[...])
        exps = jnp.where(inside, jnp.exp(CAP * ratio), 0.0)
        others = jnp.where(is_label, 0.0, exps * (1.0 - ratio * ratio))
        stats_ref[0:1, :] = jnp.sum(exps, axis=0, keepdims=True)
        stats_ref[1:2, :] = jnp.sum(others * raw, axis=0, keepdims=True)
        stats_ref[2:3, :] = jnp.sum(jnp.where(is_label, raw, 0.0), axis=0, keepdims=True)
        stats_ref[3:8, :] = jnp.zeros((5, raw.shape[1]), F32)
        e_ref[0:256, :] = others.T.astype(BF16)
        e_ref[256:288, :] = slot_ref[...]


def logits_of(first, packed, embedding, labels, slots):
    return pl.pallas_call(
        logits_kernel,
        grid=(4,),
        in_specs=[
            pl.BlockSpec(memory_space=pltpu.MemorySpace.SMEM),
            pl.BlockSpec((16, PACKED, 128), lambda y: (0, 0, 0)),
            pl.BlockSpec((PADDED, WIDE), lambda y: (0, y)),
            pl.BlockSpec((1, 256), lambda y: (0, 0)),
            pl.BlockSpec((32, PADDED), lambda y: (0, 0)),
        ],
        out_specs=[
            pl.BlockSpec((288, PADDED), lambda y: (0, 0)),
            pl.BlockSpec((8, 256), lambda y: (0, 0)),
            pl.BlockSpec((256, 128), lambda y: (0, 0)),
        ],
        out_shape=[
            jax.ShapeDtypeStruct((288, PADDED), BF16),
            jax.ShapeDtypeStruct((8, 256), F32),
            jax.ShapeDtypeStruct((256, 128), F32),
        ],
        scratch_shapes=[pltpu.VMEM((4, 256, WIDE), BF16), pltpu.VMEM((PADDED, 256), F32)],
        compiler_params=BIG,
        cost_estimate=pl.CostEstimate(flops=2 * 256 * PADDED * D, bytes_accessed=2 * PADDED * D, transcendentals=2 * 256 * PADDED),
        name="logits",
    )(first, packed, embedding, labels, slots)


def three_pieces(value):
    high = value.astype(BF16).astype(F32)
    middle = (value - high).astype(BF16).astype(F32)
    low = (value - high - middle).astype(BF16).astype(F32)
    return [high, middle, low]


def stats_row(values):
    pieces = []
    for value in values:
        for piece in three_pieces(value):
            pieces += [piece, jnp.zeros((1, 128 - BLOCK), F32)]
    return jnp.concatenate(pieces, axis=1)


def read_stats(row):
    return [
        sum(row[:, (3 * i + j) * 128 : (3 * i + j) * 128 + BLOCK] for j in (2, 1, 0))
        for i in range(3)
    ]


def gradient_kernel(with_other, *refs):
    if with_other:
        e_ref, embedding_ref, stats_ref, other_ref, out_ref = refs
    else:
        e_ref, embedding_ref, stats_ref, out_ref = refs
    term = jnp.dot(e_ref[...], embedding_ref[...], preferred_element_type=F32)
    last = lax.broadcasted_iota(jnp.int32, (8, WIDE), 0) == 7
    for x in range(4):
        main = term[x * BLOCK : (x + 1) * BLOCK, :]
        extra = term[256 + 8 * x : 256 + 8 * x + 8, :]
        values = [stats_ref[i : i + 1, x * BLOCK : (x + 1) * BLOCK] for i in range(3)]
        if with_other:
            main = main + other_ref[x, 0:BLOCK, :].astype(F32)
            other_extra = other_ref[x, BLOCK : BLOCK + 8, :].astype(F32)
            extra = extra + other_extra
            values = [a + b for a, b in zip(values, read_stats(other_extra[7:8, :]))]
        row = jnp.broadcast_to(stats_row(values), (8, WIDE))
        out_ref[x, 0:BLOCK, :] = main.astype(BF16)
        out_ref[x, BLOCK : BLOCK + 8, :] = jnp.where(last, row, extra).astype(BF16)


def gradient_of(e, embedding, stats, other=None):
    payload = pl.BlockSpec((4, BLOCK + 8, WIDE), lambda y: (y, 0, 0))
    in_specs = [
        pl.BlockSpec((288, PADDED), lambda y: (0, 0)),
        pl.BlockSpec((PADDED, WIDE), lambda y: (0, y)),
        pl.BlockSpec((8, 256), lambda y: (0, 0)),
    ]
    args = [e, embedding, stats]
    if other is not None:
        in_specs.append(payload)
        args.append(other)
    return pl.pallas_call(
        functools.partial(gradient_kernel, other is not None),
        grid=(4,),
        in_specs=in_specs,
        out_specs=payload,
        out_shape=jax.ShapeDtypeStruct((16, BLOCK + 8, WIDE), BF16),
        compiler_params=BIG,
        cost_estimate=pl.CostEstimate(flops=2 * 288 * PADDED * D, bytes_accessed=2 * PADDED * D, transcendentals=0),
        name="gradient",
    )(*args)


def plane_kernel(in_ref, place_ref, more_ref, out_ref):
    total = in_ref[0, 0:BLOCK, :].astype(F32)
    for source in range(1, 16):
        total += in_ref[source, 0:BLOCK, :].astype(F32)
    extras = [in_ref[source, BLOCK : BLOCK + 8, :].astype(F32) for source in range(16)]
    stacked = jnp.concatenate(extras, axis=0).astype(BF16)
    label_rows = jnp.dot(place_ref[...], stacked, preferred_element_type=F32) + more_ref[...].astype(F32)
    row = extras[0][7:8, :]
    for source in range(1, 16):
        row = row + extras[source][7:8, :]
    pieces = []
    for value in read_stats(row):
        pieces += three_pieces(value)
    sums = jnp.concatenate(pieces + [jnp.zeros((1, 640 - 9 * BLOCK), F32)], axis=1)
    sums = jnp.broadcast_to(sums, (16, 640)).astype(BF16)
    for zl in range(4):
        for zh in range(2):
            main = total[zh * 32 : zh * 32 + 32, zl * PIECE : (zl + 1) * PIECE]
            rows = label_rows[zh * 32 : zh * 32 + 32, zl * PIECE : (zl + 1) * PIECE]
            both = jnp.concatenate([main, rows, jnp.zeros((32, 640 - 2 * PIECE), F32)], axis=1)
            out_ref[zl * 2 + zh, 0:32, :] = both.astype(BF16)
            out_ref[zl * 2 + zh, 32:48, :] = sums


def plane_sum(received, place, more):
    return pl.pallas_call(
        plane_kernel,
        out_shape=jax.ShapeDtypeStruct((8, 48, 640), BF16),
        compiler_params=BIG,
        name="plane_sum",
    )(received, place, more)


def final_kernel(half_ref, in_ref, values_ref, gain_ref, weight_ref, scale_ref, loss_ref, grad_ref):
    total = in_ref[0, 0:32, :].astype(F32)
    row = in_ref[0, 32:48, :].astype(F32)[0:1, :]
    for source in range(1, 8):
        total += in_ref[source, 0:32, :].astype(F32)
        row = row + in_ref[source, 32:48, :].astype(F32)[0:1, :]
    pick = lax.broadcasted_iota(jnp.int32, (32, BLOCK), 1) == half_ref[0] * 32 + lax.broadcasted_iota(
        jnp.int32, (32, BLOCK), 0
    )

    def column(i):
        value = sum(row[:, (3 * i + j) * BLOCK : (3 * i + j + 1) * BLOCK] for j in (2, 1, 0))
        return jnp.sum(jnp.where(pick, jnp.broadcast_to(value, (32, BLOCK)), 0.0), axis=1, keepdims=True)

    sum_exp, inner_others, raw = column(0), column(1), column(2)
    weight = weight_ref[...]
    scaling = scale_ref[:, 0:1]
    ratio = jnp.tanh(raw / CAP)
    capped = CAP * ratio
    log_total = jnp.log(sum_exp)
    loss = log_total - capped
    coefficient = (jnp.exp(capped - log_total) - 1.0) * weight * (1.0 - ratio * ratio)
    coefficient = coefficient.astype(BF16).astype(F32)
    share = weight / sum_exp
    grad_normed = total[:, 0:PIECE] * share + total[:, PIECE : 2 * PIECE] * coefficient
    inner = (inner_others * share + coefficient * raw) / scaling
    upstream = grad_normed * gain_ref[...].astype(F32)
    values = values_ref[...].astype(F32)
    grad_ref[...] = scaling * upstream - values * (scaling * scaling * scaling * inner / D)
    eye = lax.broadcasted_iota(jnp.int32, (32, 128), 0) == lax.broadcasted_iota(jnp.int32, (32, 128), 1)
    loss_ref[...] = jnp.sum(jnp.where(eye, jnp.broadcast_to(loss, (32, 128)), 0.0), axis=0, keepdims=True)


def finish(half, received, values, gain, weight, scale):
    spec = pl.BlockSpec(memory_space=VMEM)
    return pl.pallas_call(
        final_kernel,
        in_specs=[pl.BlockSpec(memory_space=pltpu.MemorySpace.SMEM)] + [spec] * 5,
        out_specs=[spec] * 2,
        out_shape=[jax.ShapeDtypeStruct((1, 128), F32), jax.ShapeDtypeStruct((32, PIECE), F32)],
        compiler_params=BIG,
        name="finish",
    )(half, received, values, gain, weight, scale)


def swap_cores(array):
    return lax.ppermute(array, "core", [(0, 1), (1, 0)])


def on_device(residual, final_gain, embedding, labels, token_weight):
    zl, y, zh, x, core = (lax.axis_index(name) for name in ("z_lo", "y", "z_hi", "x", "core"))
    chip = ((zl * 4 + y) * 2 + zh) * 4 + x
    first = (chip * 2 + core) * ROWS

    mine = jnp.concatenate([residual, final_gain[None, :], jnp.zeros((15, PIECE), BF16)], axis=0)
    gathered = lax.all_to_all(
        jnp.broadcast_to(mine[None], (8, 48, PIECE)), ("z_lo", "z_hi"), 0, 0, tiled=True
    )
    packed = lax.all_to_all(pack_tokens(gathered), ("y", "x"), 0, 0, tiled=True)

    token = jnp.arange(512, dtype=jnp.int32)
    group = (token // 32) % 2 * 4 + (token // 64) % 4
    owner = labels // (2 * ROWS)
    key = owner * 8 + group
    same = jnp.logical_and(key[:, None] == key[None, :], token[None, :] < token[:, None])
    rank = jnp.sum(same.astype(jnp.int32), axis=1)
    turn, slot = rank // SLOTS, rank % SLOTS
    slots = jnp.arange(64, dtype=jnp.int32)
    vocab = jnp.arange(PADDED, dtype=jnp.int32)

    def slot_rows(number):
        taken = jnp.where(jnp.logical_and(owner == chip, turn == number), group * 8 + slot, -1)
        match = taken[None, :] == slots[:, None]
        held = jnp.sum(jnp.where(match, (labels - first)[None, :] + 1, 0), axis=1) - 1
        return (held[:, None] == vocab[None, :]).astype(BF16)

    def by_half(array):
        return array.reshape(2, 4, 2, 32).transpose(2, 1, 0, 3)

    def own_tokens(array):
        return lax.dynamic_slice(by_half(array), (core, x, 0, 0), (1, 1, 2, 32)).reshape(BLOCK)

    own_owner, own_turn, own_slot = own_tokens(owner), own_tokens(turn), own_tokens(slot)
    own_chip = jnp.arange(16, dtype=jnp.int32)
    own_chip = ((zl * 4 + own_chip // 4) * 2 + zh) * 4 + own_chip % 4

    def places(number):
        hit = jnp.logical_and(own_owner[:, None] == own_chip[None, :], (own_turn == number)[:, None])
        at = own_slot[:, None] == jnp.arange(8, dtype=jnp.int32)[None, :]
        return jnp.logical_and(hit[:, :, None], at[:, None, :]).astype(BF16).reshape(BLOCK, 128)

    table = permute_embedding(embedding)

    def more_rows(carry):
        number, rows = carry
        found = jnp.dot(slot_rows(number), table, preferred_element_type=F32).astype(BF16)
        found = found.reshape(2, 4, 8, 4, WIDE).transpose(0, 3, 1, 2, 4).reshape(2, 16, 8, WIDE)
        ours = lax.dynamic_index_in_dim(found, core, 0, keepdims=False)
        theirs = lax.dynamic_index_in_dim(found, 1 - core, 0, keepdims=False)
        ours = ours + swap_cores(theirs)
        ours = lax.all_to_all(ours, ("y", "x"), 0, 0, tiled=True).reshape(128, WIDE)
        return number + 1, rows + jnp.dot(places(number), ours, preferred_element_type=F32).astype(BF16)

    rounds = jnp.max(turn) + 1
    _, more = lax.while_loop(
        lambda carry: carry[0] < rounds, more_rows, (jnp.int32(1), jnp.zeros((BLOCK, WIDE), BF16))
    )

    label_halves = by_half(labels).reshape(2, 1, 256)
    slot_halves = slot_rows(0).reshape(2, 32, PADDED)

    def half_of(array, which):
        return lax.dynamic_index_in_dim(array, which, 0, keepdims=False)

    start = first.reshape(1)
    other_packed = swap_cores(packed)
    e, stats, scale = logits_of(start, packed, table, half_of(label_halves, core), half_of(slot_halves, core))
    e_other, stats_other, _ = logits_of(
        start, other_packed, table, half_of(label_halves, 1 - core), half_of(slot_halves, 1 - core)
    )
    from_other = swap_cores(gradient_of(e_other, table, stats_other))
    payload = gradient_of(e, table, stats, from_other)
    plane = lax.all_to_all(payload, ("y", "x"), 0, 0, tiled=True)
    column = lax.all_to_all(plane_sum(plane, places(0), more), ("z_lo", "z_hi"), 0, 0, tiled=True)

    own_first = ((zh * 4 + x) * 2 + core) * 32
    weight = lax.dynamic_slice_in_dim(token_weight, own_first, 32, 0).reshape(32, 1)
    own_scale = lax.dynamic_slice_in_dim(scale, x * BLOCK + zh * 32, 32, 0)
    loss, grad = finish(zh.reshape(1), column, residual, final_gain.reshape(1, PIECE), weight, own_scale)
    return (loss[0, 0:32], grad)


def solution(mesh):
    fine = Mesh(mesh.devices.reshape(4, 4, 2, 4, 2), ("z_lo", "y", "z_hi", "x", "core"))
    section, fsdp = ("z_lo", "y"), ("z_hi", "x", "core")
    in_specs = (P(fsdp, section), P(section), P(section + fsdp, None), P(), P())
    out_specs = (P(fsdp), P(fsdp, section))
    return jax.shard_map(on_device, mesh=fine, in_specs=in_specs, out_specs=out_specs, check_vma=False)
```

```python
import functools

import jax
import jax.numpy as jnp
from jax import lax
from jax.experimental import pallas as pl
from jax.experimental.pallas import tpu as pltpu
from jax.sharding import Mesh, PartitionSpec as P

D = 4608
EPS = 1e-06
CAP = 30.0
ROWS = 1000
PADDED = 1024
PIECE = 288
WIDE = 1152
BLOCK = 64
TILES = WIDE // 128
SLOTS = 7
PACKED = TILES * BLOCK + 16
F32 = jnp.float32
BF16 = jnp.bfloat16
VMEM = pltpu.MemorySpace.VMEM
WHOLE = pl.BlockSpec(memory_space=VMEM)
SCALARS = pl.BlockSpec(memory_space=pltpu.MemorySpace.SMEM)
BIG = pltpu.CompilerParams(vmem_limit_bytes=20 * 1024 * 1024)


def near(array):
    return pltpu.with_memory_space_constraint(array, VMEM)


def permute_kernel(in_ref, out_ref):
    step = in_ref.shape[0]
    block = in_ref[...]
    first = pl.multiple_of(pl.program_id(0) * step, step)
    rows = first + lax.broadcasted_iota(jnp.int32, (step, 1), 0)
    for y in range(4):
        parts = [block[:, (z * 4 + y) * PIECE : (z * 4 + y + 1) * PIECE].astype(F32) for z in range(4)]
        wide = jnp.concatenate(parts, axis=1)
        out_ref[pl.ds(first, step), y * WIDE : (y + 1) * WIDE] = jnp.where(rows < ROWS, wide, 0.0).astype(BF16)


def permute_embedding(embedding):
    step = 128
    return pl.pallas_call(
        permute_kernel,
        grid=(PADDED // step,),
        in_specs=[pl.BlockSpec((step, D), lambda i: (i, 0))],
        out_specs=WHOLE,
        out_shape=pltpu.VMEM((PADDED, D), BF16),
        compiler_params=BIG,
        cost_estimate=pl.CostEstimate(flops=0, bytes_accessed=4 * ROWS * D, transcendentals=0),
        name="permute_embedding",
    )(embedding)


def pack_kernel(in_ref, out_ref):
    for zh in range(2):
        parts = [in_ref[zl * 2 + zh, 0:32, :].astype(F32) for zl in range(4)]
        wide = jnp.concatenate(parts, axis=1)
        for k in range(TILES):
            tile = wide[:, k * 128 : (k + 1) * 128].astype(BF16)
            for copy in range(16):
                out_ref[copy, k * BLOCK + zh * 32 : k * BLOCK + zh * 32 + 32, :] = tile
    gains = jnp.concatenate([in_ref[zl * 2, 32:48, :].astype(F32) for zl in range(4)], axis=1)
    rows = [gains[0:1, k * 128 : (k + 1) * 128] for k in range(TILES)]
    tile = jnp.concatenate(rows + [jnp.zeros((16 - TILES, 128), F32)], axis=0).astype(BF16)
    for copy in range(16):
        out_ref[copy, TILES * BLOCK : PACKED, :] = tile


def pack_tokens(gathered):
    return pl.pallas_call(
        pack_kernel,
        in_specs=[WHOLE],
        out_specs=WHOLE,
        out_shape=pltpu.VMEM((16, PACKED, 128), BF16),
        compiler_params=BIG,
        name="pack_tokens",
    )(near(gathered))


def logits_kernel(first_ref, packed_ref, embedding_ref, labels_ref, slot_ref, e_ref, stats_ref, scale_ref, normed):
    gains = [packed_ref[b * 4, TILES * BLOCK : PACKED, :].astype(F32) for b in range(4)]
    for x in range(4):
        squares = jnp.zeros((BLOCK, 128), F32)
        for b in range(4):
            for k in range(TILES):
                v = packed_ref[b * 4 + x, k * BLOCK : (k + 1) * BLOCK, :].astype(F32)
                squares += v * v
        scale = lax.rsqrt(jnp.sum(squares, axis=1, keepdims=True) / D + EPS)
        scale_ref[x * BLOCK : (x + 1) * BLOCK, :] = jnp.broadcast_to(scale, (BLOCK, 128))
        for b in range(4):
            for k in range(TILES):
                v = packed_ref[b * 4 + x, k * BLOCK : (k + 1) * BLOCK, :].astype(F32)
                normed[x * BLOCK : (x + 1) * BLOCK, b * WIDE + k * 128 : b * WIDE + (k + 1) * 128] = (
                    v * scale * gains[b][k : k + 1, :]
                ).astype(BF16)
    raw = lax.dot_general(
        embedding_ref[...], normed[...], (((1,), (1,)), ((), ())), preferred_element_type=F32
    )
    ratio = jnp.tanh(raw / CAP)
    row = lax.broadcasted_iota(jnp.int32, raw.shape, 0)
    inside = row < ROWS
    is_label = jnp.logical_and(inside, row + first_ref[0] == labels_ref[...])
    exps = jnp.where(inside, jnp.exp(CAP * ratio), 0.0)
    others = jnp.where(is_label, 0.0, exps * (1.0 - ratio * ratio))
    stats_ref[0:1, :] = jnp.sum(exps, axis=0, keepdims=True)
    stats_ref[1:2, :] = jnp.sum(others * raw, axis=0, keepdims=True)
    stats_ref[2:3, :] = jnp.sum(jnp.where(is_label, raw, 0.0), axis=0, keepdims=True)
    stats_ref[3:8, :] = jnp.zeros((5, raw.shape[1]), F32)
    e_ref[0:256, :] = others.T.astype(BF16)
    e_ref[256:288, :] = slot_ref[...]


def logits_of(first, packed, embedding, labels, slots):
    return pl.pallas_call(
        logits_kernel,
        in_specs=[SCALARS] + [WHOLE] * 4,
        out_specs=[WHOLE] * 3,
        out_shape=[
            pltpu.VMEM((288, PADDED), BF16),
            pltpu.VMEM((8, 256), F32),
            pltpu.VMEM((256, 128), F32),
        ],
        scratch_shapes=[pltpu.VMEM((256, D), BF16)],
        compiler_params=BIG,
        cost_estimate=pl.CostEstimate(flops=2 * 256 * PADDED * D, bytes_accessed=2 * PADDED * D, transcendentals=2 * 256 * PADDED),
        name="logits",
    )(first, near(packed), near(embedding), near(labels), near(slots))


def three_pieces(value):
    high = value.astype(BF16).astype(F32)
    middle = (value - high).astype(BF16).astype(F32)
    low = (value - high - middle).astype(BF16).astype(F32)
    return [high, middle, low]


def stats_row(values):
    pieces = []
    for value in values:
        for piece in three_pieces(value):
            pieces += [piece, jnp.zeros((1, 128 - BLOCK), F32)]
    return jnp.concatenate(pieces, axis=1)


def read_stats(row):
    return [
        sum(row[:, (3 * i + j) * 128 : (3 * i + j) * 128 + BLOCK] for j in (2, 1, 0))
        for i in range(3)
    ]


def gradient_kernel(e_ref, embedding_ref, stats_ref, out_ref):
    last = lax.broadcasted_iota(jnp.int32, (8, WIDE), 0) == 7
    rows = []
    for x in range(4):
        values = [stats_ref[i : i + 1, x * BLOCK : (x + 1) * BLOCK] for i in range(3)]
        rows.append(jnp.broadcast_to(stats_row(values), (8, WIDE)))
    for y in range(4):
        term = jnp.dot(e_ref[...], embedding_ref[:, y * WIDE : (y + 1) * WIDE], preferred_element_type=F32)
        for x in range(4):
            out_ref[y * 4 + x, 0:BLOCK, :] = term[x * BLOCK : (x + 1) * BLOCK, :].astype(BF16)
            extra = term[256 + 8 * x : 256 + 8 * x + 8, :]
            out_ref[y * 4 + x, BLOCK : BLOCK + 8, :] = jnp.where(last, rows[x], extra).astype(BF16)


def gradient_of(e, embedding, stats):
    return pl.pallas_call(
        gradient_kernel,
        in_specs=[WHOLE] * 3,
        out_specs=WHOLE,
        out_shape=pltpu.VMEM((16, BLOCK + 8, WIDE), BF16),
        compiler_params=BIG,
        cost_estimate=pl.CostEstimate(flops=2 * 288 * PADDED * D, bytes_accessed=2 * PADDED * D, transcendentals=0),
        name="gradient",
    )(e, near(embedding), stats)


def product_kernel(e_ref, embedding_ref, out_ref):
    for y in range(4):
        out_ref[:, y * WIDE : (y + 1) * WIDE] = jnp.dot(
            e_ref[...], embedding_ref[:, y * WIDE : (y + 1) * WIDE], preferred_element_type=F32
        )


def product_of(e, embedding):
    return pl.pallas_call(
        product_kernel,
        in_specs=[WHOLE] * 2,
        out_specs=WHOLE,
        out_shape=pltpu.VMEM((288, D), F32),
        compiler_params=BIG,
        cost_estimate=pl.CostEstimate(flops=2 * 288 * PADDED * D, bytes_accessed=2 * PADDED * D, transcendentals=0),
        name="product",
    )(e, near(embedding))


def combine_kernel(term_ref, stats_ref, other_ref, out_ref):
    last = lax.broadcasted_iota(jnp.int32, (8, WIDE), 0) == 7
    for x in range(4):
        values = [stats_ref[i : i + 1, x * BLOCK : (x + 1) * BLOCK] for i in range(3)]
        others = read_stats(other_ref[x, BLOCK : BLOCK + 8, :].astype(F32)[7:8, :])
        row = jnp.broadcast_to(stats_row([a + b for a, b in zip(values, others)]), (8, WIDE))
        for y in range(4):
            columns = slice(y * WIDE, (y + 1) * WIDE)
            main = term_ref[x * BLOCK : (x + 1) * BLOCK, columns] + other_ref[y * 4 + x, 0:BLOCK, :].astype(F32)
            out_ref[y * 4 + x, 0:BLOCK, :] = main.astype(BF16)
            extra = term_ref[256 + 8 * x : 256 + 8 * x + 8, columns] + other_ref[
                y * 4 + x, BLOCK : BLOCK + 8, :
            ].astype(F32)
            out_ref[y * 4 + x, BLOCK : BLOCK + 8, :] = jnp.where(last, row, extra).astype(BF16)


def combine(term, stats, other):
    return pl.pallas_call(
        combine_kernel,
        in_specs=[WHOLE] * 3,
        out_specs=WHOLE,
        out_shape=pltpu.VMEM((16, BLOCK + 8, WIDE), BF16),
        compiler_params=BIG,
        name="combine",
    )(term, stats, near(other))


def plane_kernel(in_ref, place_ref, more_ref, out_ref):
    total = in_ref[0, 0:BLOCK, :].astype(F32)
    for source in range(1, 16):
        total += in_ref[source, 0:BLOCK, :].astype(F32)
    extras = [in_ref[source, BLOCK : BLOCK + 8, :].astype(F32) for source in range(16)]
    stacked = jnp.concatenate(extras, axis=0).astype(BF16)
    label_rows = jnp.dot(place_ref[...], stacked, preferred_element_type=F32) + more_ref[...].astype(F32)
    row = extras[0][7:8, :]
    for source in range(1, 16):
        row = row + extras[source][7:8, :]
    pieces = []
    for value in read_stats(row):
        pieces += three_pieces(value)
    sums = jnp.concatenate(pieces + [jnp.zeros((1, 640 - 9 * BLOCK), F32)], axis=1)
    sums = jnp.broadcast_to(sums, (16, 640)).astype(BF16)
    for zl in range(4):
        for zh in range(2):
            main = total[zh * 32 : zh * 32 + 32, zl * PIECE : (zl + 1) * PIECE]
            rows = label_rows[zh * 32 : zh * 32 + 32, zl * PIECE : (zl + 1) * PIECE]
            both = jnp.concatenate([main, rows, jnp.zeros((32, 640 - 2 * PIECE), F32)], axis=1)
            out_ref[zl * 2 + zh, 0:32, :] = both.astype(BF16)
            out_ref[zl * 2 + zh, 32:48, :] = sums


def plane_sum(received, place, more):
    return pl.pallas_call(
        plane_kernel,
        in_specs=[WHOLE] * 3,
        out_specs=WHOLE,
        out_shape=pltpu.VMEM((8, 48, 640), BF16),
        compiler_params=BIG,
        name="plane_sum",
    )(near(received), near(place), near(more))


def final_kernel(half_ref, in_ref, values_ref, gain_ref, weight_ref, scale_ref, loss_ref, grad_ref):
    total = in_ref[0, 0:32, :].astype(F32)
    row = in_ref[0, 32:48, :].astype(F32)[0:1, :]
    for source in range(1, 8):
        total += in_ref[source, 0:32, :].astype(F32)
        row = row + in_ref[source, 32:48, :].astype(F32)[0:1, :]
    pick = lax.broadcasted_iota(jnp.int32, (32, BLOCK), 1) == half_ref[0] * 32 + lax.broadcasted_iota(
        jnp.int32, (32, BLOCK), 0
    )

    def column(i):
        value = sum(row[:, (3 * i + j) * BLOCK : (3 * i + j + 1) * BLOCK] for j in (2, 1, 0))
        return jnp.sum(jnp.where(pick, jnp.broadcast_to(value, (32, BLOCK)), 0.0), axis=1, keepdims=True)

    sum_exp, inner_others, raw = column(0), column(1), column(2)
    weight = weight_ref[...]
    scaling = scale_ref[:, 0:1]
    ratio = jnp.tanh(raw / CAP)
    capped = CAP * ratio
    log_total = jnp.log(sum_exp)
    loss = log_total - capped
    coefficient = (jnp.exp(capped - log_total) - 1.0) * weight * (1.0 - ratio * ratio)
    coefficient = coefficient.astype(BF16).astype(F32)
    share = weight / sum_exp
    grad_normed = total[:, 0:PIECE] * share + total[:, PIECE : 2 * PIECE] * coefficient
    inner = (inner_others * share + coefficient * raw) / scaling
    upstream = grad_normed * gain_ref[...].astype(F32)
    values = values_ref[...].astype(F32)
    grad_ref[...] = scaling * upstream - values * (scaling * scaling * scaling * inner / D)
    eye = lax.broadcasted_iota(jnp.int32, (32, 128), 0) == lax.broadcasted_iota(jnp.int32, (32, 128), 1)
    loss_ref[...] = jnp.sum(jnp.where(eye, jnp.broadcast_to(loss, (32, 128)), 0.0), axis=0, keepdims=True)


def finish(half, received, values, gain, weight, scale):
    return pl.pallas_call(
        final_kernel,
        in_specs=[SCALARS] + [WHOLE] * 5,
        out_specs=[WHOLE] * 2,
        out_shape=[jax.ShapeDtypeStruct((1, 128), F32), jax.ShapeDtypeStruct((32, PIECE), F32)],
        compiler_params=BIG,
        name="finish",
    )(half, *(near(a) for a in (received, values, gain, weight, scale)))


def swap_cores(array):
    return lax.ppermute(array, "core", [(0, 1), (1, 0)])


def on_device(residual, final_gain, embedding, labels, token_weight):
    zl, y, zh, x, core = (lax.axis_index(name) for name in ("z_lo", "y", "z_hi", "x", "core"))
    chip = ((zl * 4 + y) * 2 + zh) * 4 + x
    first = (chip * 2 + core) * ROWS

    mine = jnp.concatenate([residual, final_gain[None, :], jnp.zeros((15, PIECE), BF16)], axis=0)
    gathered = lax.all_to_all(
        jnp.broadcast_to(mine[None], (8, 48, PIECE)), ("z_lo", "z_hi"), 0, 0, tiled=True
    )
    copies, late_embedding = lax.optimization_barrier((pack_tokens(gathered), embedding))
    packed = lax.all_to_all(copies, ("y", "x"), 0, 0, tiled=True)

    token = jnp.arange(512, dtype=jnp.int32)
    group = (token // 32) % 2 * 4 + (token // 64) % 4
    owner = labels // (2 * ROWS)
    key = owner * 8 + group
    same = jnp.logical_and(key[:, None] == key[None, :], token[None, :] < token[:, None])
    rank = jnp.sum(same.astype(jnp.int32), axis=1)
    turn, slot = rank // SLOTS, rank % SLOTS
    slots = jnp.arange(64, dtype=jnp.int32)
    vocab = jnp.arange(PADDED, dtype=jnp.int32)

    def slot_rows(number):
        taken = jnp.where(jnp.logical_and(owner == chip, turn == number), group * 8 + slot, -1)
        match = taken[None, :] == slots[:, None]
        held = jnp.sum(jnp.where(match, (labels - first)[None, :] + 1, 0), axis=1) - 1
        return (held[:, None] == vocab[None, :]).astype(BF16)

    def by_half(array):
        return array.reshape(2, 4, 2, 32).transpose(2, 1, 0, 3)

    def own_tokens(array):
        return lax.dynamic_slice(by_half(array), (core, x, 0, 0), (1, 1, 2, 32)).reshape(BLOCK)

    own_owner, own_turn, own_slot = own_tokens(owner), own_tokens(turn), own_tokens(slot)
    own_chip = jnp.arange(16, dtype=jnp.int32)
    own_chip = ((zl * 4 + own_chip // 4) * 2 + zh) * 4 + own_chip % 4

    def places(number):
        hit = jnp.logical_and(own_owner[:, None] == own_chip[None, :], (own_turn == number)[:, None])
        at = own_slot[:, None] == jnp.arange(8, dtype=jnp.int32)[None, :]
        return jnp.logical_and(hit[:, :, None], at[:, None, :]).astype(BF16).reshape(BLOCK, 128)

    table = permute_embedding(late_embedding)

    def more_rows(carry):
        number, rows = carry
        found = jnp.dot(slot_rows(number)[:, :ROWS], embedding, preferred_element_type=F32).astype(BF16)
        found = found.reshape(2, 4, 8, 4, 4, PIECE).transpose(0, 4, 1, 2, 3, 5).reshape(2, 16, 8, WIDE)
        ours = lax.dynamic_index_in_dim(found, core, 0, keepdims=False)
        theirs = lax.dynamic_index_in_dim(found, 1 - core, 0, keepdims=False)
        ours = ours + swap_cores(theirs)
        ours = lax.all_to_all(ours, ("y", "x"), 0, 0, tiled=True).reshape(128, WIDE)
        return number + 1, rows + jnp.dot(places(number), ours, preferred_element_type=F32).astype(BF16)

    rounds = jnp.max(turn) + 1
    _, more = lax.while_loop(
        lambda carry: carry[0] < rounds, more_rows, (jnp.int32(1), jnp.zeros((BLOCK, WIDE), BF16))
    )

    label_halves = by_half(labels).reshape(2, 1, 256)
    slot_halves = slot_rows(0).reshape(2, 32, PADDED)

    def half_of(array, which):
        return lax.dynamic_index_in_dim(array, which, 0, keepdims=False)

    start = first.reshape(1)
    own_first = ((zh * 4 + x) * 2 + core) * 32
    weight = lax.dynamic_slice_in_dim(token_weight, own_first, 32, 0).reshape(32, 1)
    early = (
        table,
        half_of(label_halves, core),
        half_of(slot_halves, core),
        half_of(label_halves, 1 - core),
        half_of(slot_halves, 1 - core),
        places(0),
        more,
        weight,
    )
    packed, early = lax.optimization_barrier((packed, early))
    table, own_labels, own_slots, other_labels, other_slots, place, more, weight = early
    other_packed = swap_cores(packed)
    e, stats, scale = logits_of(start, packed, table, own_labels, own_slots)
    other_packed, e = lax.optimization_barrier((other_packed, e))
    e_other, stats_other, _ = logits_of(start, other_packed, table, other_labels, other_slots)
    other_part = gradient_of(e_other, table, stats_other)
    other_part, e = lax.optimization_barrier((other_part, e))
    payload = combine(product_of(e, table), stats, swap_cores(other_part))
    plane = lax.all_to_all(payload, ("y", "x"), 0, 0, tiled=True)
    column = lax.all_to_all(plane_sum(plane, place, more), ("z_lo", "z_hi"), 0, 0, tiled=True)

    own_scale = lax.dynamic_slice_in_dim(scale, x * BLOCK + zh * 32, 32, 0)
    loss, grad = finish(zh.reshape(1), column, residual, final_gain.reshape(1, PIECE), weight, own_scale)
    return (loss[0, 0:32], grad)


def solution(mesh):
    fine = Mesh(mesh.devices.reshape(4, 4, 2, 4, 2), ("z_lo", "y", "z_hi", "x", "core"))
    section, fsdp = ("z_lo", "y"), ("z_hi", "x", "core")
    in_specs = (P(fsdp, section), P(section), P(section + fsdp, None), P(), P())
    out_specs = (P(fsdp), P(fsdp, section))
    return jax.shard_map(on_device, mesh=fine, in_specs=in_specs, out_specs=out_specs, check_vma=False)
```

```python
import functools

import jax
import jax.numpy as jnp
from jax import lax
from jax.experimental import pallas as pl
from jax.experimental.pallas import tpu as pltpu
from jax.sharding import Mesh, PartitionSpec as P

D = 4608
EPS = 1e-06
CAP = 30.0
ROWS = 1000
PADDED = 1024
PIECE = 288
WIDE = 1152
HALF = 2 * WIDE
BLOCK = 64
ROOM = BLOCK + 8
TILES = WIDE // 128
SLOTS = 7
PACKED = TILES * BLOCK + 16
F32 = jnp.float32
BF16 = jnp.bfloat16
VMEM = pltpu.MemorySpace.VMEM
WHOLE = pl.BlockSpec(memory_space=VMEM)
SCALARS = pl.BlockSpec(memory_space=pltpu.MemorySpace.SMEM)
BIG = pltpu.CompilerParams(vmem_limit_bytes=20 * 1024 * 1024)


def near(array):
    return pltpu.with_memory_space_constraint(array, VMEM)


CHIPS = ("z_lo", "y1", "y0", "z_hi", "x1", "x0")
SHIFTS = {(0, 1): (1, 0), (1, 0): (0, 1), (1, 1): (-1, -1)}


def this_chip():
    number = 0
    for name in CHIPS:
        number = number * lax.axis_size(name) + lax.axis_index(name)
    return number


def first_row():
    return (this_chip() * 2 + lax.axis_index("core")) * ROWS


def label_kernel(labels_ref, own_labels, own_slots, other_labels, other_slots, place_ref, rounds_ref):
    zl, y1, y0, zh, x1, x0, core = (lax.axis_index(name) for name in (*CHIPS, "core"))
    labels = labels_ref[...]
    token = lax.broadcasted_iota(jnp.int32, (1, 512), 1)
    group = (token >> 5 & 1) * 4 + (token >> 6 & 1) * 2 + (token >> 7 & 1)
    owner = ((labels.astype(F32) + 0.5) * (1.0 / (2 * ROWS))).astype(jnp.int32)
    key = owner * 8 + group
    square = (512, 512)
    down = lax.broadcasted_iota(jnp.int32, square, 0)
    across = lax.broadcasted_iota(jnp.int32, square, 1)
    keys = jnp.broadcast_to(key, square)
    key_down = jnp.sum(jnp.where(down == across, keys, 0), axis=1, keepdims=True)
    earlier = jnp.logical_and(jnp.broadcast_to(key_down, square) == keys, down < across)
    rank = jnp.sum(earlier.astype(jnp.int32), axis=0, keepdims=True)
    turn = ((rank.astype(F32) + 0.5) * (1.0 / SLOTS)).astype(jnp.int32)
    slot = rank - turn * SLOTS
    rounds_ref[...] = jnp.broadcast_to(jnp.max(turn, axis=1, keepdims=True) + 1, (1, 128))

    taken = jnp.where(jnp.logical_and(owner == this_chip(), turn == 0), group * 8 + slot, -1)
    shifted_labels = labels - first_row() + 1
    for half, label_ref, slot_ref in ((core, own_labels, own_slots), (1 - core, other_labels, other_slots)):
        at = lax.broadcasted_iota(jnp.int32, (32, 512), 0)
        wanted = half * 32 + (at + 16 * x0 & 31)
        match = jnp.broadcast_to(taken, (32, 512)) == wanted
        held = jnp.sum(jnp.where(match, jnp.broadcast_to(shifted_labels, (32, 512)), 0), axis=1, keepdims=True) - 1
        vocab = lax.broadcasted_iota(jnp.int32, (32, PADDED), 1)
        slot_ref[...] = jnp.where(vocab == held, 1.0, 0.0).astype(BF16)
        chunks = []
        for chunk in range(8):
            rx, from_x1, from_zh = chunk // 4, chunk // 2 % 2, chunk % 2
            picked = jnp.zeros((1, 32), jnp.int32)
            for from_x0 in range(2):
                for from_core in range(2):
                    source = ((from_zh * 2 + from_x1) * 2 + from_x0) * 2 + from_core
                    use = jnp.logical_and(half == from_core, (x0 + rx) % 2 == from_x0)
                    picked = jnp.where(use, labels[:, source * 32 : source * 32 + 32], picked)
            chunks.append(picked)
        label_ref[...] = jnp.concatenate(chunks, axis=1)

    code = jnp.broadcast_to(jnp.where(turn == 0, owner * 8 + slot, -1), (BLOCK, 512))
    at = lax.broadcasted_iota(jnp.int32, (BLOCK, 512), 0)
    own = (at >> 5) * 256 + x1 * 128 + x0 * 64 + core * 32 + (at & 31)
    pick = lax.broadcasted_iota(jnp.int32, (BLOCK, 512), 1) == own
    own_code = jnp.sum(jnp.where(pick, code, 0), axis=1, keepdims=True)
    column = lax.broadcasted_iota(jnp.int32, (BLOCK, 128), 1)
    parity = column >> 3 & 3
    from_y = (column >> 6) * 2 + y0 + 4
    from_x = (column >> 5 & 1) * 2 + x0 + 4
    for index, (dx, dy) in enumerate(SHIFTS.values()):
        from_y = from_y - jnp.where(parity == index + 1, dy, 0)
        from_x = from_x - jnp.where(parity == index + 1, dx, 0)
    chip = ((zl * 4 + (from_y & 3)) * 2 + zh) * 4 + (from_x & 3)
    place_ref[...] = jnp.where(own_code == chip * 8 + (column & 7), 1.0, 0.0).astype(BF16)


def label_places(labels):
    return pl.pallas_call(
        label_kernel,
        in_specs=[WHOLE],
        out_specs=[WHOLE] * 6,
        out_shape=[
            pltpu.VMEM((1, 256), jnp.int32),
            pltpu.VMEM((32, PADDED), BF16),
            pltpu.VMEM((1, 256), jnp.int32),
            pltpu.VMEM((32, PADDED), BF16),
            pltpu.VMEM((BLOCK, 128), BF16),
            jax.ShapeDtypeStruct((1, 128), jnp.int32),
        ],
        compiler_params=BIG,
        cost_estimate=pl.CostEstimate(flops=10 * 512 * 512, bytes_accessed=1 << 20, transcendentals=0),
        name="label_places",
    )(labels)


def permute_kernel(in_ref, out_ref):
    step = in_ref.shape[0]
    first = pl.multiple_of(pl.program_id(0) * step, step)
    rows = first + lax.broadcasted_iota(jnp.int32, (step, 1), 0)
    block = jnp.where(rows < ROWS, in_ref[...].astype(F32), 0.0)
    for y0 in range(2):

        @pl.when(lax.axis_index("y0") == y0)
        def _():
            for at in range(4):
                y = at % 2 * 2 + (at // 2 + y0) % 2
                parts = [block[:, (z * 4 + y) * PIECE : (z * 4 + y + 1) * PIECE] for z in range(4)]
                wide = jnp.concatenate(parts, axis=1).astype(BF16)
                out_ref[pl.ds(first, step), at * WIDE : (at + 1) * WIDE] = wide


def permute_embedding(embedding):
    step = 128
    return pl.pallas_call(
        permute_kernel,
        grid=(PADDED // step,),
        in_specs=[pl.BlockSpec((step, D), lambda i: (i, 0))],
        out_specs=WHOLE,
        out_shape=pltpu.VMEM((PADDED, D), BF16),
        compiler_params=BIG,
        cost_estimate=pl.CostEstimate(flops=0, bytes_accessed=4 * ROWS * D, transcendentals=0),
        name="permute_embedding",
    )(embedding)


def spread_kernel(residual_ref, gain_ref, out_ref):
    values = residual_ref[...].astype(F32)
    gain = gain_ref[...].astype(F32)
    corner = jnp.concatenate([values[8 * g : 8 * g + 8, 256:PIECE] for g in range(4)], axis=1)
    last = jnp.concatenate([gain[:, 256:PIECE], jnp.zeros((1, 96), F32)], axis=1)
    rows = [values[:, 0:128], values[:, 128:256], corner, gain[:, 0:128], gain[:, 128:256], last, jnp.zeros((5, 128), F32)]
    tiles = jnp.concatenate(rows, axis=0).astype(BF16)
    for copy in range(8):
        out_ref[copy] = tiles


def spread(residual, gain):
    return pl.pallas_call(
        spread_kernel,
        in_specs=[WHOLE] * 2,
        out_specs=WHOLE,
        out_shape=pltpu.VMEM((8, 80, 128), BF16),
        compiler_params=BIG,
        name="spread",
    )(residual, gain)


def pack_kernel(in_ref, out_ref):
    for zh in range(2):
        parts = []
        for zl in range(4):
            tiles = in_ref[zl * 2 + zh].astype(F32)
            corner = jnp.concatenate([tiles[64:72, 32 * g : 32 * g + 32] for g in range(4)], axis=0)
            parts += [tiles[0:32, :], tiles[32:64, :], corner]
        wide = jnp.concatenate(parts, axis=1)
        for k in range(TILES):
            tile = wide[:, k * 128 : (k + 1) * 128].astype(BF16)
            for copy in range(4):
                out_ref[copy, k * BLOCK + zh * 32 : k * BLOCK + zh * 32 + 32, :] = tile
    parts = []
    for zl in range(4):
        tiles = in_ref[zl * 2].astype(F32)
        parts += [tiles[72:73, :], tiles[73:74, :], tiles[74:75, 0:32]]
    gains = jnp.concatenate(parts, axis=1)
    rows = [gains[:, k * 128 : (k + 1) * 128] for k in range(TILES)]
    tile = jnp.concatenate(rows + [jnp.zeros((16 - TILES, 128), F32)], axis=0).astype(BF16)
    for copy in range(4):
        out_ref[copy, TILES * BLOCK : PACKED, :] = tile


def pack_tokens(gathered):
    return pl.pallas_call(
        pack_kernel,
        in_specs=[WHOLE],
        out_specs=WHOLE,
        out_shape=pltpu.VMEM((4, PACKED, 128), BF16),
        compiler_params=BIG,
        name="pack_tokens",
    )(near(gathered))


def logits_kernel(*refs):
    blocks, (embedding_ref, labels_ref, slot_ref, e_ref, stats_ref, scale_ref, normed) = refs[:4], refs[4:]
    gains = [
        [blocks[ry * 2][y1 * 2, TILES * BLOCK : PACKED, :].astype(F32) for y1 in range(2)] for ry in range(2)
    ]
    for x in range(4):
        tokens = slice(x * BLOCK, (x + 1) * BLOCK)

        def tile(ry, y1, k):
            return blocks[ry * 2 + x // 2][y1 * 2 + x % 2, k * BLOCK : (k + 1) * BLOCK, :].astype(F32)

        places = [(ry, y1, k) for ry in range(2) for y1 in range(2) for k in range(TILES)]
        squares = jnp.zeros((BLOCK, 128), F32)
        for place in places:
            v = tile(*place)
            squares += v * v
        scale = lax.rsqrt(jnp.sum(squares, axis=1, keepdims=True) / D + EPS)
        scale_ref[tokens, :] = jnp.broadcast_to(scale, (BLOCK, 128))
        for ry, y1, k in places:
            column = ry * HALF + y1 * WIDE + k * 128
            normed[tokens, column : column + 128] = (
                tile(ry, y1, k) * scale * gains[ry][y1][k : k + 1, :]
            ).astype(BF16)
    raw = lax.dot_general(
        embedding_ref[...], normed[...], (((1,), (1,)), ((), ())), preferred_element_type=F32
    )
    ratio = jnp.tanh(raw / CAP)
    row = lax.broadcasted_iota(jnp.int32, raw.shape, 0)
    inside = row < ROWS
    is_label = jnp.logical_and(inside, row + first_row() == labels_ref[...])
    exps = jnp.where(inside, jnp.exp(CAP * ratio), 0.0)
    others = jnp.where(is_label, 0.0, exps * (1.0 - ratio * ratio))
    stats_ref[0:1, :] = jnp.sum(exps, axis=0, keepdims=True)
    stats_ref[1:2, :] = jnp.sum(others * raw, axis=0, keepdims=True)
    stats_ref[2:3, :] = jnp.sum(jnp.where(is_label, raw, 0.0), axis=0, keepdims=True)
    stats_ref[3:8, :] = jnp.zeros((5, raw.shape[1]), F32)
    e_ref[0:256, :] = others.T.astype(BF16)
    e_ref[256:288, :] = slot_ref[...]


def logits_of(blocks, embedding, labels, slots):
    return pl.pallas_call(
        logits_kernel,
        in_specs=[WHOLE] * 7,
        out_specs=[WHOLE] * 3,
        out_shape=[
            pltpu.VMEM((288, PADDED), BF16),
            pltpu.VMEM((8, 256), F32),
            pltpu.VMEM((256, 128), F32),
        ],
        scratch_shapes=[pltpu.VMEM((256, D), BF16)],
        compiler_params=BIG,
        cost_estimate=pl.CostEstimate(flops=2 * 256 * PADDED * D, bytes_accessed=2 * PADDED * D, transcendentals=2 * 256 * PADDED),
        name="logits",
    )(*(near(a) for a in (*blocks, embedding, labels, slots)))


def three_pieces(value):
    high = value.astype(BF16).astype(F32)
    middle = (value - high).astype(BF16).astype(F32)
    low = (value - high - middle).astype(BF16).astype(F32)
    return [high, middle, low]


def stats_row(values):
    pieces = []
    for value in values:
        for piece in three_pieces(value):
            pieces += [piece, jnp.zeros((1, 128 - BLOCK), F32)]
    return jnp.concatenate(pieces, axis=1)


def read_stats(row):
    return [
        sum(row[:, (3 * i + j) * 128 : (3 * i + j) * 128 + BLOCK] for j in (2, 1, 0))
        for i in range(3)
    ]


def gradient_kernel(ry, e_ref, embedding_ref, stats_ref, out_ref):
    last = lax.broadcasted_iota(jnp.int32, (8, WIDE), 0) == 7
    rows = []
    for x in range(4):
        values = [stats_ref[i : i + 1, x * BLOCK : (x + 1) * BLOCK] for i in range(3)]
        rows.append(jnp.broadcast_to(stats_row(values), (8, WIDE)))
    for y1 in range(2):
        column = ry * HALF + y1 * WIDE
        term = jnp.dot(e_ref[...], embedding_ref[:, column : column + WIDE], preferred_element_type=F32)
        for x in range(4):
            at = (x // 2 * 2 + y1) * 2 + x % 2
            out_ref[at, 0:BLOCK, :] = term[x * BLOCK : (x + 1) * BLOCK, :].astype(BF16)
            extra = term[256 + 8 * x : 256 + 8 * x + 8, :]
            out_ref[at, BLOCK:ROOM, :] = jnp.where(last, rows[x], extra).astype(BF16)


def gradient_of(ry, e, embedding, stats):
    return pl.pallas_call(
        functools.partial(gradient_kernel, ry),
        in_specs=[WHOLE] * 3,
        out_specs=WHOLE,
        out_shape=pltpu.VMEM((8, ROOM, WIDE), BF16),
        compiler_params=BIG,
        cost_estimate=pl.CostEstimate(flops=288 * PADDED * D, bytes_accessed=PADDED * D, transcendentals=0),
        name="gradient",
    )(e, near(embedding), stats)


def product_kernel(ry, e_ref, embedding_ref, out_ref):
    out_ref[...] = jnp.dot(
        e_ref[...], embedding_ref[:, ry * HALF : (ry + 1) * HALF], preferred_element_type=F32
    )


def product_of(ry, e, embedding):
    return pl.pallas_call(
        functools.partial(product_kernel, ry),
        in_specs=[WHOLE] * 2,
        out_specs=WHOLE,
        out_shape=pltpu.VMEM((288, HALF), F32),
        compiler_params=BIG,
        cost_estimate=pl.CostEstimate(flops=288 * PADDED * D, bytes_accessed=PADDED * D, transcendentals=0),
        name="product",
    )(e, near(embedding))


def combine_kernel(term_ref, stats_ref, other_ref, *out_refs):
    last = lax.broadcasted_iota(jnp.int32, (8, WIDE), 0) == 7
    for x in range(4):
        values = [stats_ref[i : i + 1, x * BLOCK : (x + 1) * BLOCK] for i in range(3)]
        others = read_stats(other_ref[x // 2 * 4 + x % 2, BLOCK:ROOM, :].astype(F32)[7:8, :])
        row = jnp.broadcast_to(stats_row([a + b for a, b in zip(values, others)]), (8, WIDE))
        for y1 in range(2):
            at = (x // 2 * 2 + y1) * 2 + x % 2
            out_ref = out_refs[x // 2]
            columns = slice(y1 * WIDE, (y1 + 1) * WIDE)
            main = term_ref[x * BLOCK : (x + 1) * BLOCK, columns] + other_ref[at, 0:BLOCK, :].astype(F32)
            out_ref[y1 * 2 + x % 2, 0:BLOCK, :] = main.astype(BF16)
            extra = term_ref[256 + 8 * x : 256 + 8 * x + 8, columns] + other_ref[at, BLOCK:ROOM, :].astype(F32)
            out_ref[y1 * 2 + x % 2, BLOCK:ROOM, :] = jnp.where(last, row, extra).astype(BF16)


def combine(term, stats, other):
    return pl.pallas_call(
        combine_kernel,
        in_specs=[WHOLE] * 3,
        out_specs=[WHOLE] * 2,
        out_shape=[pltpu.VMEM((4, ROOM, WIDE), BF16)] * 2,
        compiler_params=BIG,
        name="combine",
    )(term, stats, near(other))


def class_kernel(*refs):
    in_refs, out_ref = refs[:4], refs[4]
    last = lax.broadcasted_iota(jnp.int32, (8, WIDE), 0) == 7
    for block in range(4):
        total = in_refs[0][block, 0:BLOCK, :].astype(F32)
        for ref in in_refs[1:]:
            total += ref[block, 0:BLOCK, :].astype(F32)
        out_ref[block, 0:BLOCK, :] = total.astype(BF16)
        extras = [ref[block, BLOCK:ROOM, :].astype(F32) for ref in in_refs]
        row = sum(extra[7:8, :] for extra in extras)
        row = jnp.broadcast_to(stats_row(read_stats(row)), (8, WIDE))
        extras = [jnp.where(last, row if i == 0 else 0.0, extra) for i, extra in enumerate(extras)]
        out_ref[block, BLOCK : BLOCK + 32, :] = jnp.concatenate(extras, axis=0).astype(BF16)


def class_sum(blocks):
    return pl.pallas_call(
        class_kernel,
        in_specs=[WHOLE] * 4,
        out_specs=WHOLE,
        out_shape=pltpu.VMEM((4, BLOCK + 32, WIDE), BF16),
        compiler_params=BIG,
        name="class_sum",
    )(*(near(a) for a in blocks))


def plane_kernel(in_ref, place_ref, more_ref, out_ref):
    total = in_ref[0, 0:BLOCK, :].astype(F32)
    for source in range(1, 4):
        total += in_ref[source, 0:BLOCK, :].astype(F32)
    extras = [in_ref[source, BLOCK : BLOCK + 32, :].astype(F32) for source in range(4)]
    stacked = jnp.concatenate(extras, axis=0).astype(BF16)
    label_rows = jnp.dot(place_ref[...], stacked, preferred_element_type=F32) + more_ref[...].astype(F32)
    row = sum(extra[7:8, :] for extra in extras)
    pieces = []
    for value in read_stats(row):
        pieces += three_pieces(value)
    sums = jnp.concatenate(pieces + [jnp.zeros((32 - 9, BLOCK), F32)], axis=0)
    for zl in range(4):
        for zh in range(2):
            main = total[zh * 32 : zh * 32 + 32, zl * PIECE : (zl + 1) * PIECE]
            rows = label_rows[zh * 32 : zh * 32 + 32, zl * PIECE : (zl + 1) * PIECE]
            out_ref[zl * 2 + zh] = jnp.concatenate([main, rows, sums], axis=1).astype(BF16)


def plane_sum(received, place, more):
    return pl.pallas_call(
        plane_kernel,
        in_specs=[WHOLE] * 3,
        out_specs=WHOLE,
        out_shape=pltpu.VMEM((8, 32, 640), BF16),
        compiler_params=BIG,
        name="plane_sum",
    )(near(received), near(place), near(more))


def final_kernel(in_ref, values_ref, gain_ref, weight_ref, scale_ref, loss_ref, grad_ref):
    zh, x1, x0, core = (lax.axis_index(name) for name in ("z_hi", "x1", "x0", "core"))
    total = in_ref[0].astype(F32)
    for source in range(1, 8):
        total += in_ref[source].astype(F32)
    sums = total[0:16, 2 * PIECE : 640]
    pick = lax.broadcasted_iota(jnp.int32, (32, BLOCK), 1) == zh * 32 + lax.broadcasted_iota(
        jnp.int32, (32, BLOCK), 0
    )

    def column(i):
        value = sum(sums[3 * i + j : 3 * i + j + 1, :] for j in (2, 1, 0))
        return jnp.sum(jnp.where(pick, jnp.broadcast_to(value, (32, BLOCK)), 0.0), axis=1, keepdims=True)

    sum_exp, inner_others, raw = column(0), column(1), column(2)
    own = (((zh * 2 + x1) * 2 + x0) * 2 + core) * 32 + lax.broadcasted_iota(jnp.int32, (32, 512), 0)
    own_weight = jnp.where(lax.broadcasted_iota(jnp.int32, (32, 512), 1) == own, weight_ref[...], 0.0)
    weight = jnp.sum(own_weight, axis=1, keepdims=True)
    scaling = scale_ref[pl.ds(pl.multiple_of(x1 * BLOCK + zh * 32, 32), 32), 0:1]
    ratio = jnp.tanh(raw / CAP)
    capped = CAP * ratio
    log_total = jnp.log(sum_exp)
    loss = log_total - capped
    coefficient = (jnp.exp(capped - log_total) - 1.0) * weight * (1.0 - ratio * ratio)
    coefficient = coefficient.astype(BF16).astype(F32)
    share = weight / sum_exp
    grad_normed = total[:, 0:PIECE] * share + total[:, PIECE : 2 * PIECE] * coefficient
    inner = (inner_others * share + coefficient * raw) / scaling
    upstream = grad_normed * gain_ref[...].astype(F32)
    values = values_ref[...].astype(F32)
    grad_ref[...] = scaling * upstream - values * (scaling * scaling * scaling * inner / D)
    eye = lax.broadcasted_iota(jnp.int32, (32, 32), 0) == lax.broadcasted_iota(jnp.int32, (32, 32), 1)
    loss_ref[...] = jnp.sum(jnp.where(eye, jnp.broadcast_to(loss, (32, 32)), 0.0), axis=0, keepdims=True)


def finish(received, values, gain, weight, scale):
    return pl.pallas_call(
        final_kernel,
        in_specs=[WHOLE] * 5,
        out_specs=[WHOLE] * 2,
        out_shape=[jax.ShapeDtypeStruct((1, 32), F32), jax.ShapeDtypeStruct((32, PIECE), F32)],
        compiler_params=BIG,
        name="finish",
    )(*(near(a) for a in (received, values, gain, weight, scale)))


def swap_cores(array):
    return lax.ppermute(array, "core", [(0, 1), (1, 0)])


def shifted(array, parity):
    dx, dy = SHIFTS[parity]
    pairs = []
    for chip in range(128):
        line, y, zh, x = chip // 32, chip // 8 % 4, chip // 4 % 2, chip % 4
        pairs.append((chip, ((line * 4 + (y + dy) % 4) * 2 + zh) * 4 + (x + dx) % 4))
    return lax.ppermute(array, CHIPS, pairs)


def later_rows(labels, embedding, rounds):
    def one_round(carry):
        number, rows = carry
        _, tokens = lax.optimization_barrier((number, labels))
        zl, y1, y0, zh, x1, x0, core = (lax.axis_index(name) for name in (*CHIPS, "core"))
        token = jnp.arange(512, dtype=jnp.int32)
        group = (token // 32) % 2 * 4 + (token // 64) % 2 * 2 + (token // 128) % 2
        owner = tokens // (2 * ROWS)
        key = owner * 8 + group
        same = jnp.logical_and(key[:, None] == key[None, :], token[None, :] < token[:, None])
        rank = jnp.sum(same.astype(jnp.int32), axis=1)
        turn, slot = rank // SLOTS, rank % SLOTS
        taken = jnp.where(jnp.logical_and(owner == this_chip(), turn == number), group * 8 + slot, -1)
        match = taken[None, :] == jnp.arange(64, dtype=jnp.int32)[:, None]
        held = jnp.sum(jnp.where(match, (tokens - first_row())[None, :] + 1, 0), axis=1) - 1
        chosen = (held[:, None] == jnp.arange(ROWS, dtype=jnp.int32)[None, :]).astype(BF16)
        found = jnp.dot(chosen, embedding, preferred_element_type=F32).astype(BF16)
        found = found.reshape(2, 2, 2, 8, 4, 4, PIECE).transpose(0, 5, 2, 1, 3, 4, 6).reshape(2, 16, 8, WIDE)
        ours = lax.dynamic_index_in_dim(found, core, 0, keepdims=False)
        theirs = lax.dynamic_index_in_dim(found, 1 - core, 0, keepdims=False)
        ours = ours + swap_cores(theirs)
        ours = lax.all_to_all(ours, ("y1", "y0", "x1", "x0"), 0, 0, tiled=True).reshape(128, WIDE)
        local = jnp.arange(BLOCK, dtype=jnp.int32)
        own = (((local // 32 * 2 + x1) * 2 + x0) * 2 + core) * 32 + local % 32
        place = jnp.arange(16, dtype=jnp.int32)
        chips = ((zl * 4 + place // 4) * 2 + zh) * 4 + place % 4
        hit = jnp.logical_and(owner[own][:, None] == chips[None, :], (turn[own] == number)[:, None])
        at = slot[own][:, None] == jnp.arange(8, dtype=jnp.int32)[None, :]
        put = jnp.logical_and(hit[:, :, None], at[:, None, :]).astype(BF16).reshape(BLOCK, 128)
        return number + 1, rows + jnp.dot(put, ours, preferred_element_type=F32).astype(BF16)

    start = (jnp.int32(1), jnp.zeros((BLOCK, WIDE), BF16))
    return lax.while_loop(lambda carry: carry[0] < rounds, one_round, start)[1]


def on_device(residual, final_gain, embedding, labels, token_weight):
    gain = final_gain.reshape(1, PIECE)
    gathered = lax.all_to_all(spread(residual, gain), ("z_lo", "z_hi"), 0, 0, tiled=True)
    own_labels, own_slots, other_labels, other_slots, place, rounds = label_places(labels.reshape(1, 512))
    more = later_rows(labels, embedding, rounds[0, 0])
    early = (own_labels, own_slots, other_labels, other_slots, place, more)
    copies, embedding, early = lax.optimization_barrier((pack_tokens(gathered), embedding, early))
    own_labels, own_slots, other_labels, other_slots, place, more = early

    packed = lax.all_to_all(copies, ("y1", "x1"), 0, 0, tiled=True)
    table = permute_embedding(embedding)
    blocks = [packed] + [shifted(packed, parity) for parity in SHIFTS]
    blocks[1:], table = lax.optimization_barrier((blocks[1:], table))
    other_blocks = [swap_cores(block) for block in blocks]

    e, stats, scale = logits_of(blocks, table, own_labels, own_slots)
    other_blocks, e = lax.optimization_barrier((other_blocks, e))
    e_other, stats_other, _ = logits_of(other_blocks, table, other_labels, other_slots)
    far_part, e_other = lax.optimization_barrier((gradient_of(1, e_other, table, stats_other), e_other))
    near_part, e = lax.optimization_barrier((gradient_of(0, e_other, table, stats_other), e))
    far_blocks = combine(product_of(1, e, table), stats, swap_cores(far_part))
    far_blocks, e = lax.optimization_barrier((far_blocks, e))
    near_blocks = combine(product_of(0, e, table), stats, swap_cores(near_part))
    parts = [*near_blocks, *far_blocks]
    mine = class_sum([parts[0]] + [shifted(part, parity) for part, parity in zip(parts[1:], SHIFTS)])
    plane = lax.all_to_all(mine, ("y1", "x1"), 0, 0, tiled=True)
    column = lax.all_to_all(plane_sum(plane, place, more), ("z_lo", "z_hi"), 0, 0, tiled=True)

    loss, grad = finish(column, residual, gain, token_weight.reshape(1, 512), scale)
    return (loss.reshape(32), grad)


def solution(mesh):
    fine = Mesh(mesh.devices.reshape(4, 2, 2, 2, 2, 2, 2), (*CHIPS, "core"))
    section, fsdp = ("z_lo", "y1", "y0"), ("z_hi", "x1", "x0", "core")
    in_specs = (P(fsdp, section), P(section), P(section + fsdp, None), P(), P())
    out_specs = (P(fsdp), P(fsdp, section))
    return jax.shard_map(on_device, mesh=fine, in_specs=in_specs, out_specs=out_specs, check_vma=False)
```

```python
import functools

import jax
import jax.numpy as jnp
from jax import lax
from jax.experimental import pallas as pl
from jax.experimental.pallas import tpu as pltpu
from jax.sharding import Mesh, PartitionSpec as P

D = 4608
EPS = 1e-06
CAP = 30.0
ROWS = 1000
PADDED = 1024
PIECE = 288
WIDE = 1152
HALF = 2 * WIDE
BLOCK = 64
ROOM = BLOCK + 8
TILES = WIDE // 128
SLOTS = 7
PACKED = TILES * BLOCK + 16
F32 = jnp.float32
BF16 = jnp.bfloat16
VMEM = pltpu.MemorySpace.VMEM
WHOLE = pl.BlockSpec(memory_space=VMEM)
SCALARS = pl.BlockSpec(memory_space=pltpu.MemorySpace.SMEM)
BIG = pltpu.CompilerParams(vmem_limit_bytes=20 * 1024 * 1024)


def near(array):
    return pltpu.with_memory_space_constraint(array, VMEM)


CHIPS = ("z_lo", "y1", "y0", "z_hi", "x1", "x0")
SHIFTS = {(0, 1): (1, 0), (1, 0): (0, 1), (1, 1): (-1, -1)}
PLACES = ((0, 0), *SHIFTS)


def this_chip():
    number = 0
    for name in CHIPS:
        number = number * lax.axis_size(name) + lax.axis_index(name)
    return number


def first_row():
    return (this_chip() * 2 + lax.axis_index("core")) * ROWS


def label_kernel(labels_ref, own_labels, own_slots, other_labels, other_slots, place_ref, rounds_ref):
    zl, y1, y0, zh, x1, x0, core = (lax.axis_index(name) for name in (*CHIPS, "core"))
    labels = labels_ref[...]
    token = lax.broadcasted_iota(jnp.int32, (1, 512), 1)
    group = (token >> 5 & 1) * 4 + (token >> 6 & 1) * 2 + (token >> 7 & 1)
    owner = ((labels.astype(F32) + 0.5) * (1.0 / (2 * ROWS))).astype(jnp.int32)
    key = owner * 8 + group
    square = (512, 512)
    down = lax.broadcasted_iota(jnp.int32, square, 0)
    across = lax.broadcasted_iota(jnp.int32, square, 1)
    keys = jnp.broadcast_to(key, square)
    key_down = jnp.sum(jnp.where(down == across, keys, 0), axis=1, keepdims=True)
    earlier = jnp.logical_and(jnp.broadcast_to(key_down, square) == keys, down < across)
    rank = jnp.sum(earlier.astype(jnp.int32), axis=0, keepdims=True)
    turn = ((rank.astype(F32) + 0.5) * (1.0 / SLOTS)).astype(jnp.int32)
    slot = rank - turn * SLOTS
    rounds_ref[...] = jnp.broadcast_to(jnp.max(turn, axis=1, keepdims=True) + 1, (1, 128))

    taken = jnp.where(jnp.logical_and(owner == this_chip(), turn == 0), group * 8 + slot, -1)
    shifted_labels = labels - first_row() + 1
    for half, label_ref, slot_ref in ((core, own_labels, own_slots), (1 - core, other_labels, other_slots)):
        at = lax.broadcasted_iota(jnp.int32, (32, 512), 0)
        wanted = half * 32 + (at + 16 * x0 & 31)
        match = jnp.broadcast_to(taken, (32, 512)) == wanted
        held = jnp.sum(jnp.where(match, jnp.broadcast_to(shifted_labels, (32, 512)), 0), axis=1, keepdims=True) - 1
        vocab = lax.broadcasted_iota(jnp.int32, (32, PADDED), 1)
        slot_ref[...] = jnp.where(vocab == held, 1.0, 0.0).astype(BF16)
        chunks = []
        for chunk in range(8):
            rx, from_x1, from_zh = chunk // 4, chunk // 2 % 2, chunk % 2
            picked = jnp.zeros((1, 32), jnp.int32)
            for from_x0 in range(2):
                for from_core in range(2):
                    source = ((from_zh * 2 + from_x1) * 2 + from_x0) * 2 + from_core
                    use = jnp.logical_and(half == from_core, (x0 + rx) % 2 == from_x0)
                    picked = jnp.where(use, labels[:, source * 32 : source * 32 + 32], picked)
            chunks.append(picked)
        label_ref[...] = jnp.concatenate(chunks, axis=1)

    code = jnp.broadcast_to(jnp.where(turn == 0, owner * 8 + slot, -1), (BLOCK, 512))
    at = lax.broadcasted_iota(jnp.int32, (BLOCK, 512), 0)
    own = (at >> 5) * 256 + x1 * 128 + x0 * 64 + core * 32 + (at & 31)
    pick = lax.broadcasted_iota(jnp.int32, (BLOCK, 512), 1) == own
    own_code = jnp.sum(jnp.where(pick, code, 0), axis=1, keepdims=True)
    column = lax.broadcasted_iota(jnp.int32, (BLOCK, 128), 1)
    parity = column >> 3 & 3
    from_y = (column >> 6 ^ y1) * 2 + y0 + 4
    from_x = (column >> 5 & 1 ^ x1) * 2 + x0 + 4
    for index, (dx, dy) in enumerate(SHIFTS.values()):
        from_y = from_y - jnp.where(parity == index + 1, dy, 0)
        from_x = from_x - jnp.where(parity == index + 1, dx, 0)
    chip = ((zl * 4 + (from_y & 3)) * 2 + zh) * 4 + (from_x & 3)
    place_ref[...] = jnp.where(own_code == chip * 8 + (column & 7), 1.0, 0.0).astype(BF16)


def label_places(labels):
    return pl.pallas_call(
        label_kernel,
        in_specs=[WHOLE],
        out_specs=[WHOLE] * 6,
        out_shape=[
            pltpu.VMEM((1, 256), jnp.int32),
            pltpu.VMEM((32, PADDED), BF16),
            pltpu.VMEM((1, 256), jnp.int32),
            pltpu.VMEM((32, PADDED), BF16),
            pltpu.VMEM((BLOCK, 128), BF16),
            jax.ShapeDtypeStruct((1, 128), jnp.int32),
        ],
        compiler_params=BIG,
        cost_estimate=pl.CostEstimate(flops=10 * 512 * 512, bytes_accessed=1 << 20, transcendentals=0),
        name="label_places",
    )(labels)


def far(array):
    return pltpu.with_memory_space_constraint(array, pltpu.MemorySpace.HBM)


def permute_kernel(in_ref, out_ref):
    step = in_ref.shape[0]
    number = pl.program_id(0)
    first = pl.multiple_of(number * step, step)
    tail = PADDED - ROWS
    for y0 in range(2):

        @pl.when(lax.axis_index("y0") == y0)
        def _():
            for at in range(4):
                y = at % 2 * 2 + (at // 2 + y0) % 2
                parts = [in_ref[:, (z * 4 + y) * PIECE : (z * 4 + y + 1) * PIECE] for z in range(4)]
                out_ref[pl.ds(first, step), at * WIDE : (at + 1) * WIDE] = jnp.concatenate(parts, axis=1)

    @pl.when(number == PADDED // step - 1)
    def _():
        rows = lax.broadcasted_iota(jnp.int32, (32, 1), 0)
        kept = out_ref[PADDED - 32 : PADDED, :].astype(F32)
        out_ref[PADDED - 32 : PADDED, :] = jnp.where(rows < 32 - tail, kept, 0.0).astype(BF16)


def permute_embedding(embedding):
    step = 128
    return pl.pallas_call(
        permute_kernel,
        grid=(PADDED // step,),
        in_specs=[pl.BlockSpec((step, D), lambda i: (i, 0))],
        out_specs=WHOLE,
        out_shape=pltpu.VMEM((PADDED, D), BF16),
        compiler_params=BIG,
        cost_estimate=pl.CostEstimate(flops=0, bytes_accessed=4 * ROWS * D, transcendentals=0),
        name="permute_embedding",
    )(embedding)


def spread_kernel(residual_hbm, gain_hbm, out_ref, residual_ref, gain_ref, arrived):
    copies = [
        pltpu.make_async_copy(residual_hbm, residual_ref, arrived.at[0]),
        pltpu.make_async_copy(gain_hbm, gain_ref, arrived.at[1]),
    ]
    for copy in copies:
        copy.start()
    for copy in copies:
        copy.wait()
    values = residual_ref[...].astype(F32)
    gain = gain_ref[...].astype(F32).reshape(1, PIECE)
    corner = jnp.concatenate([values[8 * g : 8 * g + 8, 256:PIECE] for g in range(4)], axis=1)
    last = jnp.concatenate([gain[:, 256:PIECE], jnp.zeros((1, 96), F32)], axis=1)
    rows = [values[:, 0:128], values[:, 128:256], corner, gain[:, 0:128], gain[:, 128:256], last, jnp.zeros((5, 128), F32)]
    tiles = jnp.concatenate(rows, axis=0).astype(BF16)
    for place in range(8):
        out_ref[place] = tiles


def spread(residual, gain):
    return pl.pallas_call(
        spread_kernel,
        in_specs=[pl.BlockSpec(memory_space=pl.ANY)] * 2,
        out_specs=WHOLE,
        out_shape=pltpu.VMEM((8, 80, 128), BF16),
        scratch_shapes=[
            pltpu.VMEM((32, PIECE), BF16),
            pltpu.VMEM((PIECE,), BF16),
            pltpu.SemaphoreType.DMA((2,)),
        ],
        compiler_params=BIG,
        name="spread",
    )(far(residual), far(gain))


def pack_kernel(in_ref, out_ref):
    for zh in range(2):
        parts = []
        for zl in range(4):
            tiles = in_ref[zl * 2 + zh].astype(F32)
            corner = jnp.concatenate([tiles[64:72, 32 * g : 32 * g + 32] for g in range(4)], axis=0)
            parts += [tiles[0:32, :], tiles[32:64, :], corner]
        wide = jnp.concatenate(parts, axis=1)
        for k in range(TILES):
            tile = wide[:, k * 128 : (k + 1) * 128].astype(BF16)
            out_ref[k * BLOCK + zh * 32 : k * BLOCK + zh * 32 + 32, :] = tile
    parts = []
    for zl in range(4):
        tiles = in_ref[zl * 2].astype(F32)
        parts += [tiles[72:73, :], tiles[73:74, :], tiles[74:75, 0:32]]
    gains = jnp.concatenate(parts, axis=1)
    rows = [gains[:, k * 128 : (k + 1) * 128] for k in range(TILES)]
    tile = jnp.concatenate(rows + [jnp.zeros((16 - TILES, 128), F32)], axis=0).astype(BF16)
    out_ref[TILES * BLOCK : PACKED, :] = tile


def pack_tokens(gathered):
    return pl.pallas_call(
        pack_kernel,
        in_specs=[WHOLE],
        out_specs=WHOLE,
        out_shape=pltpu.VMEM((PACKED, 128), BF16),
        compiler_params=BIG,
        name="pack_tokens",
    )(near(gathered))


def absolute(relative):
    return (lax.axis_index("y1") + relative // 2) % 2 * 2 + (lax.axis_index("x1") + relative % 2) % 2


def order_kernel(*refs):
    in_refs, out_ref = refs[:4], refs[4]
    for relative, ref in enumerate(in_refs):
        out_ref[absolute(relative)] = ref[...]


def in_order(pieces):
    return pl.pallas_call(
        order_kernel,
        in_specs=[WHOLE] * 4,
        out_specs=WHOLE,
        out_shape=pltpu.VMEM((4, PACKED, 128), BF16),
        compiler_params=BIG,
        name="in_order",
    )(*(near(a) for a in pieces))


def logits_kernel(*refs):
    blocks, (embedding_ref, labels_ref, slot_ref, e_ref, stats_ref, scale_ref, normed) = refs[:4], refs[4:]
    gains = [
        [blocks[ry * 2][y1 * 2, TILES * BLOCK : PACKED, :].astype(F32) for y1 in range(2)] for ry in range(2)
    ]
    for x in range(4):
        tokens = slice(x * BLOCK, (x + 1) * BLOCK)

        def tile(ry, y1, k):
            return blocks[ry * 2 + x // 2][y1 * 2 + x % 2, k * BLOCK : (k + 1) * BLOCK, :].astype(F32)

        places = [(ry, y1, k) for ry in range(2) for y1 in range(2) for k in range(TILES)]
        squares = jnp.zeros((BLOCK, 128), F32)
        for place in places:
            v = tile(*place)
            squares += v * v
        scale = lax.rsqrt(jnp.sum(squares, axis=1, keepdims=True) / D + EPS)
        scale_ref[tokens, :] = jnp.broadcast_to(scale, (BLOCK, 128))
        for ry, y1, k in places:
            column = ry * HALF + y1 * WIDE + k * 128
            normed[tokens, column : column + 128] = (
                tile(ry, y1, k) * scale * gains[ry][y1][k : k + 1, :]
            ).astype(BF16)
    raw = lax.dot_general(
        embedding_ref[...], normed[...], (((1,), (1,)), ((), ())), preferred_element_type=F32
    )
    ratio = jnp.tanh(raw / CAP)
    row = lax.broadcasted_iota(jnp.int32, raw.shape, 0)
    inside = row < ROWS
    is_label = jnp.logical_and(inside, row + first_row() == labels_ref[...])
    exps = jnp.where(inside, jnp.exp(CAP * ratio), 0.0)
    others = jnp.where(is_label, 0.0, exps * (1.0 - ratio * ratio))
    stats_ref[0:1, :] = jnp.sum(exps, axis=0, keepdims=True)
    stats_ref[1:2, :] = jnp.sum(others * raw, axis=0, keepdims=True)
    stats_ref[2:3, :] = jnp.sum(jnp.where(is_label, raw, 0.0), axis=0, keepdims=True)
    stats_ref[3:8, :] = jnp.zeros((5, raw.shape[1]), F32)
    e_ref[0:256, :] = others.T.astype(BF16)
    e_ref[256:288, :] = slot_ref[...]


def logits_of(blocks, embedding, labels, slots):
    return pl.pallas_call(
        logits_kernel,
        in_specs=[WHOLE] * 7,
        out_specs=[WHOLE] * 3,
        out_shape=[
            pltpu.VMEM((288, PADDED), BF16),
            pltpu.VMEM((8, 256), F32),
            pltpu.VMEM((256, 128), F32),
        ],
        scratch_shapes=[pltpu.VMEM((256, D), BF16)],
        compiler_params=BIG,
        cost_estimate=pl.CostEstimate(flops=2 * 256 * PADDED * D, bytes_accessed=2 * PADDED * D, transcendentals=2 * 256 * PADDED),
        name="logits",
    )(*(near(a) for a in (*blocks, embedding, labels, slots)))


def three_pieces(value):
    high = value.astype(BF16).astype(F32)
    middle = (value - high).astype(BF16).astype(F32)
    low = (value - high - middle).astype(BF16).astype(F32)
    return [high, middle, low]


def stats_row(values):
    pieces = []
    for value in values:
        for piece in three_pieces(value):
            pieces += [piece, jnp.zeros((1, 128 - BLOCK), F32)]
    return jnp.concatenate(pieces, axis=1)


def read_stats(row):
    return [
        sum(row[:, (3 * i + j) * 128 : (3 * i + j) * 128 + BLOCK] for j in (2, 1, 0))
        for i in range(3)
    ]


def gradient_kernel(ry, e_ref, embedding_ref, stats_ref, out_ref):
    last = lax.broadcasted_iota(jnp.int32, (8, WIDE), 0) == 7
    rows = []
    for x in range(4):
        values = [stats_ref[i : i + 1, x * BLOCK : (x + 1) * BLOCK] for i in range(3)]
        rows.append(jnp.broadcast_to(stats_row(values), (8, WIDE)))
    for y1 in range(2):
        column = ry * HALF + y1 * WIDE
        term = jnp.dot(e_ref[...], embedding_ref[:, column : column + WIDE], preferred_element_type=F32)
        for x in range(4):
            at = (x // 2 * 2 + y1) * 2 + x % 2
            out_ref[at, 0:BLOCK, :] = term[x * BLOCK : (x + 1) * BLOCK, :].astype(BF16)
            extra = term[256 + 8 * x : 256 + 8 * x + 8, :]
            out_ref[at, BLOCK:ROOM, :] = jnp.where(last, rows[x], extra).astype(BF16)


def gradient_of(ry, e, embedding, stats):
    return pl.pallas_call(
        functools.partial(gradient_kernel, ry),
        in_specs=[WHOLE] * 3,
        out_specs=WHOLE,
        out_shape=pltpu.VMEM((8, ROOM, WIDE), BF16),
        compiler_params=BIG,
        cost_estimate=pl.CostEstimate(flops=288 * PADDED * D, bytes_accessed=PADDED * D, transcendentals=0),
        name="gradient",
    )(e, near(embedding), stats)


def product_kernel(ry, e_ref, embedding_ref, out_ref):
    out_ref[...] = jnp.dot(
        e_ref[...], embedding_ref[:, ry * HALF : (ry + 1) * HALF], preferred_element_type=F32
    )


def product_of(ry, e, embedding):
    return pl.pallas_call(
        functools.partial(product_kernel, ry),
        in_specs=[WHOLE] * 2,
        out_specs=WHOLE,
        out_shape=pltpu.VMEM((288, HALF), F32),
        compiler_params=BIG,
        cost_estimate=pl.CostEstimate(flops=288 * PADDED * D, bytes_accessed=PADDED * D, transcendentals=0),
        name="product",
    )(e, near(embedding))


def combine_kernel(term_ref, stats_ref, other_ref, *out_refs):
    last = lax.broadcasted_iota(jnp.int32, (8, WIDE), 0) == 7
    for x in range(4):
        values = [stats_ref[i : i + 1, x * BLOCK : (x + 1) * BLOCK] for i in range(3)]
        others = read_stats(other_ref[x // 2 * 4 + x % 2, BLOCK:ROOM, :].astype(F32)[7:8, :])
        row = jnp.broadcast_to(stats_row([a + b for a, b in zip(values, others)]), (8, WIDE))
        for y1 in range(2):
            at = (x // 2 * 2 + y1) * 2 + x % 2
            out_ref = out_refs[x // 2]
            columns = slice(y1 * WIDE, (y1 + 1) * WIDE)
            main = term_ref[x * BLOCK : (x + 1) * BLOCK, columns] + other_ref[at, 0:BLOCK, :].astype(F32)
            out_ref[y1 * 2 + x % 2, 0:BLOCK, :] = main.astype(BF16)
            extra = term_ref[256 + 8 * x : 256 + 8 * x + 8, columns] + other_ref[at, BLOCK:ROOM, :].astype(F32)
            out_ref[y1 * 2 + x % 2, BLOCK:ROOM, :] = jnp.where(last, row, extra).astype(BF16)


def combine(term, stats, other):
    return pl.pallas_call(
        combine_kernel,
        in_specs=[WHOLE] * 3,
        out_specs=[WHOLE] * 2,
        out_shape=[pltpu.VMEM((4, ROOM, WIDE), BF16)] * 2,
        compiler_params=BIG,
        name="combine",
    )(term, stats, near(other))


def class_kernel(*refs):
    in_refs, out_refs = refs[:4], refs[4:]
    last = lax.broadcasted_iota(jnp.int32, (8, WIDE), 0) == 7
    for relative, out_ref in enumerate(out_refs):
        block = absolute(relative)
        total = in_refs[0][block, 0:BLOCK, :].astype(F32)
        for ref in in_refs[1:]:
            total += ref[block, 0:BLOCK, :].astype(F32)
        out_ref[0:BLOCK, :] = total.astype(BF16)
        extras = [ref[block, BLOCK:ROOM, :].astype(F32) for ref in in_refs]
        row = sum(extra[7:8, :] for extra in extras)
        row = jnp.broadcast_to(stats_row(read_stats(row)), (8, WIDE))
        extras = [jnp.where(last, row if i == 0 else 0.0, extra) for i, extra in enumerate(extras)]
        out_ref[BLOCK : BLOCK + 32, :] = jnp.concatenate(extras, axis=0).astype(BF16)


def class_sum(blocks):
    return pl.pallas_call(
        class_kernel,
        in_specs=[WHOLE] * 4,
        out_specs=[WHOLE] * 4,
        out_shape=[pltpu.VMEM((BLOCK + 32, WIDE), BF16)] * 4,
        compiler_params=BIG,
        name="class_sum",
    )(*(near(a) for a in blocks))


def plane_kernel(*refs):
    in_refs, (place_ref, more_ref, out_ref) = refs[:4], refs[4:]
    total = in_refs[0][0:BLOCK, :].astype(F32)
    for ref in in_refs[1:]:
        total += ref[0:BLOCK, :].astype(F32)
    extras = [ref[BLOCK : BLOCK + 32, :].astype(F32) for ref in in_refs]
    stacked = jnp.concatenate(extras, axis=0).astype(BF16)
    label_rows = jnp.dot(place_ref[...], stacked, preferred_element_type=F32) + more_ref[...].astype(F32)
    row = sum(extra[7:8, :] for extra in extras)
    pieces = []
    for value in read_stats(row):
        pieces += three_pieces(value)
    sums = jnp.concatenate(pieces + [jnp.zeros((32 - 9, BLOCK), F32)], axis=0)
    for zl in range(4):
        for zh in range(2):
            main = total[zh * 32 : zh * 32 + 32, zl * PIECE : (zl + 1) * PIECE]
            rows = label_rows[zh * 32 : zh * 32 + 32, zl * PIECE : (zl + 1) * PIECE]
            out_ref[zl * 2 + zh] = jnp.concatenate([main, rows, sums], axis=1).astype(BF16)


def plane_sum(received, place, more):
    return pl.pallas_call(
        plane_kernel,
        in_specs=[WHOLE] * 6,
        out_specs=WHOLE,
        out_shape=pltpu.VMEM((8, 32, 640), BF16),
        compiler_params=BIG,
        name="plane_sum",
    )(*(near(a) for a in (*received, place, more)))


def final_kernel(in_ref, values_ref, gain_ref, weight_ref, scale_ref, loss_ref, grad_ref):
    zh, x1, x0, core = (lax.axis_index(name) for name in ("z_hi", "x1", "x0", "core"))
    total = in_ref[0].astype(F32)
    for source in range(1, 8):
        total += in_ref[source].astype(F32)
    sums = total[0:16, 2 * PIECE : 640]
    pick = lax.broadcasted_iota(jnp.int32, (32, BLOCK), 1) == zh * 32 + lax.broadcasted_iota(
        jnp.int32, (32, BLOCK), 0
    )

    def column(i):
        value = sum(sums[3 * i + j : 3 * i + j + 1, :] for j in (2, 1, 0))
        return jnp.sum(jnp.where(pick, jnp.broadcast_to(value, (32, BLOCK)), 0.0), axis=1, keepdims=True)

    sum_exp, inner_others, raw = column(0), column(1), column(2)
    own = (((zh * 2 + x1) * 2 + x0) * 2 + core) * 32 + lax.broadcasted_iota(jnp.int32, (32, 512), 0)
    own_weight = jnp.where(lax.broadcasted_iota(jnp.int32, (32, 512), 1) == own, weight_ref[...], 0.0)
    weight = jnp.sum(own_weight, axis=1, keepdims=True)
    scaling = scale_ref[pl.ds(pl.multiple_of(x1 * BLOCK + zh * 32, 32), 32), 0:1]
    ratio = jnp.tanh(raw / CAP)
    capped = CAP * ratio
    log_total = jnp.log(sum_exp)
    loss = log_total - capped
    coefficient = (jnp.exp(capped - log_total) - 1.0) * weight * (1.0 - ratio * ratio)
    coefficient = coefficient.astype(BF16).astype(F32)
    share = weight / sum_exp
    grad_normed = total[:, 0:PIECE] * share + total[:, PIECE : 2 * PIECE] * coefficient
    inner = (inner_others * share + coefficient * raw) / scaling
    upstream = grad_normed * gain_ref[...].astype(F32)
    values = values_ref[...].astype(F32)
    grad_ref[...] = scaling * upstream - values * (scaling * scaling * scaling * inner / D)
    eye = lax.broadcasted_iota(jnp.int32, (32, 32), 0) == lax.broadcasted_iota(jnp.int32, (32, 32), 1)
    loss_ref[...] = jnp.sum(jnp.where(eye, jnp.broadcast_to(loss, (32, 32)), 0.0), axis=0, keepdims=True)


def finish(received, values, gain, weight, scale):
    return pl.pallas_call(
        final_kernel,
        in_specs=[WHOLE] * 5,
        out_specs=[WHOLE] * 2,
        out_shape=[jax.ShapeDtypeStruct((1, 32), F32), jax.ShapeDtypeStruct((32, PIECE), F32)],
        compiler_params=BIG,
        name="finish",
    )(*(near(a) for a in (received, values, gain, weight, scale)))


def swap_cores(array):
    return lax.ppermute(array, "core", [(0, 1), (1, 0)])


def shifted(array, dx, dy):
    pairs = []
    for chip in range(128):
        line, y, zh, x = chip // 32, chip // 8 % 4, chip // 4 % 2, chip % 4
        pairs.append((chip, ((line * 4 + (y + dy) % 4) * 2 + zh) * 4 + (x + dx) % 4))
    return lax.ppermute(array, CHIPS, pairs)


def later_rows(labels, embedding, rounds):
    def one_round(carry):
        number, rows = carry
        _, tokens = lax.optimization_barrier((number, labels))
        zl, y1, y0, zh, x1, x0, core = (lax.axis_index(name) for name in (*CHIPS, "core"))
        token = jnp.arange(512, dtype=jnp.int32)
        group = (token // 32) % 2 * 4 + (token // 64) % 2 * 2 + (token // 128) % 2
        owner = tokens // (2 * ROWS)
        key = owner * 8 + group
        same = jnp.logical_and(key[:, None] == key[None, :], token[None, :] < token[:, None])
        rank = jnp.sum(same.astype(jnp.int32), axis=1)
        turn, slot = rank // SLOTS, rank % SLOTS
        taken = jnp.where(jnp.logical_and(owner == this_chip(), turn == number), group * 8 + slot, -1)
        match = taken[None, :] == jnp.arange(64, dtype=jnp.int32)[:, None]
        held = jnp.sum(jnp.where(match, (tokens - first_row())[None, :] + 1, 0), axis=1) - 1
        chosen = (held[:, None] == jnp.arange(ROWS, dtype=jnp.int32)[None, :]).astype(BF16)
        found = jnp.dot(chosen, embedding, preferred_element_type=F32).astype(BF16)
        found = found.reshape(2, 2, 2, 8, 4, 4, PIECE).transpose(0, 5, 2, 1, 3, 4, 6).reshape(2, 16, 8, WIDE)
        ours = lax.dynamic_index_in_dim(found, core, 0, keepdims=False)
        theirs = lax.dynamic_index_in_dim(found, 1 - core, 0, keepdims=False)
        ours = ours + swap_cores(theirs)
        ours = lax.all_to_all(ours, ("y1", "y0", "x1", "x0"), 0, 0, tiled=True).reshape(128, WIDE)
        local = jnp.arange(BLOCK, dtype=jnp.int32)
        own = (((local // 32 * 2 + x1) * 2 + x0) * 2 + core) * 32 + local % 32
        place = jnp.arange(16, dtype=jnp.int32)
        chips = ((zl * 4 + place // 4) * 2 + zh) * 4 + place % 4
        hit = jnp.logical_and(owner[own][:, None] == chips[None, :], (turn[own] == number)[:, None])
        at = slot[own][:, None] == jnp.arange(8, dtype=jnp.int32)[None, :]
        put = jnp.logical_and(hit[:, :, None], at[:, None, :]).astype(BF16).reshape(BLOCK, 128)
        return number + 1, rows + jnp.dot(put, ours, preferred_element_type=F32).astype(BF16)

    start = (jnp.int32(1), jnp.zeros((BLOCK, WIDE), BF16))
    return lax.while_loop(lambda carry: carry[0] < rounds, one_round, start)[1]


def on_device(residual, final_gain, embedding, labels, token_weight):
    gain = final_gain.reshape(1, PIECE)
    gathered = lax.all_to_all(spread(residual, final_gain), ("z_lo", "z_hi"), 0, 0, tiled=True)
    *early, rounds = label_places(labels.reshape(1, 512))
    early.append(later_rows(labels, embedding, rounds[0, 0]))
    piece, embedding, early = lax.optimization_barrier((pack_tokens(gathered), embedding, early))
    own_labels, own_slots, other_labels, other_slots, place, more = early

    packed = in_order([piece] + [shifted(piece, 2 * dx, 2 * dy) for dy, dx in PLACES[1:]])
    table = permute_embedding(embedding)
    blocks = [packed] + [shifted(packed, *SHIFTS[parity]) for parity in PLACES[1:]]
    blocks[1:], table = lax.optimization_barrier((blocks[1:], table))
    other_blocks = [swap_cores(block) for block in blocks]

    e, stats, scale = logits_of(blocks, table, own_labels, own_slots)
    other_blocks, e = lax.optimization_barrier((other_blocks, e))
    e_other, stats_other, _ = logits_of(other_blocks, table, other_labels, other_slots)
    far_part, e_other = lax.optimization_barrier((gradient_of(1, e_other, table, stats_other), e_other))
    near_part, e = lax.optimization_barrier((gradient_of(0, e_other, table, stats_other), e))
    far_blocks = combine(product_of(1, e, table), stats, swap_cores(far_part))
    far_blocks, e = lax.optimization_barrier((far_blocks, e))
    near_blocks = combine(product_of(0, e, table), stats, swap_cores(near_part))
    parts = [*near_blocks, *far_blocks]
    sums = class_sum([parts[0]] + [shifted(part, *SHIFTS[parity]) for part, parity in zip(parts[1:], PLACES[1:])])
    plane = [sums[0]] + [shifted(block, 2 * dx, 2 * dy) for block, (dy, dx) in zip(sums[1:], PLACES[1:])]
    column = lax.all_to_all(plane_sum(plane, place, more), ("z_lo", "z_hi"), 0, 0, tiled=True)

    loss, grad = finish(column, residual, gain, token_weight.reshape(1, 512), scale)
    return (loss.reshape(32), grad)


def solution(mesh):
    fine = Mesh(mesh.devices.reshape(4, 2, 2, 2, 2, 2, 2), (*CHIPS, "core"))
    section, fsdp = ("z_lo", "y1", "y0"), ("z_hi", "x1", "x0", "core")
    in_specs = (P(fsdp, section), P(section), P(section + fsdp, None), P(), P())
    out_specs = (P(fsdp), P(fsdp, section))
    return jax.shard_map(on_device, mesh=fine, in_specs=in_specs, out_specs=out_specs, check_vma=False)
```

```python
import functools

import jax
import jax.numpy as jnp
from jax import lax
from jax.experimental import pallas as pl
from jax.experimental.pallas import tpu as pltpu
from jax.sharding import Mesh, PartitionSpec as P

D = 4608
EPS = 1e-06
CAP = 30.0
ROWS = 1000
PADDED = 1024
PIECE = 288
WIDE = 1152
HALF = 2 * WIDE
BLOCK = 64
ROOM = BLOCK + 8
TILES = WIDE // 128
SLOTS = 7
PACKED = TILES * BLOCK + 16
F32 = jnp.float32
BF16 = jnp.bfloat16
VMEM = pltpu.MemorySpace.VMEM
WHOLE = pl.BlockSpec(memory_space=VMEM)
SCALARS = pl.BlockSpec(memory_space=pltpu.MemorySpace.SMEM)
BIG = pltpu.CompilerParams(vmem_limit_bytes=20 * 1024 * 1024)


def near(array):
    return pltpu.with_memory_space_constraint(array, VMEM)


CHIPS = ("z_lo", "y1", "y0", "z_hi", "x1", "x0")
SHIFTS = {(0, 1): (1, 0), (1, 0): (0, 1), (1, 1): (-1, -1)}
PLACES = ((0, 0), *SHIFTS)


def this_chip():
    number = 0
    for name in CHIPS:
        number = number * lax.axis_size(name) + lax.axis_index(name)
    return number


def first_row():
    return (this_chip() * 2 + lax.axis_index("core")) * ROWS


def label_kernel(labels_ref, own_labels, own_slots, other_labels, other_slots, place_ref, rounds_ref):
    zl, y1, y0, zh, x1, x0, core = (lax.axis_index(name) for name in (*CHIPS, "core"))
    labels = labels_ref[...]
    token = lax.broadcasted_iota(jnp.int32, (1, 512), 1)
    group = (token >> 5 & 1) * 4 + (token >> 6 & 1) * 2 + (token >> 7 & 1)
    owner = ((labels.astype(F32) + 0.5) * (1.0 / (2 * ROWS))).astype(jnp.int32)
    key = owner * 8 + group
    square = (512, 512)
    down = lax.broadcasted_iota(jnp.int32, square, 0)
    across = lax.broadcasted_iota(jnp.int32, square, 1)
    keys = jnp.broadcast_to(key, square)
    key_down = jnp.sum(jnp.where(down == across, keys, 0), axis=1, keepdims=True)
    earlier = jnp.logical_and(jnp.broadcast_to(key_down, square) == keys, down < across)
    rank = jnp.sum(earlier.astype(jnp.int32), axis=0, keepdims=True)
    turn = ((rank.astype(F32) + 0.5) * (1.0 / SLOTS)).astype(jnp.int32)
    slot = rank - turn * SLOTS
    rounds_ref[...] = jnp.broadcast_to(jnp.max(turn, axis=1, keepdims=True) + 1, (1, 128))

    taken = jnp.where(jnp.logical_and(owner == this_chip(), turn == 0), group * 8 + slot, -1)
    shifted_labels = labels - first_row() + 1
    for half, label_ref, slot_ref in ((core, own_labels, own_slots), (1 - core, other_labels, other_slots)):
        at = lax.broadcasted_iota(jnp.int32, (32, 512), 0)
        wanted = half * 32 + (at + 16 * x0 & 31)
        match = jnp.broadcast_to(taken, (32, 512)) == wanted
        held = jnp.sum(jnp.where(match, jnp.broadcast_to(shifted_labels, (32, 512)), 0), axis=1, keepdims=True) - 1
        vocab = lax.broadcasted_iota(jnp.int32, (32, PADDED), 1)
        slot_ref[...] = jnp.where(vocab == held, 1.0, 0.0).astype(BF16)
        chunks = []
        for chunk in range(8):
            rx, from_x1, from_zh = chunk // 4, chunk // 2 % 2, chunk % 2
            picked = jnp.zeros((1, 32), jnp.int32)
            for from_x0 in range(2):
                for from_core in range(2):
                    source = ((from_zh * 2 + from_x1) * 2 + from_x0) * 2 + from_core
                    use = jnp.logical_and(half == from_core, (x0 + rx) % 2 == from_x0)
                    picked = jnp.where(use, labels[:, source * 32 : source * 32 + 32], picked)
            chunks.append(picked)
        label_ref[...] = jnp.concatenate(chunks, axis=1)

    code = jnp.broadcast_to(jnp.where(turn == 0, owner * 8 + slot, -1), (BLOCK, 512))
    at = lax.broadcasted_iota(jnp.int32, (BLOCK, 512), 0)
    own = (at >> 5) * 256 + x1 * 128 + x0 * 64 + core * 32 + (at & 31)
    pick = lax.broadcasted_iota(jnp.int32, (BLOCK, 512), 1) == own
    own_code = jnp.sum(jnp.where(pick, code, 0), axis=1, keepdims=True)
    column = lax.broadcasted_iota(jnp.int32, (BLOCK, 128), 1)
    parity = column >> 3 & 3
    from_y = (column >> 6 ^ y1) * 2 + y0 + 4
    from_x = (column >> 5 & 1 ^ x1) * 2 + x0 + 4
    for index, (dx, dy) in enumerate(SHIFTS.values()):
        from_y = from_y - jnp.where(parity == index + 1, dy, 0)
        from_x = from_x - jnp.where(parity == index + 1, dx, 0)
    chip = ((zl * 4 + (from_y & 3)) * 2 + zh) * 4 + (from_x & 3)
    place_ref[...] = jnp.where(own_code == chip * 8 + (column & 7), 1.0, 0.0).astype(BF16)


def label_places(labels):
    return pl.pallas_call(
        label_kernel,
        in_specs=[WHOLE],
        out_specs=[WHOLE] * 6,
        out_shape=[
            pltpu.VMEM((1, 256), jnp.int32),
            pltpu.VMEM((32, PADDED), BF16),
            pltpu.VMEM((1, 256), jnp.int32),
            pltpu.VMEM((32, PADDED), BF16),
            pltpu.VMEM((BLOCK, 128), BF16),
            jax.ShapeDtypeStruct((1, 128), jnp.int32),
        ],
        compiler_params=BIG,
        cost_estimate=pl.CostEstimate(flops=10 * 512 * 512, bytes_accessed=1 << 20, transcendentals=0),
        name="label_places",
    )(labels)


def far(array):
    return pltpu.with_memory_space_constraint(array, pltpu.MemorySpace.HBM)


def permute_kernel(in_ref, out_ref):
    step = in_ref.shape[0]
    number = pl.program_id(0)
    first = pl.multiple_of(number * step, step)
    tail = PADDED - ROWS
    for y0 in range(2):

        @pl.when(lax.axis_index("y0") == y0)
        def _():
            for at in range(4):
                y = at % 2 * 2 + (at // 2 + y0) % 2
                parts = [in_ref[:, (z * 4 + y) * PIECE : (z * 4 + y + 1) * PIECE] for z in range(4)]
                out_ref[pl.ds(first, step), at * WIDE : (at + 1) * WIDE] = jnp.concatenate(parts, axis=1)

    @pl.when(number == PADDED // step - 1)
    def _():
        rows = lax.broadcasted_iota(jnp.int32, (32, 1), 0)
        kept = out_ref[PADDED - 32 : PADDED, :].astype(F32)
        out_ref[PADDED - 32 : PADDED, :] = jnp.where(rows < 32 - tail, kept, 0.0).astype(BF16)


def permute_embedding(embedding):
    step = 128
    return pl.pallas_call(
        permute_kernel,
        grid=(PADDED // step,),
        in_specs=[pl.BlockSpec((step, D), lambda i: (i, 0))],
        out_specs=WHOLE,
        out_shape=pltpu.VMEM((PADDED, D), BF16),
        compiler_params=BIG,
        cost_estimate=pl.CostEstimate(flops=0, bytes_accessed=4 * ROWS * D, transcendentals=0),
        name="permute_embedding",
    )(embedding)


def spread_kernel(residual_hbm, gain_hbm, out_ref, residual_ref, gain_ref, arrived):
    copies = [
        pltpu.make_async_copy(residual_hbm, residual_ref, arrived.at[0]),
        pltpu.make_async_copy(gain_hbm, gain_ref, arrived.at[1]),
    ]
    for copy in copies:
        copy.start()
    for copy in copies:
        copy.wait()
    values = residual_ref[...].astype(F32)
    gain = gain_ref[...].astype(F32).reshape(1, PIECE)
    corner = jnp.concatenate([values[8 * g : 8 * g + 8, 256:PIECE] for g in range(4)], axis=1)
    last = jnp.concatenate([gain[:, 256:PIECE], jnp.zeros((1, 96), F32)], axis=1)
    rows = [values[:, 0:128], values[:, 128:256], corner, gain[:, 0:128], gain[:, 128:256], last, jnp.zeros((5, 128), F32)]
    tiles = jnp.concatenate(rows, axis=0).astype(BF16)
    for place in range(8):
        out_ref[place] = tiles


def spread(residual, gain):
    return pl.pallas_call(
        spread_kernel,
        in_specs=[pl.BlockSpec(memory_space=pl.ANY)] * 2,
        out_specs=WHOLE,
        out_shape=pltpu.VMEM((8, 80, 128), BF16),
        scratch_shapes=[
            pltpu.VMEM((32, PIECE), BF16),
            pltpu.VMEM((PIECE,), BF16),
            pltpu.SemaphoreType.DMA((2,)),
        ],
        compiler_params=BIG,
        name="spread",
    )(far(residual), far(gain))


def pack_kernel(in_ref, out_ref):
    for zh in range(2):
        parts = []
        for zl in range(4):
            tiles = in_ref[zl * 2 + zh].astype(F32)
            corner = jnp.concatenate([tiles[64:72, 32 * g : 32 * g + 32] for g in range(4)], axis=0)
            parts += [tiles[0:32, :], tiles[32:64, :], corner]
        wide = jnp.concatenate(parts, axis=1)
        for k in range(TILES):
            tile = wide[:, k * 128 : (k + 1) * 128].astype(BF16)
            out_ref[k * BLOCK + zh * 32 : k * BLOCK + zh * 32 + 32, :] = tile
    parts = []
    for zl in range(4):
        tiles = in_ref[zl * 2].astype(F32)
        parts += [tiles[72:73, :], tiles[73:74, :], tiles[74:75, 0:32]]
    gains = jnp.concatenate(parts, axis=1)
    rows = [gains[:, k * 128 : (k + 1) * 128] for k in range(TILES)]
    tile = jnp.concatenate(rows + [jnp.zeros((16 - TILES, 128), F32)], axis=0).astype(BF16)
    out_ref[TILES * BLOCK : PACKED, :] = tile


def pack_tokens(gathered):
    return pl.pallas_call(
        pack_kernel,
        in_specs=[WHOLE],
        out_specs=WHOLE,
        out_shape=pltpu.VMEM((PACKED, 128), BF16),
        compiler_params=BIG,
        name="pack_tokens",
    )(near(gathered))


def absolute(relative):
    return (lax.axis_index("y1") + relative // 2) % 2 * 2 + (lax.axis_index("x1") + relative % 2) % 2


def order_kernel(*refs):
    in_refs, out_ref = refs[:4], refs[4]
    for relative, ref in enumerate(in_refs):
        out_ref[absolute(relative)] = ref[...]


def in_order(pieces):
    return pl.pallas_call(
        order_kernel,
        in_specs=[WHOLE] * 4,
        out_specs=WHOLE,
        out_shape=pltpu.VMEM((4, PACKED, 128), BF16),
        compiler_params=BIG,
        name="in_order",
    )(*(near(a) for a in pieces))


def logits_kernel(*refs):
    blocks, (embedding_ref, labels_ref, slot_ref, e_near, e_far, stats_ref, scale_ref, normed) = refs[:4], refs[4:]
    gains = [
        [blocks[ry * 2][y1 * 2, TILES * BLOCK : PACKED, :].astype(F32) for y1 in range(2)] for ry in range(2)
    ]
    for x in range(4):
        tokens = slice(x * BLOCK, (x + 1) * BLOCK)

        def tile(ry, y1, k):
            return blocks[ry * 2 + x // 2][y1 * 2 + x % 2, k * BLOCK : (k + 1) * BLOCK, :].astype(F32)

        places = [(ry, y1, k) for ry in range(2) for y1 in range(2) for k in range(TILES)]
        squares = jnp.zeros((BLOCK, 128), F32)
        for place in places:
            v = tile(*place)
            squares += v * v
        scale = lax.rsqrt(jnp.sum(squares, axis=1, keepdims=True) / D + EPS)
        scale_ref[tokens, :] = jnp.broadcast_to(scale, (BLOCK, 128))
        for ry, y1, k in places:
            column = ry * HALF + y1 * WIDE + k * 128
            normed[tokens, column : column + 128] = (
                tile(ry, y1, k) * scale * gains[ry][y1][k : k + 1, :]
            ).astype(BF16)
    raw = lax.dot_general(
        embedding_ref[...], normed[...], (((1,), (1,)), ((), ())), preferred_element_type=F32
    )
    ratio = jnp.tanh(raw / CAP)
    row = lax.broadcasted_iota(jnp.int32, raw.shape, 0)
    inside = row < ROWS
    is_label = jnp.logical_and(inside, row + first_row() == labels_ref[...])
    exps = jnp.where(inside, jnp.exp(CAP * ratio), 0.0)
    others = jnp.where(is_label, 0.0, exps * (1.0 - ratio * ratio))
    stats_ref[0:1, :] = jnp.sum(exps, axis=0, keepdims=True)
    stats_ref[1:2, :] = jnp.sum(others * raw, axis=0, keepdims=True)
    stats_ref[2:3, :] = jnp.sum(jnp.where(is_label, raw, 0.0), axis=0, keepdims=True)
    stats_ref[3:8, :] = jnp.zeros((5, raw.shape[1]), F32)
    for rx, e_ref in enumerate((e_near, e_far)):
        e_ref[0:128, :] = others[:, rx * 128 : (rx + 1) * 128].T.astype(BF16)
        e_ref[128:144, :] = slot_ref[rx * 16 : (rx + 1) * 16, :]


def logits_of(blocks, embedding, labels, slots):
    return pl.pallas_call(
        logits_kernel,
        in_specs=[WHOLE] * 7,
        out_specs=[WHOLE] * 4,
        out_shape=[
            pltpu.VMEM((144, PADDED), BF16),
            pltpu.VMEM((144, PADDED), BF16),
            pltpu.VMEM((8, 256), F32),
            pltpu.VMEM((256, 128), F32),
        ],
        scratch_shapes=[pltpu.VMEM((256, D), BF16)],
        compiler_params=BIG,
        cost_estimate=pl.CostEstimate(flops=2 * 256 * PADDED * D, bytes_accessed=2 * PADDED * D, transcendentals=2 * 256 * PADDED),
        name="logits",
    )(*(near(a) for a in (*blocks, embedding, labels, slots)))


def three_pieces(value):
    high = value.astype(BF16).astype(F32)
    middle = (value - high).astype(BF16).astype(F32)
    low = (value - high - middle).astype(BF16).astype(F32)
    return [high, middle, low]


def stats_row(values):
    pieces = []
    for value in values:
        for piece in three_pieces(value):
            pieces += [piece, jnp.zeros((1, 128 - BLOCK), F32)]
    return jnp.concatenate(pieces, axis=1)


def read_stats(row):
    return [
        sum(row[:, (3 * i + j) * 128 : (3 * i + j) * 128 + BLOCK] for j in (2, 1, 0))
        for i in range(3)
    ]


def rows_of(term, parity, x1):
    at = parity * 144
    return term[at + x1 * BLOCK : at + (x1 + 1) * BLOCK, :], term[at + 128 + 8 * x1 : at + 128 + 8 * x1 + 8, :]


def gradient_kernel(ry, parities, *refs):
    e_refs, (embedding_ref, stats_ref, *out_refs) = refs[: len(parities)], refs[len(parities) :]
    last = lax.broadcasted_iota(jnp.int32, (8, WIDE), 0) == 7
    left = jnp.concatenate([ref[...] for ref in e_refs], axis=0)
    rows = {}
    for rx in parities:
        for x1 in range(2):
            at = (rx * 2 + x1) * BLOCK
            values = [stats_ref[i : i + 1, at : at + BLOCK] for i in range(3)]
            rows[rx, x1] = jnp.broadcast_to(stats_row(values), (8, WIDE))
    for y1 in range(2):
        column = ry * HALF + y1 * WIDE
        term = jnp.dot(left, embedding_ref[:, column : column + WIDE], preferred_element_type=F32)
        for place, rx in enumerate(parities):
            for x1 in range(2):
                out_ref, at = out_refs[y1 * len(out_refs) // 2], place * 4 // len(out_refs) + x1
                at += y1 * 2 if len(out_refs) == 1 else 0
                main, extra = rows_of(term, place, x1)
                out_ref[at, 0:BLOCK, :] = main.astype(BF16)
                out_ref[at, BLOCK:ROOM, :] = jnp.where(last, rows[rx, x1], extra).astype(BF16)


def gradient_of(ry, parities, e, embedding, stats, pieces=1):
    count = len(parities)
    return pl.pallas_call(
        functools.partial(gradient_kernel, ry, parities),
        in_specs=[WHOLE] * (2 + count),
        out_specs=[WHOLE] * pieces,
        out_shape=[pltpu.VMEM((4 * count // pieces, ROOM, WIDE), BF16)] * pieces,
        compiler_params=BIG,
        cost_estimate=pl.CostEstimate(flops=144 * count * PADDED * D, bytes_accessed=PADDED * D, transcendentals=0),
        name="gradient",
    )(*(near(e[rx]) for rx in parities), near(embedding), near(stats))


def product_kernel(ry, *refs):
    e_refs, (embedding_ref, out_ref) = refs[:-2], refs[-2:]
    left = jnp.concatenate([ref[...] for ref in e_refs], axis=0)
    out_ref[...] = jnp.dot(left, embedding_ref[:, ry * HALF : (ry + 1) * HALF], preferred_element_type=F32)


def product_of(ry, parities, e, embedding):
    count = len(parities)
    return pl.pallas_call(
        functools.partial(product_kernel, ry),
        in_specs=[WHOLE] * (1 + count),
        out_specs=WHOLE,
        out_shape=pltpu.VMEM((144 * count, HALF), F32),
        compiler_params=BIG,
        cost_estimate=pl.CostEstimate(flops=144 * count * PADDED * D, bytes_accessed=PADDED * D, transcendentals=0),
        name="product",
    )(*(near(e[rx]) for rx in parities), near(embedding))


def combine_kernel(parities, term_ref, stats_ref, *refs):
    other_refs, out_refs = refs[: -len(parities)], refs[-len(parities) :]
    last = lax.broadcasted_iota(jnp.int32, (8, WIDE), 0) == 7
    for place, rx in enumerate(parities):
        for x1 in range(2):
            at = (rx * 2 + x1) * BLOCK
            values = [stats_ref[i : i + 1, at : at + BLOCK] for i in range(3)]
            others = other_refs[0][place * 4 // len(other_refs) + x1, BLOCK:ROOM, :].astype(F32)
            others = read_stats(others[7:8, :])
            row = jnp.broadcast_to(stats_row([a + b for a, b in zip(values, others)]), (8, WIDE))
            for y1 in range(2):
                other_ref, at = other_refs[y1 * len(other_refs) // 2], place * 4 // len(other_refs) + x1
                at += y1 * 2 if len(other_refs) == 1 else 0
                main, extra = rows_of(term_ref[:, y1 * WIDE : (y1 + 1) * WIDE], place, x1)
                main = main + other_ref[at, 0:BLOCK, :].astype(F32)
                extra = extra + other_ref[at, BLOCK:ROOM, :].astype(F32)
                out_refs[place][y1 * 2 + x1, 0:BLOCK, :] = main.astype(BF16)
                out_refs[place][y1 * 2 + x1, BLOCK:ROOM, :] = jnp.where(last, row, extra).astype(BF16)


def combine(parities, term, stats, other):
    count = len(parities)
    return pl.pallas_call(
        functools.partial(combine_kernel, parities),
        in_specs=[WHOLE] * (2 + len(other)),
        out_specs=[WHOLE] * count,
        out_shape=[pltpu.VMEM((4, ROOM, WIDE), BF16)] * count,
        compiler_params=BIG,
        name="combine",
    )(near(term), near(stats), *(near(a) for a in other))


def class_kernel(*refs):
    in_refs, out_refs = refs[:4], refs[4:]
    last = lax.broadcasted_iota(jnp.int32, (8, WIDE), 0) == 7
    for relative, out_ref in enumerate(out_refs):
        block = absolute(relative)
        total = in_refs[0][block, 0:BLOCK, :].astype(F32)
        for ref in in_refs[1:]:
            total += ref[block, 0:BLOCK, :].astype(F32)
        out_ref[0:BLOCK, :] = total.astype(BF16)
        extras = [ref[block, BLOCK:ROOM, :].astype(F32) for ref in in_refs]
        row = sum(extra[7:8, :] for extra in extras)
        row = jnp.broadcast_to(stats_row(read_stats(row)), (8, WIDE))
        extras = [jnp.where(last, row if i == 0 else 0.0, extra) for i, extra in enumerate(extras)]
        out_ref[BLOCK : BLOCK + 32, :] = jnp.concatenate(extras, axis=0).astype(BF16)


def class_sum(blocks):
    return pl.pallas_call(
        class_kernel,
        in_specs=[WHOLE] * 4,
        out_specs=[WHOLE] * 4,
        out_shape=[pltpu.VMEM((BLOCK + 32, WIDE), BF16)] * 4,
        compiler_params=BIG,
        name="class_sum",
    )(*(near(a) for a in blocks))


def plane_kernel(*refs):
    in_refs, (place_ref, more_ref, out_ref) = refs[:4], refs[4:]
    total = in_refs[0][0:BLOCK, :].astype(F32)
    for ref in in_refs[1:]:
        total += ref[0:BLOCK, :].astype(F32)
    extras = [ref[BLOCK : BLOCK + 32, :].astype(F32) for ref in in_refs]
    stacked = jnp.concatenate(extras, axis=0).astype(BF16)
    label_rows = jnp.dot(place_ref[...], stacked, preferred_element_type=F32) + more_ref[...].astype(F32)
    row = sum(extra[7:8, :] for extra in extras)
    pieces = []
    for value in read_stats(row):
        pieces += three_pieces(value)
    sums = jnp.concatenate(pieces + [jnp.zeros((32 - 9, BLOCK), F32)], axis=0)
    for zl in range(4):
        for zh in range(2):
            main = total[zh * 32 : zh * 32 + 32, zl * PIECE : (zl + 1) * PIECE]
            rows = label_rows[zh * 32 : zh * 32 + 32, zl * PIECE : (zl + 1) * PIECE]
            out_ref[zl * 2 + zh] = jnp.concatenate([main, rows, sums], axis=1).astype(BF16)


def plane_sum(received, place, more):
    return pl.pallas_call(
        plane_kernel,
        in_specs=[WHOLE] * 6,
        out_specs=WHOLE,
        out_shape=pltpu.VMEM((8, 32, 640), BF16),
        compiler_params=BIG,
        name="plane_sum",
    )(*(near(a) for a in (*received, place, more)))


def final_kernel(in_ref, values_ref, gain_ref, weight_ref, scale_ref, loss_ref, grad_ref):
    zh, x1, x0, core = (lax.axis_index(name) for name in ("z_hi", "x1", "x0", "core"))
    total = in_ref[0].astype(F32)
    for source in range(1, 8):
        total += in_ref[source].astype(F32)
    sums = total[0:16, 2 * PIECE : 640]
    pick = lax.broadcasted_iota(jnp.int32, (32, BLOCK), 1) == zh * 32 + lax.broadcasted_iota(
        jnp.int32, (32, BLOCK), 0
    )

    def column(i):
        value = sum(sums[3 * i + j : 3 * i + j + 1, :] for j in (2, 1, 0))
        return jnp.sum(jnp.where(pick, jnp.broadcast_to(value, (32, BLOCK)), 0.0), axis=1, keepdims=True)

    sum_exp, inner_others, raw = column(0), column(1), column(2)
    own = (((zh * 2 + x1) * 2 + x0) * 2 + core) * 32 + lax.broadcasted_iota(jnp.int32, (32, 512), 0)
    own_weight = jnp.where(lax.broadcasted_iota(jnp.int32, (32, 512), 1) == own, weight_ref[...], 0.0)
    weight = jnp.sum(own_weight, axis=1, keepdims=True)
    scaling = scale_ref[pl.ds(pl.multiple_of(x1 * BLOCK + zh * 32, 32), 32), 0:1]
    ratio = jnp.tanh(raw / CAP)
    capped = CAP * ratio
    log_total = jnp.log(sum_exp)
    loss = log_total - capped
    coefficient = (jnp.exp(capped - log_total) - 1.0) * weight * (1.0 - ratio * ratio)
    coefficient = coefficient.astype(BF16).astype(F32)
    share = weight / sum_exp
    grad_normed = total[:, 0:PIECE] * share + total[:, PIECE : 2 * PIECE] * coefficient
    inner = (inner_others * share + coefficient * raw) / scaling
    upstream = grad_normed * gain_ref[...].astype(F32)
    values = values_ref[...].astype(F32)
    grad_ref[...] = scaling * upstream - values * (scaling * scaling * scaling * inner / D)
    eye = lax.broadcasted_iota(jnp.int32, (32, 32), 0) == lax.broadcasted_iota(jnp.int32, (32, 32), 1)
    loss_ref[...] = jnp.sum(jnp.where(eye, jnp.broadcast_to(loss, (32, 32)), 0.0), axis=0, keepdims=True)


def finish(received, values, gain, weight, scale):
    return pl.pallas_call(
        final_kernel,
        in_specs=[WHOLE] * 5,
        out_specs=[WHOLE] * 2,
        out_shape=[jax.ShapeDtypeStruct((1, 32), F32), jax.ShapeDtypeStruct((32, PIECE), F32)],
        compiler_params=BIG,
        name="finish",
    )(*(near(a) for a in (received, values, gain, weight, scale)))


def swap_cores(array):
    return lax.ppermute(array, "core", [(0, 1), (1, 0)])


def shifted(array, dx, dy):
    pairs = []
    for chip in range(128):
        line, y, zh, x = chip // 32, chip // 8 % 4, chip // 4 % 2, chip % 4
        pairs.append((chip, ((line * 4 + (y + dy) % 4) * 2 + zh) * 4 + (x + dx) % 4))
    return lax.ppermute(array, CHIPS, pairs)


def later_rows(labels, embedding, rounds):
    def one_round(carry):
        number, rows = carry
        _, tokens = lax.optimization_barrier((number, labels))
        zl, y1, y0, zh, x1, x0, core = (lax.axis_index(name) for name in (*CHIPS, "core"))
        token = jnp.arange(512, dtype=jnp.int32)
        group = (token // 32) % 2 * 4 + (token // 64) % 2 * 2 + (token // 128) % 2
        owner = tokens // (2 * ROWS)
        key = owner * 8 + group
        same = jnp.logical_and(key[:, None] == key[None, :], token[None, :] < token[:, None])
        rank = jnp.sum(same.astype(jnp.int32), axis=1)
        turn, slot = rank // SLOTS, rank % SLOTS
        taken = jnp.where(jnp.logical_and(owner == this_chip(), turn == number), group * 8 + slot, -1)
        match = taken[None, :] == jnp.arange(64, dtype=jnp.int32)[:, None]
        held = jnp.sum(jnp.where(match, (tokens - first_row())[None, :] + 1, 0), axis=1) - 1
        chosen = (held[:, None] == jnp.arange(ROWS, dtype=jnp.int32)[None, :]).astype(BF16)
        found = jnp.dot(chosen, embedding, preferred_element_type=F32).astype(BF16)
        found = found.reshape(2, 2, 2, 8, 4, 4, PIECE).transpose(0, 5, 2, 1, 3, 4, 6).reshape(2, 16, 8, WIDE)
        ours = lax.dynamic_index_in_dim(found, core, 0, keepdims=False)
        theirs = lax.dynamic_index_in_dim(found, 1 - core, 0, keepdims=False)
        ours = ours + swap_cores(theirs)
        ours = lax.all_to_all(ours, ("y1", "y0", "x1", "x0"), 0, 0, tiled=True).reshape(128, WIDE)
        local = jnp.arange(BLOCK, dtype=jnp.int32)
        own = (((local // 32 * 2 + x1) * 2 + x0) * 2 + core) * 32 + local % 32
        place = jnp.arange(16, dtype=jnp.int32)
        chips = ((zl * 4 + place // 4) * 2 + zh) * 4 + place % 4
        hit = jnp.logical_and(owner[own][:, None] == chips[None, :], (turn[own] == number)[:, None])
        at = slot[own][:, None] == jnp.arange(8, dtype=jnp.int32)[None, :]
        put = jnp.logical_and(hit[:, :, None], at[:, None, :]).astype(BF16).reshape(BLOCK, 128)
        return number + 1, rows + jnp.dot(put, ours, preferred_element_type=F32).astype(BF16)

    start = (jnp.int32(1), jnp.zeros((BLOCK, WIDE), BF16))
    return lax.while_loop(lambda carry: carry[0] < rounds, one_round, start)[1]


def on_device(residual, final_gain, embedding, labels, token_weight):
    gain = final_gain.reshape(1, PIECE)
    gathered = lax.all_to_all(spread(residual, final_gain), ("z_lo", "z_hi"), 0, 0, tiled=True)
    *early, rounds = label_places(labels.reshape(1, 512))
    piece, embedding, rounds, early = lax.optimization_barrier((pack_tokens(gathered), embedding, rounds, early))
    own_labels, own_slots, other_labels, other_slots, place = early
    more = later_rows(labels, embedding, rounds[0, 0])

    moved = [shifted(piece, 2 * dx, 2 * dy) for dy, dx in PLACES[1:]]
    moved, more = lax.optimization_barrier((moved, more))
    packed = in_order([piece] + moved)
    table = permute_embedding(embedding)
    blocks = [packed] + [shifted(packed, *SHIFTS[parity]) for parity in PLACES[1:]]
    blocks[1:], table = lax.optimization_barrier((blocks[1:], table))
    other_blocks = [swap_cores(block) for block in blocks]

    *e, stats, scale = logits_of(blocks, table, own_labels, own_slots)
    other_blocks, e = lax.optimization_barrier((other_blocks, e))
    *e_other, stats_other, _ = logits_of(other_blocks, table, other_labels, other_slots)
    far_part, e_other = lax.optimization_barrier((gradient_of(1, (0, 1), e_other, table, stats_other), e_other))
    near_part, e = lax.optimization_barrier((gradient_of(0, (1,), e_other, table, stats_other), e))
    far_blocks = combine((0, 1), product_of(1, (0, 1), e, table), stats, [swap_cores(part) for part in far_part])
    far_blocks, e = lax.optimization_barrier((far_blocks, e))
    (near_block,) = combine((1,), product_of(0, (1,), e, table), stats, [swap_cores(part) for part in near_part])
    near_block, e, e_other = lax.optimization_barrier((near_block, e, e_other))
    stay_part, e = lax.optimization_barrier((gradient_of(0, (0,), e_other, table, stats_other, 2), e))
    (stay_block,) = combine((0,), product_of(0, (0,), e, table), stats, [swap_cores(part) for part in stay_part])
    parts = [stay_block, near_block, *far_blocks]
    sums = class_sum([parts[0]] + [shifted(part, *SHIFTS[parity]) for part, parity in zip(parts[1:], PLACES[1:])])
    plane = [sums[0]] + [shifted(block, 2 * dx, 2 * dy) for block, (dy, dx) in zip(sums[1:], PLACES[1:])]
    column = lax.all_to_all(plane_sum(plane, place, more), ("z_lo", "z_hi"), 0, 0, tiled=True)

    loss, grad = finish(column, residual, gain, token_weight.reshape(1, 512), scale)
    return (loss.reshape(32), grad)


def solution(mesh):
    fine = Mesh(mesh.devices.reshape(4, 2, 2, 2, 2, 2, 2), (*CHIPS, "core"))
    section, fsdp = ("z_lo", "y1", "y0"), ("z_hi", "x1", "x0", "core")
    in_specs = (P(fsdp, section), P(section), P(section + fsdp, None), P(), P())
    out_specs = (P(fsdp), P(fsdp, section))
    return jax.shard_map(on_device, mesh=fine, in_specs=in_specs, out_specs=out_specs, check_vma=False)
```

```python
import functools

import jax
import jax.numpy as jnp
from jax import lax
from jax.experimental import pallas as pl
from jax.experimental.pallas import tpu as pltpu
from jax.sharding import Mesh, PartitionSpec as P

D = 4608
EPS = 1e-06
CAP = 30.0
ROWS = 1000
PADDED = 1024
PIECE = 288
WIDE = 1152
HALF = 2 * WIDE
BLOCK = 64
ROOM = BLOCK + 8
TILES = WIDE // 128
SLOTS = 7
PACKED = TILES * BLOCK + 16
F32 = jnp.float32
BF16 = jnp.bfloat16
VMEM = pltpu.MemorySpace.VMEM
WHOLE = pl.BlockSpec(memory_space=VMEM)
SCALARS = pl.BlockSpec(memory_space=pltpu.MemorySpace.SMEM)
BIG = pltpu.CompilerParams(vmem_limit_bytes=20 * 1024 * 1024)


def near(array):
    return pltpu.with_memory_space_constraint(array, VMEM)


CHIPS = ("z_lo", "y1", "y0", "z_hi", "x1", "x0")
SHIFTS = {(0, 1): (1, 0), (1, 0): (0, 1), (1, 1): (-1, -1)}
PLACES = ((0, 0), *SHIFTS)


def this_chip():
    number = 0
    for name in CHIPS:
        number = number * lax.axis_size(name) + lax.axis_index(name)
    return number


def first_row():
    return (this_chip() * 2 + lax.axis_index("core")) * ROWS


def label_kernel(labels_ref, own_labels, own_slots, other_labels, other_slots, place_ref, rounds_ref):
    zl, y1, y0, zh, x1, x0, core = (lax.axis_index(name) for name in (*CHIPS, "core"))
    labels = labels_ref[...]
    token = lax.broadcasted_iota(jnp.int32, (1, 512), 1)
    group = (token >> 5 & 1) * 4 + (token >> 6 & 1) * 2 + (token >> 7 & 1)
    owner = ((labels.astype(F32) + 0.5) * (1.0 / (2 * ROWS))).astype(jnp.int32)
    key = owner * 8 + group
    square = (512, 512)
    down = lax.broadcasted_iota(jnp.int32, square, 0)
    across = lax.broadcasted_iota(jnp.int32, square, 1)
    keys = jnp.broadcast_to(key, square)
    key_down = jnp.sum(jnp.where(down == across, keys, 0), axis=1, keepdims=True)
    earlier = jnp.logical_and(jnp.broadcast_to(key_down, square) == keys, down < across)
    rank = jnp.sum(earlier.astype(jnp.int32), axis=0, keepdims=True)
    turn = ((rank.astype(F32) + 0.5) * (1.0 / SLOTS)).astype(jnp.int32)
    slot = rank - turn * SLOTS
    rounds_ref[...] = jnp.broadcast_to(jnp.max(turn, axis=1, keepdims=True) + 1, (1, 128))

    taken = jnp.where(jnp.logical_and(owner == this_chip(), turn == 0), group * 8 + slot, -1)
    shifted_labels = labels - first_row() + 1
    for half, label_ref, slot_ref in ((core, own_labels, own_slots), (1 - core, other_labels, other_slots)):
        at = lax.broadcasted_iota(jnp.int32, (32, 512), 0)
        wanted = half * 32 + (at + 16 * x0 & 31)
        match = jnp.broadcast_to(taken, (32, 512)) == wanted
        held = jnp.sum(jnp.where(match, jnp.broadcast_to(shifted_labels, (32, 512)), 0), axis=1, keepdims=True) - 1
        vocab = lax.broadcasted_iota(jnp.int32, (32, PADDED), 1)
        slot_ref[...] = jnp.where(vocab == held, 1.0, 0.0).astype(BF16)
        chunks = []
        for chunk in range(8):
            rx, from_x1, from_zh = chunk // 4, chunk // 2 % 2, chunk % 2
            picked = jnp.zeros((1, 32), jnp.int32)
            for from_x0 in range(2):
                for from_core in range(2):
                    source = ((from_zh * 2 + from_x1) * 2 + from_x0) * 2 + from_core
                    use = jnp.logical_and(half == from_core, (x0 + rx) % 2 == from_x0)
                    picked = jnp.where(use, labels[:, source * 32 : source * 32 + 32], picked)
            chunks.append(picked)
        label_ref[...] = jnp.concatenate(chunks, axis=1)

    code = jnp.broadcast_to(jnp.where(turn == 0, owner * 8 + slot, -1), (BLOCK, 512))
    at = lax.broadcasted_iota(jnp.int32, (BLOCK, 512), 0)
    own = (at >> 5) * 256 + x1 * 128 + x0 * 64 + core * 32 + (at & 31)
    pick = lax.broadcasted_iota(jnp.int32, (BLOCK, 512), 1) == own
    own_code = jnp.sum(jnp.where(pick, code, 0), axis=1, keepdims=True)
    column = lax.broadcasted_iota(jnp.int32, (BLOCK, 128), 1)
    parity = column >> 3 & 3
    from_y = (column >> 6 ^ y1) * 2 + y0 + 4
    from_x = (column >> 5 & 1 ^ x1) * 2 + x0 + 4
    for index, (dx, dy) in enumerate(SHIFTS.values()):
        from_y = from_y - jnp.where(parity == index + 1, dy, 0)
        from_x = from_x - jnp.where(parity == index + 1, dx, 0)
    chip = ((zl * 4 + (from_y & 3)) * 2 + zh) * 4 + (from_x & 3)
    place_ref[...] = jnp.where(own_code == chip * 8 + (column & 7), 1.0, 0.0).astype(BF16)


def label_places(labels):
    return pl.pallas_call(
        label_kernel,
        in_specs=[WHOLE],
        out_specs=[WHOLE] * 6,
        out_shape=[
            pltpu.VMEM((1, 256), jnp.int32),
            pltpu.VMEM((32, PADDED), BF16),
            pltpu.VMEM((1, 256), jnp.int32),
            pltpu.VMEM((32, PADDED), BF16),
            pltpu.VMEM((BLOCK, 128), BF16),
            jax.ShapeDtypeStruct((1, 128), jnp.int32),
        ],
        compiler_params=BIG,
        cost_estimate=pl.CostEstimate(flops=10 * 512 * 512, bytes_accessed=1 << 20, transcendentals=0),
        name="label_places",
    )(labels)


def far(array):
    return pltpu.with_memory_space_constraint(array, pltpu.MemorySpace.HBM)


def permute_kernel(in_ref, out_ref):
    step = in_ref.shape[0]
    number = pl.program_id(0)
    first = pl.multiple_of(number * step, step)
    tail = PADDED - ROWS
    for y0 in range(2):

        @pl.when(lax.axis_index("y0") == y0)
        def _():
            for at in range(4):
                y = at % 2 * 2 + (at // 2 + y0) % 2
                parts = [in_ref[:, (z * 4 + y) * PIECE : (z * 4 + y + 1) * PIECE] for z in range(4)]
                out_ref[pl.ds(first, step), at * WIDE : (at + 1) * WIDE] = jnp.concatenate(parts, axis=1)

    @pl.when(number == PADDED // step - 1)
    def _():
        rows = lax.broadcasted_iota(jnp.int32, (32, 1), 0)
        kept = out_ref[PADDED - 32 : PADDED, :].astype(F32)
        out_ref[PADDED - 32 : PADDED, :] = jnp.where(rows < 32 - tail, kept, 0.0).astype(BF16)


def permute_embedding(embedding):
    step = 128
    return pl.pallas_call(
        permute_kernel,
        grid=(PADDED // step,),
        in_specs=[pl.BlockSpec((step, D), lambda i: (i, 0))],
        out_specs=WHOLE,
        out_shape=pltpu.VMEM((PADDED, D), BF16),
        compiler_params=BIG,
        cost_estimate=pl.CostEstimate(flops=0, bytes_accessed=4 * ROWS * D, transcendentals=0),
        name="permute_embedding",
    )(embedding)


def spread_kernel(residual_hbm, gain_hbm, out_ref, residual_ref, gain_ref, arrived):
    copies = [
        pltpu.make_async_copy(residual_hbm, residual_ref, arrived.at[0]),
        pltpu.make_async_copy(gain_hbm, gain_ref, arrived.at[1]),
    ]
    for copy in copies:
        copy.start()
    for copy in copies:
        copy.wait()
    values = residual_ref[...].astype(F32)
    gain = gain_ref[...].astype(F32).reshape(1, PIECE)
    corner = jnp.concatenate([values[8 * g : 8 * g + 8, 256:PIECE] for g in range(4)], axis=1)
    last = jnp.concatenate([gain[:, 256:PIECE], jnp.zeros((1, 96), F32)], axis=1)
    rows = [values[:, 0:128], values[:, 128:256], corner, gain[:, 0:128], gain[:, 128:256], last, jnp.zeros((5, 128), F32)]
    tiles = jnp.concatenate(rows, axis=0).astype(BF16)
    for place in range(8):
        out_ref[place] = tiles


def spread(residual, gain):
    return pl.pallas_call(
        spread_kernel,
        in_specs=[pl.BlockSpec(memory_space=pl.ANY)] * 2,
        out_specs=WHOLE,
        out_shape=pltpu.VMEM((8, 80, 128), BF16),
        scratch_shapes=[
            pltpu.VMEM((32, PIECE), BF16),
            pltpu.VMEM((PIECE,), BF16),
            pltpu.SemaphoreType.DMA((2,)),
        ],
        compiler_params=BIG,
        name="spread",
    )(far(residual), far(gain))


def pack_kernel(in_ref, out_ref):
    for zh in range(2):
        parts = []
        for zl in range(4):
            tiles = in_ref[zl * 2 + zh].astype(F32)
            corner = jnp.concatenate([tiles[64:72, 32 * g : 32 * g + 32] for g in range(4)], axis=0)
            parts += [tiles[0:32, :], tiles[32:64, :], corner]
        wide = jnp.concatenate(parts, axis=1)
        for k in range(TILES):
            tile = wide[:, k * 128 : (k + 1) * 128].astype(BF16)
            out_ref[k * BLOCK + zh * 32 : k * BLOCK + zh * 32 + 32, :] = tile
    parts = []
    for zl in range(4):
        tiles = in_ref[zl * 2].astype(F32)
        parts += [tiles[72:73, :], tiles[73:74, :], tiles[74:75, 0:32]]
    gains = jnp.concatenate(parts, axis=1)
    rows = [gains[:, k * 128 : (k + 1) * 128] for k in range(TILES)]
    tile = jnp.concatenate(rows + [jnp.zeros((16 - TILES, 128), F32)], axis=0).astype(BF16)
    out_ref[TILES * BLOCK : PACKED, :] = tile


def pack_tokens(gathered):
    return pl.pallas_call(
        pack_kernel,
        in_specs=[WHOLE],
        out_specs=WHOLE,
        out_shape=pltpu.VMEM((PACKED, 128), BF16),
        compiler_params=BIG,
        name="pack_tokens",
    )(near(gathered))


def absolute(relative):
    return (lax.axis_index("y1") + relative // 2) % 2 * 2 + (lax.axis_index("x1") + relative % 2) % 2


def order_kernel(*refs):
    in_refs, out_ref = refs[:4], refs[4]
    for relative, ref in enumerate(in_refs):
        out_ref[absolute(relative)] = ref[...]


def in_order(pieces):
    return pl.pallas_call(
        order_kernel,
        in_specs=[WHOLE] * 4,
        out_specs=WHOLE,
        out_shape=pltpu.VMEM((4, PACKED, 128), BF16),
        compiler_params=BIG,
        name="in_order",
    )(*(near(a) for a in pieces))


def logits_kernel(*refs):
    blocks, (embedding_ref, labels_ref, slot_ref, e_near, e_far, stats_ref, *scale_ref, normed) = refs[:4], refs[4:]
    gains = [
        [blocks[ry * 2][y1 * 2, TILES * BLOCK : PACKED, :].astype(F32) for y1 in range(2)] for ry in range(2)
    ]
    for x in range(4):
        tokens = slice(x * BLOCK, (x + 1) * BLOCK)

        def tile(ry, y1, k):
            return blocks[ry * 2 + x // 2][y1 * 2 + x % 2, k * BLOCK : (k + 1) * BLOCK, :].astype(F32)

        places = [(ry, y1, k) for ry in range(2) for y1 in range(2) for k in range(TILES)]
        squares = jnp.zeros((BLOCK, 128), F32)
        for place in places:
            v = tile(*place)
            squares += v * v
        scale = lax.rsqrt(jnp.sum(squares, axis=1, keepdims=True) / D + EPS)
        for ref in scale_ref:
            ref[tokens, :] = jnp.broadcast_to(scale, (BLOCK, 128))
        for ry, y1, k in places:
            column = ry * HALF + y1 * WIDE + k * 128
            normed[tokens, column : column + 128] = (
                tile(ry, y1, k) * scale * gains[ry][y1][k : k + 1, :]
            ).astype(BF16)
    raw = lax.dot_general(
        embedding_ref[...], normed[...], (((1,), (1,)), ((), ())), preferred_element_type=F32
    )
    ratio = jnp.tanh(raw / CAP)
    row = lax.broadcasted_iota(jnp.int32, raw.shape, 0)
    inside = row < ROWS
    is_label = jnp.logical_and(inside, row + first_row() == labels_ref[...])
    exps = jnp.where(inside, jnp.exp(CAP * ratio), 0.0)
    others = jnp.where(is_label, 0.0, exps * (1.0 - ratio * ratio))
    stats_ref[0:1, :] = jnp.sum(exps, axis=0, keepdims=True)
    stats_ref[1:2, :] = jnp.sum(others * raw, axis=0, keepdims=True)
    stats_ref[2:3, :] = jnp.sum(jnp.where(is_label, raw, 0.0), axis=0, keepdims=True)
    stats_ref[3:8, :] = jnp.zeros((5, raw.shape[1]), F32)
    for rx, e_ref in enumerate((e_near, e_far)):
        e_ref[0:128, :] = others[:, rx * 128 : (rx + 1) * 128].T.astype(BF16)
        e_ref[128:144, :] = slot_ref[rx * 16 : (rx + 1) * 16, :]


def logits_of(blocks, embedding, labels, slots, with_scale):
    return pl.pallas_call(
        logits_kernel,
        in_specs=[WHOLE] * 7,
        out_specs=[WHOLE] * (3 + with_scale),
        out_shape=[
            pltpu.VMEM((144, PADDED), BF16),
            pltpu.VMEM((144, PADDED), BF16),
            pltpu.VMEM((8, 256), F32),
        ]
        + [pltpu.VMEM((256, 128), F32)] * with_scale,
        scratch_shapes=[pltpu.VMEM((256, D), BF16)],
        compiler_params=BIG,
        cost_estimate=pl.CostEstimate(flops=2 * 256 * PADDED * D, bytes_accessed=2 * PADDED * D, transcendentals=2 * 256 * PADDED),
        name="logits",
    )(*(near(a) for a in (*blocks, embedding, labels, slots)))


def three_pieces(value):
    high = value.astype(BF16).astype(F32)
    middle = (value - high).astype(BF16).astype(F32)
    low = (value - high - middle).astype(BF16).astype(F32)
    return [high, middle, low]


def stats_row(values):
    pieces = []
    for value in values:
        for piece in three_pieces(value):
            pieces += [piece, jnp.zeros((1, 128 - BLOCK), F32)]
    return jnp.concatenate(pieces, axis=1)


def read_stats(row):
    return [
        sum(row[:, (3 * i + j) * 128 : (3 * i + j) * 128 + BLOCK] for j in (2, 1, 0))
        for i in range(3)
    ]


def rows_of(term, parity, x1):
    at = parity * 144
    return term[at + x1 * BLOCK : at + (x1 + 1) * BLOCK, :], term[at + 128 + 8 * x1 : at + 128 + 8 * x1 + 8, :]


def gradient_kernel(ry, parities, *refs):
    e_refs, (embedding_ref, stats_ref, *out_refs) = refs[: len(parities)], refs[len(parities) :]
    last = lax.broadcasted_iota(jnp.int32, (8, WIDE), 0) == 7
    left = jnp.concatenate([ref[...] for ref in e_refs], axis=0)
    rows = {}
    for rx in parities:
        for x1 in range(2):
            at = (rx * 2 + x1) * BLOCK
            values = [stats_ref[i : i + 1, at : at + BLOCK] for i in range(3)]
            rows[rx, x1] = jnp.broadcast_to(stats_row(values), (8, WIDE))
    for y1 in range(2):
        column = ry * HALF + y1 * WIDE
        term = jnp.dot(left, embedding_ref[:, column : column + WIDE], preferred_element_type=F32)
        for place, rx in enumerate(parities):
            for x1 in range(2):
                out_ref, at = out_refs[y1 * len(out_refs) // 2], place * 4 // len(out_refs) + x1
                at += y1 * 2 if len(out_refs) == 1 else 0
                main, extra = rows_of(term, place, x1)
                out_ref[at, 0:BLOCK, :] = main.astype(BF16)
                out_ref[at, BLOCK:ROOM, :] = jnp.where(last, rows[rx, x1], extra).astype(BF16)


def gradient_of(ry, parities, e, embedding, stats, pieces=1):
    count = len(parities)
    return pl.pallas_call(
        functools.partial(gradient_kernel, ry, parities),
        in_specs=[WHOLE] * (2 + count),
        out_specs=[WHOLE] * pieces,
        out_shape=[pltpu.VMEM((4 * count // pieces, ROOM, WIDE), BF16)] * pieces,
        compiler_params=BIG,
        cost_estimate=pl.CostEstimate(flops=144 * count * PADDED * D, bytes_accessed=PADDED * D, transcendentals=0),
        name="gradient",
    )(*(near(e[rx]) for rx in parities), near(embedding), near(stats))


def product_kernel(ry, *refs):
    e_refs, (embedding_ref, out_ref) = refs[:-2], refs[-2:]
    left = jnp.concatenate([ref[...] for ref in e_refs], axis=0)
    out_ref[...] = jnp.dot(left, embedding_ref[:, ry * HALF : (ry + 1) * HALF], preferred_element_type=F32)


def product_of(ry, parities, e, embedding):
    count = len(parities)
    return pl.pallas_call(
        functools.partial(product_kernel, ry),
        in_specs=[WHOLE] * (1 + count),
        out_specs=WHOLE,
        out_shape=pltpu.VMEM((144 * count, HALF), F32),
        compiler_params=BIG,
        cost_estimate=pl.CostEstimate(flops=144 * count * PADDED * D, bytes_accessed=PADDED * D, transcendentals=0),
        name="product",
    )(*(near(e[rx]) for rx in parities), near(embedding))


def combine_kernel(parities, term_ref, stats_ref, *refs):
    other_refs, out_refs = refs[: -len(parities)], refs[-len(parities) :]
    last = lax.broadcasted_iota(jnp.int32, (8, WIDE), 0) == 7
    for place, rx in enumerate(parities):
        for x1 in range(2):
            at = (rx * 2 + x1) * BLOCK
            values = [stats_ref[i : i + 1, at : at + BLOCK] for i in range(3)]
            others = other_refs[0][place * 4 // len(other_refs) + x1, BLOCK:ROOM, :].astype(F32)
            others = read_stats(others[7:8, :])
            row = jnp.broadcast_to(stats_row([a + b for a, b in zip(values, others)]), (8, WIDE))
            for y1 in range(2):
                other_ref, at = other_refs[y1 * len(other_refs) // 2], place * 4 // len(other_refs) + x1
                at += y1 * 2 if len(other_refs) == 1 else 0
                main, extra = rows_of(term_ref[:, y1 * WIDE : (y1 + 1) * WIDE], place, x1)
                main = main + other_ref[at, 0:BLOCK, :].astype(F32)
                extra = extra + other_ref[at, BLOCK:ROOM, :].astype(F32)
                out_refs[place][y1 * 2 + x1, 0:BLOCK, :] = main.astype(BF16)
                out_refs[place][y1 * 2 + x1, BLOCK:ROOM, :] = jnp.where(last, row, extra).astype(BF16)


def combine(parities, term, stats, other):
    count = len(parities)
    return pl.pallas_call(
        functools.partial(combine_kernel, parities),
        in_specs=[WHOLE] * (2 + len(other)),
        out_specs=[WHOLE] * count,
        out_shape=[pltpu.VMEM((4, ROOM, WIDE), BF16)] * count,
        compiler_params=BIG,
        name="combine",
    )(near(term), near(stats), *(near(a) for a in other))


def class_kernel(*refs):
    in_refs, out_refs = refs[:4], refs[4:]
    last = lax.broadcasted_iota(jnp.int32, (8, WIDE), 0) == 7
    for relative, out_ref in enumerate(out_refs):
        block = absolute(relative)
        total = in_refs[0][block, 0:BLOCK, :].astype(F32)
        for ref in in_refs[1:]:
            total += ref[block, 0:BLOCK, :].astype(F32)
        out_ref[0:BLOCK, :] = total.astype(BF16)
        extras = [ref[block, BLOCK:ROOM, :].astype(F32) for ref in in_refs]
        row = sum(extra[7:8, :] for extra in extras)
        row = jnp.broadcast_to(stats_row(read_stats(row)), (8, WIDE))
        extras = [jnp.where(last, row if i == 0 else 0.0, extra) for i, extra in enumerate(extras)]
        out_ref[BLOCK : BLOCK + 32, :] = jnp.concatenate(extras, axis=0).astype(BF16)


def class_sum(blocks):
    return pl.pallas_call(
        class_kernel,
        in_specs=[WHOLE] * 4,
        out_specs=[WHOLE] * 4,
        out_shape=[pltpu.VMEM((BLOCK + 32, WIDE), BF16)] * 4,
        compiler_params=BIG,
        name="class_sum",
    )(*(near(a) for a in blocks))


def plane_kernel(*refs):
    in_refs, (place_ref, more_ref, values_ref, gain_ref, weight_ref, scale_ref, out_ref, *kept) = refs[:4], refs[4:]
    zh, x1, x0, core = (lax.axis_index(name) for name in ("z_hi", "x1", "x0", "core"))
    own = (((zh * 2 + x1) * 2 + x0) * 2 + core) * 32 + lax.broadcasted_iota(jnp.int32, (32, 512), 0)
    own_weight = jnp.where(lax.broadcasted_iota(jnp.int32, (32, 512), 1) == own, weight_ref[...], 0.0)
    kept[0][...] = values_ref[...].astype(F32)
    kept[1][...] = gain_ref[...].astype(F32)
    kept[2][...] = jnp.broadcast_to(jnp.sum(own_weight, axis=1, keepdims=True), (32, 128))
    kept[3][...] = scale_ref[pl.ds(pl.multiple_of(x1 * BLOCK + zh * 32, 32), 32), :]
    total = in_refs[0][0:BLOCK, :].astype(F32)
    for ref in in_refs[1:]:
        total += ref[0:BLOCK, :].astype(F32)
    extras = [ref[BLOCK : BLOCK + 32, :].astype(F32) for ref in in_refs]
    stacked = jnp.concatenate(extras, axis=0).astype(BF16)
    label_rows = jnp.dot(place_ref[...], stacked, preferred_element_type=F32) + more_ref[...].astype(F32)
    row = sum(extra[7:8, :] for extra in extras)
    pieces = []
    for value in read_stats(row):
        pieces += three_pieces(value)
    sums = jnp.concatenate(pieces + [jnp.zeros((32 - 9, BLOCK), F32)], axis=0)
    for zl in range(4):
        for zh in range(2):
            main = total[zh * 32 : zh * 32 + 32, zl * PIECE : (zl + 1) * PIECE]
            rows = label_rows[zh * 32 : zh * 32 + 32, zl * PIECE : (zl + 1) * PIECE]
            out_ref[zl * 2 + zh] = jnp.concatenate([main, rows, sums], axis=1).astype(BF16)


def plane_sum(received, place, more, values, gain, weight, scale):
    args = (*received, place, more, values, gain, weight, scale)
    return pl.pallas_call(
        plane_kernel,
        in_specs=[WHOLE] * len(args),
        out_specs=[WHOLE] * 5,
        out_shape=[
            pltpu.VMEM((8, 32, 640), BF16),
            pltpu.VMEM((32, PIECE), F32),
            pltpu.VMEM((1, PIECE), F32),
            pltpu.VMEM((32, 128), F32),
            pltpu.VMEM((32, 128), F32),
        ],
        compiler_params=BIG,
        name="plane_sum",
    )(*(near(a) for a in args))


def final_kernel(in_ref, values_ref, gain_ref, weight_ref, scale_ref, loss_ref, grad_ref):
    zh = lax.axis_index("z_hi")
    total = in_ref[0].astype(F32)
    for source in range(1, 8):
        total += in_ref[source].astype(F32)
    sums = total[0:16, 2 * PIECE : 640]
    pick = lax.broadcasted_iota(jnp.int32, (32, BLOCK), 1) == zh * 32 + lax.broadcasted_iota(
        jnp.int32, (32, BLOCK), 0
    )

    def column(i):
        value = sum(sums[3 * i + j : 3 * i + j + 1, :] for j in (2, 1, 0))
        return jnp.sum(jnp.where(pick, jnp.broadcast_to(value, (32, BLOCK)), 0.0), axis=1, keepdims=True)

    sum_exp, inner_others, raw = column(0), column(1), column(2)
    weight = weight_ref[:, 0:1]
    scaling = scale_ref[:, 0:1]
    ratio = jnp.tanh(raw / CAP)
    capped = CAP * ratio
    log_total = jnp.log(sum_exp)
    loss = log_total - capped
    coefficient = (jnp.exp(capped - log_total) - 1.0) * weight * (1.0 - ratio * ratio)
    coefficient = coefficient.astype(BF16).astype(F32)
    share = weight / sum_exp
    grad_normed = total[:, 0:PIECE] * share + total[:, PIECE : 2 * PIECE] * coefficient
    inner = (inner_others * share + coefficient * raw) / scaling
    upstream = grad_normed * gain_ref[...]
    values = values_ref[...]
    grad_ref[...] = scaling * upstream - values * (scaling * scaling * scaling * inner / D)
    eye = lax.broadcasted_iota(jnp.int32, (32, 32), 0) == lax.broadcasted_iota(jnp.int32, (32, 32), 1)
    loss_ref[...] = jnp.sum(jnp.where(eye, jnp.broadcast_to(loss, (32, 32)), 0.0), axis=0, keepdims=True)


def finish(received, values, gain, weight, scale):
    return pl.pallas_call(
        final_kernel,
        in_specs=[WHOLE] * 5,
        out_specs=[WHOLE] * 2,
        out_shape=[jax.ShapeDtypeStruct((1, 32), F32), jax.ShapeDtypeStruct((32, PIECE), F32)],
        compiler_params=BIG,
        name="finish",
    )(*(near(a) for a in (received, values, gain, weight, scale)))


def swap_cores(array):
    return lax.ppermute(array, "core", [(0, 1), (1, 0)])


def shifted(array, dx, dy):
    pairs = []
    for chip in range(128):
        line, y, zh, x = chip // 32, chip // 8 % 4, chip // 4 % 2, chip % 4
        pairs.append((chip, ((line * 4 + (y + dy) % 4) * 2 + zh) * 4 + (x + dx) % 4))
    return lax.ppermute(array, CHIPS, pairs)


def later_rows(labels, embedding, rounds):
    def one_round(carry):
        number, rows = carry
        _, tokens = lax.optimization_barrier((number, labels))
        zl, y1, y0, zh, x1, x0, core = (lax.axis_index(name) for name in (*CHIPS, "core"))
        token = jnp.arange(512, dtype=jnp.int32)
        group = (token // 32) % 2 * 4 + (token // 64) % 2 * 2 + (token // 128) % 2
        owner = tokens // (2 * ROWS)
        key = owner * 8 + group
        same = jnp.logical_and(key[:, None] == key[None, :], token[None, :] < token[:, None])
        rank = jnp.sum(same.astype(jnp.int32), axis=1)
        turn, slot = rank // SLOTS, rank % SLOTS
        taken = jnp.where(jnp.logical_and(owner == this_chip(), turn == number), group * 8 + slot, -1)
        match = taken[None, :] == jnp.arange(64, dtype=jnp.int32)[:, None]
        held = jnp.sum(jnp.where(match, (tokens - first_row())[None, :] + 1, 0), axis=1) - 1
        chosen = (held[:, None] == jnp.arange(ROWS, dtype=jnp.int32)[None, :]).astype(BF16)
        found = jnp.dot(chosen, embedding, preferred_element_type=F32).astype(BF16)
        found = found.reshape(2, 2, 2, 8, 4, 4, PIECE).transpose(0, 5, 2, 1, 3, 4, 6).reshape(2, 16, 8, WIDE)
        ours = lax.dynamic_index_in_dim(found, core, 0, keepdims=False)
        theirs = lax.dynamic_index_in_dim(found, 1 - core, 0, keepdims=False)
        ours = ours + swap_cores(theirs)
        ours = lax.all_to_all(ours, ("y1", "y0", "x1", "x0"), 0, 0, tiled=True).reshape(128, WIDE)
        local = jnp.arange(BLOCK, dtype=jnp.int32)
        own = (((local // 32 * 2 + x1) * 2 + x0) * 2 + core) * 32 + local % 32
        place = jnp.arange(16, dtype=jnp.int32)
        chips = ((zl * 4 + place // 4) * 2 + zh) * 4 + place % 4
        hit = jnp.logical_and(owner[own][:, None] == chips[None, :], (turn[own] == number)[:, None])
        at = slot[own][:, None] == jnp.arange(8, dtype=jnp.int32)[None, :]
        put = jnp.logical_and(hit[:, :, None], at[:, None, :]).astype(BF16).reshape(BLOCK, 128)
        return number + 1, rows + jnp.dot(put, ours, preferred_element_type=F32).astype(BF16)

    start = (jnp.int32(1), jnp.zeros((BLOCK, WIDE), BF16))
    return lax.while_loop(lambda carry: carry[0] < rounds, one_round, start)[1]


def on_device(residual, final_gain, embedding, labels, token_weight):
    gain = final_gain.reshape(1, PIECE)
    gathered = lax.all_to_all(spread(residual, final_gain), ("z_lo", "z_hi"), 0, 0, tiled=True)
    piece, embedding, labels = lax.optimization_barrier((pack_tokens(gathered), embedding, labels))

    moved = [shifted(piece, 2 * dx, 2 * dy) for dy, dx in PLACES[1:]]
    *early, rounds = label_places(labels.reshape(1, 512))
    more = later_rows(labels, embedding, rounds[0, 0])
    moved, more, early = lax.optimization_barrier((moved, more, early))
    own_labels, own_slots, other_labels, other_slots, place = early
    packed = in_order([piece] + moved)
    table = permute_embedding(embedding)
    blocks = [packed] + [shifted(packed, *SHIFTS[parity]) for parity in PLACES[1:]]
    blocks[1:], table = lax.optimization_barrier((blocks[1:], table))
    other_blocks = [swap_cores(block) for block in blocks]

    *e, stats, scale = logits_of(blocks, table, own_labels, own_slots, True)
    other_blocks, e = lax.optimization_barrier((other_blocks, e))
    *e_other, stats_other = logits_of(other_blocks, table, other_labels, other_slots, False)
    far_part, e_other = lax.optimization_barrier((gradient_of(1, (0, 1), e_other, table, stats_other), e_other))
    near_part, e = lax.optimization_barrier((gradient_of(0, (1,), e_other, table, stats_other), e))
    far_blocks = combine((0, 1), product_of(1, (0, 1), e, table), stats, [swap_cores(part) for part in far_part])
    far_blocks, e = lax.optimization_barrier((far_blocks, e))
    (near_block,) = combine((1,), product_of(0, (1,), e, table), stats, [swap_cores(part) for part in near_part])
    near_block, e, e_other = lax.optimization_barrier((near_block, e, e_other))
    stay_part, e = lax.optimization_barrier((gradient_of(0, (0,), e_other, table, stats_other, 2), e))
    (stay_block,) = combine((0,), product_of(0, (0,), e, table), stats, [swap_cores(part) for part in stay_part])
    parts = [stay_block, near_block, *far_blocks]
    sums = class_sum([parts[0]] + [shifted(part, *SHIFTS[parity]) for part, parity in zip(parts[1:], PLACES[1:])])
    plane = [shifted(block, 2 * dx, 2 * dy) for block, (dy, dx) in zip(sums[:0:-1], PLACES[:0:-1])]
    plane = [sums[0]] + plane[::-1]
    plane, *kept = plane_sum(plane, place, more, residual, gain, token_weight.reshape(1, 512), scale)
    column = lax.all_to_all(plane, ("z_lo", "z_hi"), 0, 0, tiled=True)
    loss, grad = finish(column, *kept)
    return (loss.reshape(32), grad)


def solution(mesh):
    fine = Mesh(mesh.devices.reshape(4, 2, 2, 2, 2, 2, 2), (*CHIPS, "core"))
    section, fsdp = ("z_lo", "y1", "y0"), ("z_hi", "x1", "x0", "core")
    in_specs = (P(fsdp, section), P(section), P(section + fsdp, None), P(), P())
    out_specs = (P(fsdp), P(fsdp, section))
    return jax.shard_map(on_device, mesh=fine, in_specs=in_specs, out_specs=out_specs, check_vma=False)
```

```python
import functools

import jax
import jax.numpy as jnp
from jax import lax
from jax.experimental import pallas as pl
from jax.experimental.pallas import tpu as pltpu
from jax.sharding import Mesh, PartitionSpec as P

D = 4608
EPS = 1e-06
CAP = 30.0
ROWS = 1000
PADDED = 1024
PIECE = 288
WIDE = 1152
HALF = 2 * WIDE
BLOCK = 64
ROOM = BLOCK + 8
TILES = WIDE // 128
SLOTS = 7
PACKED = TILES * BLOCK + 16
F32 = jnp.float32
BF16 = jnp.bfloat16
VMEM = pltpu.MemorySpace.VMEM
WHOLE = pl.BlockSpec(memory_space=VMEM)
SCALARS = pl.BlockSpec(memory_space=pltpu.MemorySpace.SMEM)
BIG = pltpu.CompilerParams(vmem_limit_bytes=20 * 1024 * 1024)


def near(array):
    return pltpu.with_memory_space_constraint(array, VMEM)


CHIPS = ("z_lo", "y1", "y0", "z_hi", "x1", "x0")
SHIFTS = {(0, 1): (1, 0), (1, 0): (0, 1), (1, 1): (-1, -1)}
PLACES = ((0, 0), *SHIFTS)


def this_chip():
    number = 0
    for name in CHIPS:
        number = number * lax.axis_size(name) + lax.axis_index(name)
    return number


def first_row():
    return (this_chip() * 2 + lax.axis_index("core")) * ROWS


def label_kernel(labels_ref, own_labels, own_slots, other_labels, other_slots, place_ref, rounds_ref):
    zl, y1, y0, zh, x1, x0, core = (lax.axis_index(name) for name in (*CHIPS, "core"))
    labels = labels_ref[...]
    token = lax.broadcasted_iota(jnp.int32, (1, 512), 1)
    group = (token >> 5 & 1) * 4 + (token >> 6 & 1) * 2 + (token >> 7 & 1)
    owner = ((labels.astype(F32) + 0.5) * (1.0 / (2 * ROWS))).astype(jnp.int32)
    key = owner * 8 + group
    square = (512, 512)
    down = lax.broadcasted_iota(jnp.int32, square, 0)
    across = lax.broadcasted_iota(jnp.int32, square, 1)
    keys = jnp.broadcast_to(key, square)
    key_down = jnp.sum(jnp.where(down == across, keys, 0), axis=1, keepdims=True)
    earlier = jnp.logical_and(jnp.broadcast_to(key_down, square) == keys, down < across)
    rank = jnp.sum(earlier.astype(jnp.int32), axis=0, keepdims=True)
    turn = ((rank.astype(F32) + 0.5) * (1.0 / SLOTS)).astype(jnp.int32)
    slot = rank - turn * SLOTS
    rounds_ref[...] = jnp.broadcast_to(jnp.max(turn, axis=1, keepdims=True) + 1, (1, 128))

    taken = jnp.where(jnp.logical_and(owner == this_chip(), turn == 0), group * 8 + slot, -1)
    shifted_labels = labels - first_row() + 1
    for half, label_ref, slot_ref in ((core, own_labels, own_slots), (1 - core, other_labels, other_slots)):
        at = lax.broadcasted_iota(jnp.int32, (32, 512), 0)
        wanted = half * 32 + (at + 16 * x0 & 31)
        match = jnp.broadcast_to(taken, (32, 512)) == wanted
        held = jnp.sum(jnp.where(match, jnp.broadcast_to(shifted_labels, (32, 512)), 0), axis=1, keepdims=True) - 1
        vocab = lax.broadcasted_iota(jnp.int32, (32, PADDED), 1)
        slot_ref[...] = jnp.where(vocab == held, 1.0, 0.0).astype(BF16)
        chunks = []
        for chunk in range(8):
            rx, from_x1, from_zh = chunk // 4, chunk // 2 % 2, chunk % 2
            picked = jnp.zeros((1, 32), jnp.int32)
            for from_x0 in range(2):
                for from_core in range(2):
                    source = ((from_zh * 2 + from_x1) * 2 + from_x0) * 2 + from_core
                    use = jnp.logical_and(half == from_core, (x0 + rx) % 2 == from_x0)
                    picked = jnp.where(use, labels[:, source * 32 : source * 32 + 32], picked)
            chunks.append(picked)
        label_ref[...] = jnp.concatenate(chunks, axis=1)

    code = jnp.broadcast_to(jnp.where(turn == 0, owner * 8 + slot, -1), (BLOCK, 512))
    at = lax.broadcasted_iota(jnp.int32, (BLOCK, 512), 0)
    own = (at >> 5) * 256 + x1 * 128 + x0 * 64 + core * 32 + (at & 31)
    pick = lax.broadcasted_iota(jnp.int32, (BLOCK, 512), 1) == own
    own_code = jnp.sum(jnp.where(pick, code, 0), axis=1, keepdims=True)
    column = lax.broadcasted_iota(jnp.int32, (BLOCK, 128), 1)
    parity = column >> 3 & 3
    from_y = (column >> 6 ^ y1) * 2 + y0 + 4
    from_x = (column >> 5 & 1 ^ x1) * 2 + x0 + 4
    for index, (dx, dy) in enumerate(SHIFTS.values()):
        from_y = from_y - jnp.where(parity == index + 1, dy, 0)
        from_x = from_x - jnp.where(parity == index + 1, dx, 0)
    chip = ((zl * 4 + (from_y & 3)) * 2 + zh) * 4 + (from_x & 3)
    place_ref[...] = jnp.where(own_code == chip * 8 + (column & 7), 1.0, 0.0).astype(BF16)


def label_places(labels):
    return pl.pallas_call(
        label_kernel,
        in_specs=[WHOLE],
        out_specs=[WHOLE] * 6,
        out_shape=[
            pltpu.VMEM((1, 256), jnp.int32),
            pltpu.VMEM((32, PADDED), BF16),
            pltpu.VMEM((1, 256), jnp.int32),
            pltpu.VMEM((32, PADDED), BF16),
            pltpu.VMEM((BLOCK, 128), BF16),
            jax.ShapeDtypeStruct((1, 128), jnp.int32),
        ],
        compiler_params=BIG,
        cost_estimate=pl.CostEstimate(flops=10 * 512 * 512, bytes_accessed=1 << 20, transcendentals=0),
        name="label_places",
    )(labels)


def far(array):
    return pltpu.with_memory_space_constraint(array, pltpu.MemorySpace.HBM)


def permute_kernel(in_ref, out_ref):
    step = in_ref.shape[0]
    number = pl.program_id(0)
    first = pl.multiple_of(number * step, step)
    tail = PADDED - ROWS
    for y0 in range(2):

        @pl.when(lax.axis_index("y0") == y0)
        def _():
            for at in range(4):
                y = at % 2 * 2 + (at // 2 + y0) % 2
                parts = [in_ref[:, (z * 4 + y) * PIECE : (z * 4 + y + 1) * PIECE] for z in range(4)]
                out_ref[pl.ds(first, step), at * WIDE : (at + 1) * WIDE] = jnp.concatenate(parts, axis=1)

    @pl.when(number == PADDED // step - 1)
    def _():
        rows = lax.broadcasted_iota(jnp.int32, (32, 1), 0)
        kept = out_ref[PADDED - 32 : PADDED, :].astype(F32)
        out_ref[PADDED - 32 : PADDED, :] = jnp.where(rows < 32 - tail, kept, 0.0).astype(BF16)


def permute_embedding(embedding):
    step = 128
    return pl.pallas_call(
        permute_kernel,
        grid=(PADDED // step,),
        in_specs=[pl.BlockSpec((step, D), lambda i: (i, 0))],
        out_specs=WHOLE,
        out_shape=pltpu.VMEM((PADDED, D), BF16),
        compiler_params=BIG,
        cost_estimate=pl.CostEstimate(flops=0, bytes_accessed=4 * ROWS * D, transcendentals=0),
        name="permute_embedding",
    )(embedding)


def spread_kernel(residual_hbm, gain_hbm, out_ref, residual_ref, gain_ref, arrived):
    copies = [
        pltpu.make_async_copy(residual_hbm, residual_ref, arrived.at[0]),
        pltpu.make_async_copy(gain_hbm, gain_ref, arrived.at[1]),
    ]
    for copy in copies:
        copy.start()
    for copy in copies:
        copy.wait()
    values = residual_ref[...].astype(F32)
    gain = gain_ref[...].astype(F32).reshape(1, PIECE)
    corner = jnp.concatenate([values[8 * g : 8 * g + 8, 256:PIECE] for g in range(4)], axis=1)
    last = jnp.concatenate([gain[:, 256:PIECE], jnp.zeros((1, 96), F32)], axis=1)
    rows = [values[:, 0:128], values[:, 128:256], corner, gain[:, 0:128], gain[:, 128:256], last, jnp.zeros((5, 128), F32)]
    tiles = jnp.concatenate(rows, axis=0).astype(BF16)
    for place in range(8):
        out_ref[place] = tiles


def spread(residual, gain):
    return pl.pallas_call(
        spread_kernel,
        in_specs=[pl.BlockSpec(memory_space=pl.ANY)] * 2,
        out_specs=WHOLE,
        out_shape=pltpu.VMEM((8, 80, 128), BF16),
        scratch_shapes=[
            pltpu.VMEM((32, PIECE), BF16),
            pltpu.VMEM((PIECE,), BF16),
            pltpu.SemaphoreType.DMA((2,)),
        ],
        compiler_params=BIG,
        name="spread",
    )(far(residual), far(gain))


def pack_kernel(in_ref, out_ref):
    for zh in range(2):
        parts = []
        for zl in range(4):
            tiles = in_ref[zl * 2 + zh].astype(F32)
            corner = jnp.concatenate([tiles[64:72, 32 * g : 32 * g + 32] for g in range(4)], axis=0)
            parts += [tiles[0:32, :], tiles[32:64, :], corner]
        wide = jnp.concatenate(parts, axis=1)
        for k in range(TILES):
            tile = wide[:, k * 128 : (k + 1) * 128].astype(BF16)
            out_ref[k * BLOCK + zh * 32 : k * BLOCK + zh * 32 + 32, :] = tile
    parts = []
    for zl in range(4):
        tiles = in_ref[zl * 2].astype(F32)
        parts += [tiles[72:73, :], tiles[73:74, :], tiles[74:75, 0:32]]
    gains = jnp.concatenate(parts, axis=1)
    rows = [gains[:, k * 128 : (k + 1) * 128] for k in range(TILES)]
    tile = jnp.concatenate(rows + [jnp.zeros((16 - TILES, 128), F32)], axis=0).astype(BF16)
    out_ref[TILES * BLOCK : PACKED, :] = tile


def pack_tokens(gathered):
    return pl.pallas_call(
        pack_kernel,
        in_specs=[WHOLE],
        out_specs=WHOLE,
        out_shape=pltpu.VMEM((PACKED, 128), BF16),
        compiler_params=BIG,
        name="pack_tokens",
    )(near(gathered))


def absolute(relative):
    return (lax.axis_index("y1") + relative // 2) % 2 * 2 + (lax.axis_index("x1") + relative % 2) % 2


def order_kernel(*refs):
    in_refs, out_ref = refs[:4], refs[4]
    for relative, ref in enumerate(in_refs):
        out_ref[absolute(relative)] = ref[...]


def in_order(pieces):
    return pl.pallas_call(
        order_kernel,
        in_specs=[WHOLE] * 4,
        out_specs=WHOLE,
        out_shape=pltpu.VMEM((4, PACKED, 128), BF16),
        compiler_params=BIG,
        name="in_order",
    )(*(near(a) for a in pieces))


def logits_kernel(*refs):
    blocks, (embedding_ref, labels_ref, slot_ref, e_near, e_far, stats_ref, *scale_ref, normed) = refs[:4], refs[4:]
    gains = [
        [blocks[ry * 2][y1 * 2, TILES * BLOCK : PACKED, :].astype(F32) for y1 in range(2)] for ry in range(2)
    ]
    for x in range(4):
        tokens = slice(x * BLOCK, (x + 1) * BLOCK)

        def tile(ry, y1, k):
            return blocks[ry * 2 + x // 2][y1 * 2 + x % 2, k * BLOCK : (k + 1) * BLOCK, :].astype(F32)

        places = [(ry, y1, k) for ry in range(2) for y1 in range(2) for k in range(TILES)]
        squares = jnp.zeros((BLOCK, 128), F32)
        for place in places:
            v = tile(*place)
            squares += v * v
        scale = lax.rsqrt(jnp.sum(squares, axis=1, keepdims=True) / D + EPS)
        for ref in scale_ref:
            ref[tokens, :] = jnp.broadcast_to(scale, (BLOCK, 128))
        for ry, y1, k in places:
            column = ry * HALF + y1 * WIDE + k * 128
            normed[tokens, column : column + 128] = (
                tile(ry, y1, k) * scale * gains[ry][y1][k : k + 1, :]
            ).astype(BF16)
    raw = lax.dot_general(
        embedding_ref[...], normed[...], (((1,), (1,)), ((), ())), preferred_element_type=F32
    )
    ratio = jnp.tanh(raw / CAP)
    row = lax.broadcasted_iota(jnp.int32, raw.shape, 0)
    inside = row < ROWS
    is_label = jnp.logical_and(inside, row + first_row() == labels_ref[...])
    exps = jnp.where(inside, jnp.exp(CAP * ratio), 0.0)
    others = jnp.where(is_label, 0.0, exps * (1.0 - ratio * ratio))
    stats_ref[0:1, :] = jnp.sum(exps, axis=0, keepdims=True)
    stats_ref[1:2, :] = jnp.sum(others * raw, axis=0, keepdims=True)
    stats_ref[2:3, :] = jnp.sum(jnp.where(is_label, raw, 0.0), axis=0, keepdims=True)
    stats_ref[3:8, :] = jnp.zeros((5, raw.shape[1]), F32)
    for rx, e_ref in enumerate((e_near, e_far)):
        e_ref[0:128, :] = others[:, rx * 128 : (rx + 1) * 128].T.astype(BF16)
        e_ref[128:144, :] = slot_ref[rx * 16 : (rx + 1) * 16, :]


def logits_of(blocks, embedding, labels, slots, with_scale):
    return pl.pallas_call(
        logits_kernel,
        in_specs=[WHOLE] * 7,
        out_specs=[WHOLE] * (3 + with_scale),
        out_shape=[
            pltpu.VMEM((144, PADDED), BF16),
            pltpu.VMEM((144, PADDED), BF16),
            pltpu.VMEM((8, 256), F32),
        ]
        + [pltpu.VMEM((256, 128), F32)] * with_scale,
        scratch_shapes=[pltpu.VMEM((256, D), BF16)],
        compiler_params=BIG,
        cost_estimate=pl.CostEstimate(flops=2 * 256 * PADDED * D, bytes_accessed=2 * PADDED * D, transcendentals=2 * 256 * PADDED),
        name="logits",
    )(*(near(a) for a in (*blocks, embedding, labels, slots)))


def three_pieces(value):
    high = value.astype(BF16).astype(F32)
    middle = (value - high).astype(BF16).astype(F32)
    low = (value - high - middle).astype(BF16).astype(F32)
    return [high, middle, low]


def stats_row(values):
    pieces = []
    for value in values:
        for piece in three_pieces(value):
            pieces += [piece, jnp.zeros((1, 128 - BLOCK), F32)]
    return jnp.concatenate(pieces, axis=1)


def read_stats(row):
    return [
        sum(row[:, (3 * i + j) * 128 : (3 * i + j) * 128 + BLOCK] for j in (2, 1, 0))
        for i in range(3)
    ]


def rows_of(term, parity, x1):
    at = parity * 144
    return term[at + x1 * BLOCK : at + (x1 + 1) * BLOCK, :], term[at + 128 + 8 * x1 : at + 128 + 8 * x1 + 8, :]


def gradient_kernel(ry, parities, *refs):
    e_refs, (embedding_ref, stats_ref, *out_refs) = refs[: len(parities)], refs[len(parities) :]
    last = lax.broadcasted_iota(jnp.int32, (8, WIDE), 0) == 7
    left = jnp.concatenate([ref[...] for ref in e_refs], axis=0)
    rows = {}
    for rx in parities:
        for x1 in range(2):
            at = (rx * 2 + x1) * BLOCK
            values = [stats_ref[i : i + 1, at : at + BLOCK] for i in range(3)]
            rows[rx, x1] = jnp.broadcast_to(stats_row(values), (8, WIDE))
    for y1 in range(2):
        column = ry * HALF + y1 * WIDE
        term = jnp.dot(left, embedding_ref[:, column : column + WIDE], preferred_element_type=F32)
        for place, rx in enumerate(parities):
            for x1 in range(2):
                out_ref, at = out_refs[y1 * len(out_refs) // 2], place * 4 // len(out_refs) + x1
                at += y1 * 2 if len(out_refs) == 1 else 0
                main, extra = rows_of(term, place, x1)
                out_ref[at, 0:BLOCK, :] = main.astype(BF16)
                out_ref[at, BLOCK:ROOM, :] = jnp.where(last, rows[rx, x1], extra).astype(BF16)


def gradient_of(ry, parities, e, embedding, stats, pieces=1):
    count = len(parities)
    return pl.pallas_call(
        functools.partial(gradient_kernel, ry, parities),
        in_specs=[WHOLE] * (2 + count),
        out_specs=[WHOLE] * pieces,
        out_shape=[pltpu.VMEM((4 * count // pieces, ROOM, WIDE), BF16)] * pieces,
        compiler_params=BIG,
        cost_estimate=pl.CostEstimate(flops=144 * count * PADDED * D, bytes_accessed=PADDED * D, transcendentals=0),
        name="gradient",
    )(*(near(e[rx]) for rx in parities), near(embedding), near(stats))


def product_kernel(ry, *refs):
    e_refs, (embedding_ref, out_ref) = refs[:-2], refs[-2:]
    left = jnp.concatenate([ref[...] for ref in e_refs], axis=0)
    out_ref[...] = jnp.dot(left, embedding_ref[:, ry * HALF : (ry + 1) * HALF], preferred_element_type=F32)


def product_of(ry, parities, e, embedding):
    count = len(parities)
    return pl.pallas_call(
        functools.partial(product_kernel, ry),
        in_specs=[WHOLE] * (1 + count),
        out_specs=WHOLE,
        out_shape=pltpu.VMEM((144 * count, HALF), F32),
        compiler_params=BIG,
        cost_estimate=pl.CostEstimate(flops=144 * count * PADDED * D, bytes_accessed=PADDED * D, transcendentals=0),
        name="product",
    )(*(near(e[rx]) for rx in parities), near(embedding))


def combine_kernel(parities, term_ref, stats_ref, *refs):
    other_refs, out_refs = refs[: -len(parities)], refs[-len(parities) :]
    last = lax.broadcasted_iota(jnp.int32, (8, WIDE), 0) == 7
    for place, rx in enumerate(parities):
        for x1 in range(2):
            at = (rx * 2 + x1) * BLOCK
            values = [stats_ref[i : i + 1, at : at + BLOCK] for i in range(3)]
            others = other_refs[0][place * 4 // len(other_refs) + x1, BLOCK:ROOM, :].astype(F32)
            others = read_stats(others[7:8, :])
            row = jnp.broadcast_to(stats_row([a + b for a, b in zip(values, others)]), (8, WIDE))
            for y1 in range(2):
                other_ref, at = other_refs[y1 * len(other_refs) // 2], place * 4 // len(other_refs) + x1
                at += y1 * 2 if len(other_refs) == 1 else 0
                main, extra = rows_of(term_ref[:, y1 * WIDE : (y1 + 1) * WIDE], place, x1)
                main = main + other_ref[at, 0:BLOCK, :].astype(F32)
                extra = extra + other_ref[at, BLOCK:ROOM, :].astype(F32)
                out_refs[place][y1 * 2 + x1, 0:BLOCK, :] = main.astype(BF16)
                out_refs[place][y1 * 2 + x1, BLOCK:ROOM, :] = jnp.where(last, row, extra).astype(BF16)


def combine(parities, term, stats, other):
    count = len(parities)
    return pl.pallas_call(
        functools.partial(combine_kernel, parities),
        in_specs=[WHOLE] * (2 + len(other)),
        out_specs=[WHOLE] * count,
        out_shape=[pltpu.VMEM((4, ROOM, WIDE), BF16)] * count,
        compiler_params=BIG,
        name="combine",
    )(near(term), near(stats), *(near(a) for a in other))


def class_kernel(*refs):
    in_refs, out_refs = refs[:4], refs[4:]
    last = lax.broadcasted_iota(jnp.int32, (8, WIDE), 0) == 7
    for relative, out_ref in enumerate(out_refs):
        block = absolute(relative)
        total = in_refs[0][block, 0:BLOCK, :].astype(F32)
        for ref in in_refs[1:]:
            total += ref[block, 0:BLOCK, :].astype(F32)
        out_ref[0:BLOCK, :] = total.astype(BF16)
        extras = [ref[block, BLOCK:ROOM, :].astype(F32) for ref in in_refs]
        row = sum(extra[7:8, :] for extra in extras)
        row = jnp.broadcast_to(stats_row(read_stats(row)), (8, WIDE))
        extras = [jnp.where(last, row if i == 0 else 0.0, extra) for i, extra in enumerate(extras)]
        out_ref[BLOCK : BLOCK + 32, :] = jnp.concatenate(extras, axis=0).astype(BF16)


def class_sum(blocks):
    return pl.pallas_call(
        class_kernel,
        in_specs=[WHOLE] * 4,
        out_specs=[WHOLE] * 4,
        out_shape=[pltpu.VMEM((BLOCK + 32, WIDE), BF16)] * 4,
        compiler_params=BIG,
        name="class_sum",
    )(*(near(a) for a in blocks))


def plane_kernel(*refs):
    in_refs, (place_ref, more_ref, values_ref, gain_ref, weight_ref, scale_ref, out_ref, *kept) = refs[:4], refs[4:]
    zh, x1, x0, core = (lax.axis_index(name) for name in ("z_hi", "x1", "x0", "core"))
    own = (((zh * 2 + x1) * 2 + x0) * 2 + core) * 32 + lax.broadcasted_iota(jnp.int32, (32, 512), 0)
    own_weight = jnp.where(lax.broadcasted_iota(jnp.int32, (32, 512), 1) == own, weight_ref[...], 0.0)
    kept[0][...] = values_ref[...].astype(F32)
    kept[1][...] = gain_ref[...].astype(F32)
    kept[2][...] = jnp.broadcast_to(jnp.sum(own_weight, axis=1, keepdims=True), (32, 128))
    kept[3][...] = scale_ref[pl.ds(pl.multiple_of(x1 * BLOCK + zh * 32, 32), 32), :]
    total = in_refs[0][0:BLOCK, :].astype(F32)
    for ref in in_refs[1:]:
        total += ref[0:BLOCK, :].astype(F32)
    extras = [ref[BLOCK : BLOCK + 32, :].astype(F32) for ref in in_refs]
    stacked = jnp.concatenate(extras, axis=0).astype(BF16)
    label_rows = jnp.dot(place_ref[...], stacked, preferred_element_type=F32) + more_ref[...].astype(F32)
    row = sum(extra[7:8, :] for extra in extras)
    pieces = []
    for value in read_stats(row):
        pieces += three_pieces(value)
    sums = jnp.concatenate(pieces + [jnp.zeros((32 - 9, BLOCK), F32)], axis=0)
    for zl in range(4):
        for zh in range(2):
            main = total[zh * 32 : zh * 32 + 32, zl * PIECE : (zl + 1) * PIECE]
            rows = label_rows[zh * 32 : zh * 32 + 32, zl * PIECE : (zl + 1) * PIECE]
            out_ref[zl * 2 + zh] = jnp.concatenate([main, rows, sums], axis=1).astype(BF16)


def plane_sum(received, place, more, values, gain, weight, scale):
    args = (*received, place, more, values, gain, weight, scale)
    return pl.pallas_call(
        plane_kernel,
        in_specs=[WHOLE] * len(args),
        out_specs=[WHOLE] * 5,
        out_shape=[
            pltpu.VMEM((8, 32, 640), BF16),
            pltpu.VMEM((32, PIECE), F32),
            pltpu.VMEM((1, PIECE), F32),
            pltpu.VMEM((32, 128), F32),
            pltpu.VMEM((32, 128), F32),
        ],
        compiler_params=BIG,
        name="plane_sum",
    )(*(near(a) for a in args))


def final_kernel(in_ref, values_ref, gain_ref, weight_ref, scale_ref, loss_ref, grad_ref):
    zh = lax.axis_index("z_hi")
    total = in_ref[0].astype(F32)
    for source in range(1, 8):
        total += in_ref[source].astype(F32)
    sums = total[0:16, 2 * PIECE : 640]
    pick = lax.broadcasted_iota(jnp.int32, (32, BLOCK), 1) == zh * 32 + lax.broadcasted_iota(
        jnp.int32, (32, BLOCK), 0
    )

    def column(i):
        value = sum(sums[3 * i + j : 3 * i + j + 1, :] for j in (2, 1, 0))
        return jnp.sum(jnp.where(pick, jnp.broadcast_to(value, (32, BLOCK)), 0.0), axis=1, keepdims=True)

    sum_exp, inner_others, raw = column(0), column(1), column(2)
    weight = weight_ref[:, 0:1]
    scaling = scale_ref[:, 0:1]
    ratio = jnp.tanh(raw / CAP)
    capped = CAP * ratio
    log_total = jnp.log(sum_exp)
    loss = log_total - capped
    coefficient = (jnp.exp(capped - log_total) - 1.0) * weight * (1.0 - ratio * ratio)
    coefficient = coefficient.astype(BF16).astype(F32)
    share = weight / sum_exp
    grad_normed = total[:, 0:PIECE] * share + total[:, PIECE : 2 * PIECE] * coefficient
    inner = (inner_others * share + coefficient * raw) / scaling
    upstream = grad_normed * gain_ref[...]
    values = values_ref[...]
    grad_ref[...] = scaling * upstream - values * (scaling * scaling * scaling * inner / D)
    eye = lax.broadcasted_iota(jnp.int32, (32, 32), 0) == lax.broadcasted_iota(jnp.int32, (32, 32), 1)
    loss_ref[...] = jnp.sum(jnp.where(eye, jnp.broadcast_to(loss, (32, 32)), 0.0), axis=0, keepdims=True)


def finish(received, values, gain, weight, scale):
    return pl.pallas_call(
        final_kernel,
        in_specs=[WHOLE] * 5,
        out_specs=[WHOLE] * 2,
        out_shape=[jax.ShapeDtypeStruct((1, 32), F32), jax.ShapeDtypeStruct((32, PIECE), F32)],
        compiler_params=BIG,
        name="finish",
    )(*(near(a) for a in (received, values, gain, weight, scale)))


def swap_cores(array):
    return lax.ppermute(array, "core", [(0, 1), (1, 0)])


def shifted(array, dx, dy):
    pairs = []
    for chip in range(128):
        line, y, zh, x = chip // 32, chip // 8 % 4, chip // 4 % 2, chip % 4
        pairs.append((chip, ((line * 4 + (y + dy) % 4) * 2 + zh) * 4 + (x + dx) % 4))
    return lax.ppermute(array, CHIPS, pairs)


def later_rows(labels, embedding, rounds):
    def one_round(carry):
        number, rows = carry
        _, tokens = lax.optimization_barrier((number, labels))
        zl, y1, y0, zh, x1, x0, core = (lax.axis_index(name) for name in (*CHIPS, "core"))
        token = jnp.arange(512, dtype=jnp.int32)
        group = (token // 32) % 2 * 4 + (token // 64) % 2 * 2 + (token // 128) % 2
        owner = tokens // (2 * ROWS)
        key = owner * 8 + group
        same = jnp.logical_and(key[:, None] == key[None, :], token[None, :] < token[:, None])
        rank = jnp.sum(same.astype(jnp.int32), axis=1)
        turn, slot = rank // SLOTS, rank % SLOTS
        taken = jnp.where(jnp.logical_and(owner == this_chip(), turn == number), group * 8 + slot, -1)
        match = taken[None, :] == jnp.arange(64, dtype=jnp.int32)[:, None]
        held = jnp.sum(jnp.where(match, (tokens - first_row())[None, :] + 1, 0), axis=1) - 1
        chosen = (held[:, None] == jnp.arange(ROWS, dtype=jnp.int32)[None, :]).astype(BF16)
        found = jnp.dot(chosen, embedding, preferred_element_type=F32).astype(BF16)
        found = found.reshape(2, 2, 2, 8, 4, 4, PIECE).transpose(0, 5, 2, 1, 3, 4, 6).reshape(2, 16, 8, WIDE)
        ours = lax.dynamic_index_in_dim(found, core, 0, keepdims=False)
        theirs = lax.dynamic_index_in_dim(found, 1 - core, 0, keepdims=False)
        ours = ours + swap_cores(theirs)
        ours = lax.all_to_all(ours, ("y1", "y0", "x1", "x0"), 0, 0, tiled=True).reshape(128, WIDE)
        local = jnp.arange(BLOCK, dtype=jnp.int32)
        own = (((local // 32 * 2 + x1) * 2 + x0) * 2 + core) * 32 + local % 32
        place = jnp.arange(16, dtype=jnp.int32)
        chips = ((zl * 4 + place // 4) * 2 + zh) * 4 + place % 4
        hit = jnp.logical_and(owner[own][:, None] == chips[None, :], (turn[own] == number)[:, None])
        at = slot[own][:, None] == jnp.arange(8, dtype=jnp.int32)[None, :]
        put = jnp.logical_and(hit[:, :, None], at[:, None, :]).astype(BF16).reshape(BLOCK, 128)
        return number + 1, rows + jnp.dot(put, ours, preferred_element_type=F32).astype(BF16)

    start = (jnp.int32(1), jnp.zeros((BLOCK, WIDE), BF16))
    return lax.while_loop(lambda carry: carry[0] < rounds, one_round, start)[1]


def on_device(residual, final_gain, embedding, labels, token_weight):
    gain = final_gain.reshape(1, PIECE)
    gathered = lax.all_to_all(spread(residual, final_gain), ("z_lo", "z_hi"), 0, 0, tiled=True)
    piece, embedding, labels = lax.optimization_barrier((pack_tokens(gathered), embedding, labels))

    moved = [shifted(piece, 2 * dx, 2 * dy) for dy, dx in PLACES[1:]]
    *early, rounds = label_places(labels.reshape(1, 512))
    more = later_rows(labels, embedding, rounds[0, 0])
    moved, more, early = lax.optimization_barrier((moved, more, early))
    own_labels, own_slots, other_labels, other_slots, place = early
    packed = in_order([piece] + moved)
    table = permute_embedding(embedding)
    blocks = [packed] + [shifted(packed, *SHIFTS[parity]) for parity in PLACES[1:]]
    blocks[1], table = lax.optimization_barrier((blocks[1], table))
    other_blocks = [swap_cores(block) for block in blocks]

    *e, stats, scale = logits_of(blocks, table, own_labels, own_slots, True)
    other_blocks, e = lax.optimization_barrier((other_blocks, e))
    *e_other, stats_other = logits_of(other_blocks, table, other_labels, other_slots, False)
    far_part, e_other = lax.optimization_barrier((gradient_of(1, (0, 1), e_other, table, stats_other), e_other))
    near_part, e = lax.optimization_barrier((gradient_of(0, (1,), e_other, table, stats_other), e))
    far_blocks = combine((0, 1), product_of(1, (0, 1), e, table), stats, [swap_cores(part) for part in far_part])
    far_blocks, e = lax.optimization_barrier((far_blocks, e))
    (near_block,) = combine((1,), product_of(0, (1,), e, table), stats, [swap_cores(part) for part in near_part])
    near_block, e, e_other = lax.optimization_barrier((near_block, e, e_other))
    stay_part, e = lax.optimization_barrier((gradient_of(0, (0,), e_other, table, stats_other, 2), e))
    (stay_block,) = combine((0,), product_of(0, (0,), e, table), stats, [swap_cores(part) for part in stay_part])
    parts = [stay_block, near_block, *far_blocks]
    sums = class_sum([parts[0]] + [shifted(part, *SHIFTS[parity]) for part, parity in zip(parts[1:], PLACES[1:])])
    plane = [shifted(block, 2 * dx, 2 * dy) for block, (dy, dx) in zip(sums[:0:-1], PLACES[:0:-1])]
    plane = [sums[0]] + plane[::-1]
    plane, *kept = plane_sum(plane, place, more, residual, gain, token_weight.reshape(1, 512), scale)
    column = lax.all_to_all(plane, ("z_lo", "z_hi"), 0, 0, tiled=True)
    loss, grad = finish(column, *kept)
    return (loss.reshape(32), grad)


def solution(mesh):
    fine = Mesh(mesh.devices.reshape(4, 2, 2, 2, 2, 2, 2), (*CHIPS, "core"))
    section, fsdp = ("z_lo", "y1", "y0"), ("z_hi", "x1", "x0", "core")
    in_specs = (P(fsdp, section), P(section), P(section + fsdp, None), P(), P())
    out_specs = (P(fsdp), P(fsdp, section))
    return jax.shard_map(on_device, mesh=fine, in_specs=in_specs, out_specs=out_specs, check_vma=False)
```
